32 devices in a mesh: dp: 4 (over y, x), fsdp: 8 (over z, core).
Axes of the slice: x: 2, y: 2, z: 4, core: 2. Of those that a mesh axis runs over, the one named last changes fastest.
Arguments:
- tokens: bfloat16 [40960, 640], P(('dp', 'fsdp')), may hold values from -6 to 6
- lengths: int32 [32], P(('dp', 'fsdp')), may hold values from 500 to 1250, as said below
- query_weight: bfloat16 [768, 768], P('fsdp'), may hold values from -0.25 to 0.25
- key_weight: bfloat16 [768, 768], P('fsdp'), may hold values from -0.25 to 0.25
- value_weight: bfloat16 [768, 768], P('fsdp'), may hold values from -0.25 to 0.25
- out_weight: bfloat16 [768, 768], P('fsdp'), may hold values from -1 to 1
- up_weight: bfloat16 [768, 3072], P('fsdp'), may hold values from -0.25 to 0.25
- down_weight: bfloat16 [3072, 768], P('fsdp'), may hold values from -0.125 to 0.125
- query_bias: bfloat16 [768], P('fsdp'), may hold values from -3 to 3
- value_bias: bfloat16 [768], P('fsdp'), may hold values from -3 to 3
- out_bias: bfloat16 [768], P('fsdp'), may hold values from -3 to 3
- up_bias: bfloat16 [3072], P('fsdp'), may hold values from -3 to 3
- down_bias: bfloat16 [768], P('fsdp'), may hold values from -3 to 3
- first_gain: bfloat16 [768], P('fsdp'), may hold values from 0.099609375 to 1.8984375
- first_shift: bfloat16 [768], P('fsdp'), may hold values from -2 to 2
- second_gain: bfloat16 [768], P('fsdp'), may hold values from 0.099609375 to 1.8984375
- second_shift: bfloat16 [768], P('fsdp'), may hold values from -2 to 2
- cotangent: bfloat16 [40960, 640], P(('dp', 'fsdp')), may hold values from -6 to 6
Outputs:
- output: bfloat16 [40960, 640], P(('dp', 'fsdp'))
- token_grad: bfloat16 [40960, 640], P(('dp', 'fsdp'))
- grad_query_weight: float32 [768, 768], P('fsdp')
- grad_key_weight: float32 [768, 768], P('fsdp')
- grad_value_weight: float32 [768, 768], P('fsdp')
- grad_out_weight: float32 [768, 768], P('fsdp')
- grad_up_weight: float32 [768, 3072], P('fsdp')
- grad_down_weight: float32 [3072, 768], P('fsdp')
- grad_query_bias: float32 [768], P('fsdp')
- grad_value_bias: float32 [768], P('fsdp')
- grad_out_bias: float32 [768], P('fsdp')
- grad_up_bias: float32 [3072], P('fsdp')
- grad_down_bias: float32 [768], P('fsdp')
- grad_first_gain: float32 [768], P('fsdp')
- grad_first_shift: float32 [768], P('fsdp')
- grad_second_gain: float32 [768], P('fsdp')
- grad_second_shift: float32 [768], P('fsdp')
The draws below stay inside these ranges and needn't reach their ends.
Inputs may be any that keep to these rules, and one draw needn't show every extreme that they name: Utterance lengths in frames; the utterances of one dp index form one length bucket, longer on higher indices; the longest is exactly 1250.
All inputs are finite; a program needn't handle non-finite values.
Results may differ from the reference program's by a relative error of at most 0.018.
Values may be sent and summed in bfloat16 or wider, within the bound.
No kernel may reach another device: no remote copies, remote signals or barrier semaphores. Data moves between devices by JAX's collectives and lax.ppermute only.
A program may use at most 256 MiB of HBM per device.

```python
import jax
import jax.numpy as jnp
from jax import lax

SUPER_WIDTH = 768
SUPER_HIDDEN = 3072
HEAD_DIM = 64
HEAD_COUNT = 10
HIDDEN_SIZE = 2240
SLOT_LEN = 1280
MAX_LEN = 1250
MIN_LEN = 500
WIDTH = 640
UTTERANCES = 32
TOKENS = 40960
N_DP = 4


def draw_lengths(key, part):
    key = jax.random.fold_in(key, 7)
    first_key, second_key = jax.random.split(key)
    bucket_width = (MAX_LEN - MIN_LEN) // N_DP
    per_bucket = UTTERANCES // N_DP
    bucket = jnp.arange(UTTERANCES, dtype=jnp.int32) // per_bucket
    lowest = MIN_LEN + bucket * bucket_width
    sampled = jax.random.randint(first_key, (UTTERANCES,), lowest, lowest + bucket_width + 1)
    chosen = jax.random.randint(second_key, (), UTTERANCES - per_bucket, UTTERANCES)
    return jnp.where(jnp.arange(UTTERANCES, dtype=jnp.int32) == chosen, MAX_LEN, sampled).astype(jnp.int32)


def shard_levels(stream_key, extent, cuts, least, top_value):
    factor_of = 1.0
    for dim, parts in cuts:
        heights = jax.random.uniform(jax.random.fold_in(jax.random.fold_in(stream_key, 6), dim), (parts,), jnp.float32, least / len(cuts), top_value / len(cuts))
        factor_of = factor_of * jnp.repeat(jnp.exp(heights), extent[dim] // parts).reshape((-1,) + (1,) * (len(extent) - 1 - dim))
    return factor_of


def noise(rng, dims, width, most, cuts=(), kind=jnp.bfloat16):
    gain = shard_levels(rng, dims, cuts, -0.22, 0.18) if cuts else 1.0
    drawn = jax.random.normal(rng, dims, jnp.float32) * width * gain
    return jnp.minimum(jnp.maximum(drawn, -most), most).astype(kind)


def setup_inputs(seed: int = 0) -> dict:
    seeds = jax.random.split(jax.random.key(seed), 19)
    tokens = noise(seeds[0], (TOKENS, WIDTH), 1.0, 6.0, ((0, 32),))
    lengths = draw_lengths(jax.random.fold_in(seeds[18], 71), 0)
    query_weight = noise(seeds[2], (SUPER_WIDTH, SUPER_WIDTH), WIDTH ** -0.5, 0.25, ((0, 8),))
    key_weight = noise(seeds[3], (SUPER_WIDTH, SUPER_WIDTH), WIDTH ** -0.5, 0.25, ((0, 8),))
    value_weight = noise(seeds[4], (SUPER_WIDTH, SUPER_WIDTH), WIDTH ** -0.5, 0.25, ((0, 8),))
    out_weight = noise(seeds[5], (SUPER_WIDTH, SUPER_WIDTH), (WIDTH // 16) ** -0.5, 1.0, ((0, 8),))
    up_weight = noise(seeds[6], (SUPER_WIDTH, SUPER_HIDDEN), WIDTH ** -0.5, 0.25, ((0, 8),))
    down_weight = noise(seeds[7], (SUPER_HIDDEN, SUPER_WIDTH), HIDDEN_SIZE ** -0.5, 0.125, ((0, 8),))
    query_bias = noise(seeds[8], (SUPER_WIDTH,), 0.5, 3.0, ((0, 8),))
    value_bias = noise(seeds[9], (SUPER_WIDTH,), 0.5, 3.0, ((0, 8),))
    out_bias = noise(seeds[10], (SUPER_WIDTH,), 0.5, 3.0, ((0, 8),))
    up_bias = noise(seeds[11], (SUPER_HIDDEN,), 0.5, 3.0, ((0, 8),))
    down_bias = noise(seeds[12], (SUPER_WIDTH,), 0.5, 3.0, ((0, 8),))
    first_gain = jnp.clip(1.0 + 0.18 * jax.random.normal(seeds[13], (SUPER_WIDTH,), jnp.float32), 0.099609375, 1.8984375).astype(jnp.bfloat16)
    first_shift = noise(seeds[14], (SUPER_WIDTH,), 0.3, 2.0, ((0, 8),))
    second_gain = jnp.clip(1.0 + 0.18 * jax.random.normal(seeds[15], (SUPER_WIDTH,), jnp.float32), 0.099609375, 1.8984375).astype(jnp.bfloat16)
    second_shift = noise(seeds[16], (SUPER_WIDTH,), 0.3, 2.0, ((0, 8),))
    cotangent = noise(seeds[17], (TOKENS, WIDTH), 1.0, 6.0, ((0, 32),))
    return {"tokens": tokens, "lengths": lengths, "query_weight": query_weight, "key_weight": key_weight, "value_weight": value_weight, "out_weight": out_weight, "up_weight": up_weight, "down_weight": down_weight, "query_bias": query_bias, "value_bias": value_bias, "out_bias": out_bias, "up_bias": up_bias, "down_bias": down_bias, "first_gain": first_gain, "first_shift": first_shift, "second_gain": second_gain, "second_shift": second_shift, "cotangent": cotangent}


@jax.custom_vjp
def low(v):
    return lax.optimization_barrier(v.astype(jnp.bfloat16)).astype(jnp.float32)

@jax.custom_vjp
def low_back(v):
    return v

def low_keep(v):
    return (low(v), None)

def low_pass(kept, grad):
    return (grad,)

def back_keep(v):
    return (v, None)

def back_low(kept, grad):
    return (low(grad),)
low.defvjp(low_keep, low_pass)
low_back.defvjp(back_keep, back_low)
EPSILON = 1e-05
MASKED = -1e+30
HIGHEST_PRECISION = lax.Precision.HIGHEST

def matmul(left_side, right_side):
    return jnp.dot(left_side, right_side, precision=HIGHEST_PRECISION)

def rounded(values):
    return low_back(low(values))

def norm_rows(hidden, gain_row, shift_row):
    center = hidden - lax.optimization_barrier(jnp.mean(hidden, -1, keepdims=True))
    spread = lax.optimization_barrier(jnp.mean(center * center, -1, keepdims=True))
    return center * lax.rsqrt(spread + EPSILON) * gain_row + shift_row

def sub_params(params):
    query_weight, key_weight, value_weight, out_weight, up_weight, down_weight, query_bias, value_bias, out_bias, up_bias, down_bias, first_gain, first_shift, second_gain, second_shift = params
    return (query_weight[:WIDTH, :WIDTH], key_weight[:WIDTH, :WIDTH], value_weight[:WIDTH, :WIDTH], out_weight[:WIDTH, :WIDTH], up_weight[:WIDTH, :HIDDEN_SIZE], down_weight[:HIDDEN_SIZE, :WIDTH], query_bias[:WIDTH], value_bias[:WIDTH], out_bias[:WIDTH], up_bias[:HIDDEN_SIZE], down_bias[:WIDTH], first_gain[:WIDTH], first_shift[:WIDTH], second_gain[:WIDTH], second_shift[:WIDTH])

def layer_item(token_rows, length, subs):
    query_sub, key_sub, value_sub, out_sub, up_sub, down_sub, query_add, value_add, out_add, up_add, down_add, gain_one, shift_one, gain_two, shift_two = subs
    live_mask = jnp.arange(SLOT_LEN, dtype=jnp.int32) < length
    queries = rounded(matmul(token_rows, query_sub) + query_add)
    key_rows = rounded(matmul(token_rows, key_sub))
    value_rows = rounded(matmul(token_rows, value_sub) + value_add)
    query_heads = queries.reshape(SLOT_LEN, HEAD_COUNT, HEAD_DIM)
    key_heads = key_rows.reshape(SLOT_LEN, HEAD_COUNT, HEAD_DIM)
    value_heads = value_rows.reshape(SLOT_LEN, HEAD_COUNT, HEAD_DIM)
    scores = jnp.einsum('qhd,khd->hqk', query_heads, key_heads, precision=HIGHEST_PRECISION) * HEAD_DIM ** (-0.5)
    scores = jnp.where(live_mask[None, None, :], low_back(scores), MASKED)
    prob_low = low(jax.nn.softmax(scores, axis=-1))
    context = jnp.einsum('hqk,khd->qhd', prob_low, value_heads, precision=HIGHEST_PRECISION)
    context = rounded(context.reshape(SLOT_LEN, WIDTH))
    branch = low_back(matmul(context, out_sub) + out_add)
    normed = low(norm_rows(token_rows + branch, gain_one, shift_one))
    hidden = low_back(matmul(normed, up_sub) + up_add)
    active = low(jax.nn.gelu(hidden, approximate=False))
    feed_out = low_back(matmul(active, down_sub) + down_add)
    result = norm_rows(normed + feed_out, gain_two, shift_two)
    return result * live_mask[:, None].astype(jnp.float32)

def reference(tokens, lengths, query_weight, key_weight, value_weight, out_weight, up_weight, down_weight, query_bias, value_bias, out_bias, up_bias, down_bias, first_gain, first_shift, second_gain, second_shift, cotangent):
    params = tuple((array.astype(jnp.float32) for array in (query_weight, key_weight, value_weight, out_weight, up_weight, down_weight, query_bias, value_bias, out_bias, up_bias, down_bias, first_gain, first_shift, second_gain, second_shift)))
    layer_saved = jax.checkpoint(layer_item)

    def forward(token_rows, weights_all):
        subs = sub_params(weights_all)
        blocks = token_rows.reshape(UTTERANCES, SLOT_LEN, WIDTH)

        def scan_step(running, pieces):
            return (running, layer_saved(pieces[0], pieces[1], subs))
        ignored, outputs = lax.scan(scan_step, jnp.zeros((), jnp.float32), (blocks, lengths))
        return outputs.reshape(TOKENS, WIDTH)
    result, backward = jax.vjp(forward, tokens.astype(jnp.float32), params)
    grad_tokens, grads = backward(cotangent.astype(jnp.float32))
    return (result.astype(jnp.bfloat16), grad_tokens.astype(jnp.bfloat16), grads[0], grads[1], grads[2], grads[3], grads[4], grads[5], grads[6], grads[7], grads[8], grads[9], grads[10], grads[11], grads[12], grads[13], grads[14])
```

```python
import functools

import jax
import jax.numpy as jnp
from jax import lax
from jax.experimental import pallas as pl
from jax.experimental.pallas import tpu as pltpu
from jax.sharding import PartitionSpec as P

HEAD_DIM = 64
HIDDEN_SIZE = 2240
WIDTH = 640
EPSILON = 1e-05
MASKED = -1e30
PAIR = 2 * HEAD_DIM
PAIRS = WIDTH // PAIR
BF = jnp.bfloat16
F32 = jnp.float32
VMEM_BYTES = 60 * 2**20


def dot(left, right, left_dim, right_dim):
    return lax.dot_general(
        left, right, (((left_dim,), (right_dim,)), ((), ())), preferred_element_type=F32
    )


def side(shape, axis, half, own, flag):
    place = lax.broadcasted_iota(jnp.int32, shape, axis)
    mine = (place < HEAD_DIM) if half == 0 else (place >= HEAD_DIM)
    first = place == (HEAD_DIM if half == 0 else 0)
    return jnp.where(mine, own, jnp.where(first, flag, 0.0))


def attend_kernel(
    length_ref, token_ref, wq_ref, wk_ref, wv_ref, bq_ref, bv_ref,
    exp_ref, context_ref, wide_ref, inverse_ref, query_t_ref, key_ref, value_t_ref,
):
    rows = token_ref.shape[0]
    weights = jnp.concatenate([wq_ref[...], wk_ref[...], wv_ref[...]], axis=1)
    product = dot(token_ref[...], weights, 1, 0)
    query = (product[:, :PAIR] + bq_ref[...]).astype(BF)
    key = product[:, PAIR : 2 * PAIR].astype(BF)
    value = (product[:, 2 * PAIR :] + bv_ref[...]).astype(BF)
    key_t = key.T
    query_t_ref[...] = query.T
    key_ref[...] = key
    value_t_ref[...] = value.T
    key_place = lax.broadcasted_iota(jnp.int32, (1, rows), 1)
    bias = jnp.where(key_place < length_ref[0], 0.0, MASKED)
    scaled = query.astype(F32) * HEAD_DIM**-0.5
    key_wide = key_t.astype(F32)
    value_wide = value.astype(F32)
    block = 128
    results = []
    for half in range(2):
        left = side((rows, PAIR), 1, half, scaled, 1.0).astype(BF)
        place = lax.broadcasted_iota(jnp.int32, (PAIR, rows), 0)
        right = jnp.where(place == (HEAD_DIM if half == 0 else 0), bias, key_wide).astype(BF)
        for start in range(0, rows, block):
            scores = dot(left[start : start + block], right, 1, 0)
            highest = jnp.max(scores, 1, keepdims=True)
            exp_ref[half, start : start + block, :] = jnp.exp(scores - highest).astype(BF)
        values = side((rows, PAIR), 1, half, value_wide, 1.0).astype(BF)
        total = dot(exp_ref[half], values, 1, 0)
        flag = HEAD_DIM if half == 0 else 0
        inverse = 1.0 / total[:, flag : flag + 1]
        results.append((total * inverse, inverse))
    low = lax.broadcasted_iota(jnp.int32, (rows, PAIR), 1) < HEAD_DIM
    context = jnp.where(low, results[0][0], results[1][0])
    wide_ref[...] = context
    context_ref[...] = context.astype(BF)
    inverse_ref[...] = jnp.where(low, results[0][1], results[1][1])


def attend(tokens, lengths, wide_weights, vectors):
    rows = tokens.shape[0]
    column = lambda first: pl.BlockSpec((WIDTH, PAIR), lambda p: (0, first + p))
    vector = lambda: pl.BlockSpec((1, PAIR), lambda p: (0, p))
    tall = lambda: pl.BlockSpec((rows, PAIR), lambda p: (0, p))
    flat = lambda: pl.BlockSpec((PAIR, rows), lambda p: (p, 0))
    return pl.pallas_call(
        attend_kernel,
        grid=(PAIRS,),
        in_specs=[
            pl.BlockSpec(memory_space=pltpu.SMEM),
            pl.BlockSpec((rows, WIDTH), lambda p: (0, 0)),
            column(0), column(PAIRS), column(2 * PAIRS),
            vector(), vector(),
        ],
        out_specs=[
            pl.BlockSpec((2, rows, rows), lambda p: (p, 0, 0)),
            tall(), tall(), tall(), flat(), tall(), flat(),
        ],
        out_shape=[
            jax.ShapeDtypeStruct((2 * PAIRS, rows, rows), BF),
            jax.ShapeDtypeStruct((rows, WIDTH), BF),
            jax.ShapeDtypeStruct((rows, WIDTH), F32),
            jax.ShapeDtypeStruct((rows, WIDTH), F32),
            jax.ShapeDtypeStruct((WIDTH, rows), BF),
            jax.ShapeDtypeStruct((rows, WIDTH), BF),
            jax.ShapeDtypeStruct((WIDTH, rows), BF),
        ],
        compiler_params=pltpu.CompilerParams(vmem_limit_bytes=VMEM_BYTES),
    )(lengths, tokens, wide_weights, wide_weights, wide_weights, vectors[0:1], vectors[1:2])


def gelu_pair(values):
    t = 1.0 / (1.0 + (0.3275911 * 0.5**0.5) * jnp.abs(values))
    bell = jnp.exp(-0.5 * values * values)
    tail = t * (0.5 * 0.254829592 + t * (0.5 * -0.284496736 + t * (0.5 * 1.421413741 + t * (
        0.5 * -1.453152027 + t * (0.5 * 1.061405429)))))
    tail = tail * bell
    share = jnp.where(values >= 0.0, 1.0 - tail, tail)
    return values * share, share + values * bell * 0.3989422804014327


def row_mean(values):
    return jnp.sum(values, 1, keepdims=True) * (1.0 / WIDTH)


def column_sum(values):
    return jnp.sum(values, 0, keepdims=True)


def feed_kernel(
    length_ref, context_ref, token_ref, cotangent_ref, wo_ref, w1_ref, w2_ref, vector_ref, b1_ref,
    output_ref, normed_ref, active_ref, hidden_ref, feed_ref, first_ref, grad_context_ref,
    sums_ref, b1_sum_ref,
):
    step = pl.program_id(0)
    rows = token_ref.shape[0]
    place = lax.broadcasted_iota(jnp.int32, (rows, 1), 0) + step * rows
    live = jnp.where(place < length_ref[0], 1.0, 0.0)
    vector = lambda i: vector_ref[i : i + 1, :]
    out_add, down_add = vector(2), vector(3)
    gain_one, shift_one, gain_two, shift_two = vector(4), vector(5), vector(6), vector(7)
    first_sum = token_ref[...].astype(F32) + dot(context_ref[...], wo_ref[...], 1, 0) + out_add
    center = first_sum - row_mean(first_sum)
    rate_one = lax.rsqrt(row_mean(center * center) + EPSILON)
    unit_one = center * rate_one
    normed = (unit_one * gain_one + shift_one).astype(BF)
    normed_ref[...] = normed
    pre = dot(normed, w1_ref[...], 1, 0) + b1_ref[...]
    active_full, slope = gelu_pair(pre)
    active = active_full.astype(BF)
    active_ref[...] = active
    second_sum = normed.astype(F32) + dot(active, w2_ref[...], 1, 0) + down_add
    center = second_sum - row_mean(second_sum)
    rate_two = lax.rsqrt(row_mean(center * center) + EPSILON)
    unit_two = center * rate_two
    output_ref[...] = ((unit_two * gain_two + shift_two) * live).astype(BF)
    cotangent = cotangent_ref[...].astype(F32) * live
    inner = cotangent * gain_two
    grad_second = rate_two * (inner - row_mean(inner) - unit_two * row_mean(inner * unit_two))
    grad_feed = grad_second.astype(BF)
    feed_ref[...] = grad_feed
    grad_hidden = (dot(grad_feed, w2_ref[...], 1, 1) * slope).astype(BF)
    hidden_ref[...] = grad_hidden
    grad_normed = grad_second + dot(grad_hidden, w1_ref[...], 1, 1)
    inner = grad_normed * gain_one
    grad_first = rate_one * (inner - row_mean(inner) - unit_one * row_mean(inner * unit_one))
    first_ref[...] = grad_first
    grad_branch = grad_first.astype(BF)
    grad_context_ref[...] = dot(grad_branch, wo_ref[...], 1, 1).astype(BF)
    sums = jnp.concatenate(
        [
            column_sum(grad_branch.astype(F32)),
            column_sum(grad_feed.astype(F32)),
            column_sum(grad_normed * unit_one),
            column_sum(grad_normed),
            column_sum(cotangent * unit_two),
            column_sum(cotangent),
            jnp.zeros((2, WIDTH), F32),
        ],
        axis=0,
    )
    b1_sum = column_sum(grad_hidden.astype(F32))

    @pl.when(step == 0)
    def _():
        sums_ref[...] = sums
        b1_sum_ref[...] = b1_sum

    @pl.when(step > 0)
    def _():
        sums_ref[...] += sums
        b1_sum_ref[...] += b1_sum


def feed(lengths, context, tokens, cotangent, wo, w1, w2, vectors, b1):
    rows = tokens.shape[0]
    tile = 256
    part = lambda width: pl.BlockSpec((tile, width), lambda i: (i, 0))
    whole = lambda *shape: pl.BlockSpec(shape, lambda i: (0, 0))
    array = lambda width, kind: jax.ShapeDtypeStruct((rows, width), kind)
    return pl.pallas_call(
        feed_kernel,
        grid=(rows // tile,),
        in_specs=[
            pl.BlockSpec(memory_space=pltpu.SMEM),
            part(WIDTH), part(WIDTH), part(WIDTH),
            whole(WIDTH, WIDTH), whole(WIDTH, HIDDEN_SIZE), whole(HIDDEN_SIZE, WIDTH),
            whole(8, WIDTH), whole(1, HIDDEN_SIZE),
        ],
        out_specs=[
            part(WIDTH), part(WIDTH), part(HIDDEN_SIZE), part(HIDDEN_SIZE), part(WIDTH),
            part(WIDTH), part(WIDTH), whole(8, WIDTH), whole(1, HIDDEN_SIZE),
        ],
        out_shape=[
            array(WIDTH, BF), array(WIDTH, BF), array(HIDDEN_SIZE, BF), array(HIDDEN_SIZE, BF),
            array(WIDTH, BF), array(WIDTH, F32), array(WIDTH, BF),
            jax.ShapeDtypeStruct((8, WIDTH), F32),
            jax.ShapeDtypeStruct((1, HIDDEN_SIZE), F32),
        ],
        compiler_params=pltpu.CompilerParams(vmem_limit_bytes=VMEM_BYTES),
    )(lengths, context, tokens, cotangent, wo, w1, w2, vectors, b1)


def attend_back_kernel(
    grad_ref, wide_ref, inverse_ref, exp_ref, query_t_ref, key_ref, value_t_ref,
    dq_ref, dk_ref, dv_ref, sums_ref, score_ref,
):
    rows = grad_ref.shape[0]
    inverse = inverse_ref[...]
    grad = grad_ref[...].astype(F32)
    scaled = grad * inverse
    dots = scaled * wide_ref[...]
    scaled_t = scaled.T.astype(BF)
    value_wide = value_t_ref[...].astype(F32)
    lane = lax.broadcasted_iota(jnp.int32, (rows, PAIR), 1)
    place = lax.broadcasted_iota(jnp.int32, (PAIR, rows), 0)
    block = 128
    dq, dk_t, dv_t = [], [], []
    for half in range(2):
        mine = (lane < HEAD_DIM) if half == 0 else (lane >= HEAD_DIM)
        flag = HEAD_DIM if half == 0 else 0
        offset = jnp.sum(jnp.where(mine, -dots, 0.0), 1, keepdims=True)
        high = offset.astype(BF).astype(F32)
        rest = offset - high
        left = jnp.where(
            mine, scaled, jnp.where(lane == flag, high, jnp.where(lane == flag + 1, rest, 0.0))
        ).astype(BF)
        right = jnp.where((place == flag) | (place == flag + 1), 1.0, value_wide).astype(BF)
        for start in range(0, rows, block):
            grad_probs = dot(left[start : start + block], right, 1, 0)
            weight = exp_ref[half, start : start + block, :].astype(F32)
            score_ref[half, start : start + block, :] = (grad_probs * weight).astype(BF)
        own = slice(half * HEAD_DIM, (half + 1) * HEAD_DIM)
        dv_t.append(dot(scaled_t[own], exp_ref[half], 1, 0))
        dk_t.append(dot(query_t_ref[own, :], score_ref[half], 1, 0))
        dq.append(dot(score_ref[half], key_ref[...], 1, 0))
    factor = HEAD_DIM**-0.5
    dq_low = (jnp.where(lane < HEAD_DIM, dq[0], dq[1]) * factor).astype(BF)
    dk_low = (jnp.concatenate(dk_t, axis=0) * factor).T.astype(BF)
    dv_low = jnp.concatenate(dv_t, axis=0).T.astype(BF)
    dq_ref[...] = dq_low
    dk_ref[...] = dk_low
    dv_ref[...] = dv_low
    sums_ref[...] = jnp.concatenate(
        [
            column_sum(dq_low.astype(F32)),
            column_sum(dv_low.astype(F32)),
            jnp.zeros((6, PAIR), F32),
        ],
        axis=0,
    )


def attend_back(grad_context, wide, inverse, exps, query_t, key, value_t):
    rows = grad_context.shape[0]
    tall = lambda: pl.BlockSpec((rows, PAIR), lambda p: (0, p))
    flat = lambda: pl.BlockSpec((PAIR, rows), lambda p: (p, 0))
    return pl.pallas_call(
        attend_back_kernel,
        grid=(PAIRS,),
        in_specs=[
            tall(), tall(), tall(),
            pl.BlockSpec((2, rows, rows), lambda p: (p, 0, 0)),
            flat(), tall(), flat(),
        ],
        out_specs=[tall(), tall(), tall(), pl.BlockSpec((8, PAIR), lambda p: (0, p))],
        out_shape=[
            jax.ShapeDtypeStruct((rows, WIDTH), BF),
            jax.ShapeDtypeStruct((rows, WIDTH), BF),
            jax.ShapeDtypeStruct((rows, WIDTH), BF),
            jax.ShapeDtypeStruct((8, WIDTH), F32),
        ],
        scratch_shapes=[pltpu.VMEM((2, rows, rows), BF)],
        compiler_params=pltpu.CompilerParams(vmem_limit_bytes=VMEM_BYTES),
    )(grad_context, wide, inverse, exps, query_t, key, value_t)


def widen(matrix, row_count, column_count):
    return jnp.pad(matrix, ((0, row_count - matrix.shape[0]), (0, column_count - matrix.shape[1])))


def on_device(
    tokens, lengths, query_weight, key_weight, value_weight, out_weight, up_weight, down_weight,
    query_bias, value_bias, out_bias, up_bias, down_bias, first_gain, first_shift, second_gain,
    second_shift, cotangent,
):
    owned, super_width = query_weight.shape
    super_hidden = up_weight.shape[1]
    ratio = super_hidden // super_width
    gather = lambda part: lax.all_gather(part, "fsdp", axis=0, tiled=True)
    small = jnp.stack(
        [
            query_bias, value_bias, out_bias, down_bias,
            first_gain, first_shift, second_gain, second_shift,
        ],
        axis=1,
    )
    small = jnp.concatenate([small, up_bias.reshape(owned, ratio)], axis=1)
    small = widen(small, owned, 128)
    local = jnp.concatenate(
        [query_weight[:, :WIDTH], key_weight[:, :WIDTH], value_weight[:, :WIDTH], small], axis=1
    )
    first_chunk = gather(local)
    out_sub = gather(out_weight[:, :WIDTH])
    up_sub = gather(up_weight[:, :HIDDEN_SIZE])
    down_sub = gather(down_weight[:, :WIDTH])
    base = 3 * WIDTH
    vectors = first_chunk[:WIDTH, base : base + 8].astype(F32).T
    up_row = first_chunk[:, base + 8 : base + 8 + ratio].astype(F32).reshape(1, super_hidden)
    up_row = up_row[:, :HIDDEN_SIZE]

    exps, context, wide, inverse, query_t, key, value_t = attend(
        tokens, lengths, first_chunk, vectors
    )
    output, normed, active, grad_hidden, grad_feed, grad_first, grad_context, sums, up_sum = feed(
        lengths, context, tokens, cotangent, out_sub, up_sub, down_sub, vectors, up_row
    )
    grad_queries, grad_keys, grad_values, pair_sums = attend_back(
        grad_context, wide, inverse, exps, query_t, key, value_t
    )
    token_grad = (
        grad_first
        + dot(grad_queries, first_chunk[:WIDTH, :WIDTH], 1, 1)
        + dot(grad_keys, first_chunk[:WIDTH, WIDTH : 2 * WIDTH], 1, 1)
        + dot(grad_values, first_chunk[:WIDTH, 2 * WIDTH : base], 1, 1)
    ).astype(BF)
    term = lambda left, right: dot(left, right, 0, 0).astype(BF)
    scatter = lambda part: lax.psum_scatter(part, "fsdp", scatter_dimension=0, tiled=True)
    up_wide = jnp.pad(up_sum[0], (0, super_hidden - HIDDEN_SIZE)).reshape(super_width, ratio)
    small_terms = jnp.concatenate(
        [
            widen(jnp.concatenate([sums[:6], pair_sums[:2]], axis=0), 8, super_width).T,
            up_wide,
        ],
        axis=1,
    )
    small_terms = widen(small_terms, super_width, 128).astype(BF)
    qkv_terms = jnp.concatenate(
        [term(tokens, grad_queries), term(tokens, grad_keys), term(tokens, grad_values)], axis=1
    )
    summed = (
        scatter(
            jnp.concatenate([widen(qkv_terms, super_width, 3 * WIDTH), small_terms], axis=1)
        ),
        scatter(widen(term(context, grad_first.astype(BF)), super_width, WIDTH)),
        scatter(widen(term(normed, grad_hidden), super_width, HIDDEN_SIZE)),
        scatter(widen(term(active, grad_feed), super_hidden, WIDTH)),
    )
    first, out_total, up_total, down_total = [
        lax.psum(part, "dp").astype(F32) for part in summed
    ]
    full = lambda part: widen(part, part.shape[0], super_width)
    vector = lambda i: first[:, base + i]
    return (
        output,
        token_grad,
        full(first[:, :WIDTH]),
        full(first[:, WIDTH : 2 * WIDTH]),
        full(first[:, 2 * WIDTH : base]),
        full(out_total),
        widen(up_total, owned, super_hidden),
        full(down_total),
        vector(6),
        vector(7),
        vector(0),
        first[:, base + 8 : base + 8 + ratio].reshape(-1),
        vector(1),
        vector(2),
        vector(3),
        vector(4),
        vector(5),
    )


def solution(mesh):
    rows = P(("dp", "fsdp"), None)
    held = P("fsdp", None)
    line = P("fsdp")
    return jax.shard_map(
        on_device,
        mesh=mesh,
        in_specs=(rows, P(("dp", "fsdp"))) + (held,) * 6 + (line,) * 9 + (rows,),
        out_specs=(rows, rows) + (held,) * 6 + (line,) * 9,
        check_vma=False,
    )
```

```python
import functools

import jax
import jax.numpy as jnp
from jax import lax
from jax.experimental import pallas as pl
from jax.experimental.pallas import tpu as pltpu
from jax.sharding import PartitionSpec as P

HEAD_DIM = 64
HIDDEN_SIZE = 2240
WIDTH = 640
EPSILON = 1e-05
MASKED = -1e30
PAIR = 2 * HEAD_DIM
PAIRS = WIDTH // PAIR
BF = jnp.bfloat16
F32 = jnp.float32
VMEM_BYTES = 60 * 2**20
BLOCKS = 8
BLOCK = 96
QUARTERS = 4
LAYERS = BLOCKS // 2
HIDDEN_PAD = 2304
UP_PART = 768
PEAK = 10**9


def dot(left, right, left_dim, right_dim):
    return lax.dot_general(
        left, right, (((left_dim,), (right_dim,)), ((), ())), preferred_element_type=F32
    )


def side(shape, axis, half, own, flag):
    place = lax.broadcasted_iota(jnp.int32, shape, axis)
    mine = (place < HEAD_DIM) if half == 0 else (place >= HEAD_DIM)
    first = place == (HEAD_DIM if half == 0 else 0)
    return jnp.where(mine, own, jnp.where(first, flag, 0.0))


def rows_of(step):
    return pl.ds(pl.multiple_of(step * BLOCK, BLOCK), BLOCK)


def cost(microseconds):
    return pl.CostEstimate(flops=microseconds * PEAK, bytes_accessed=0, transcendentals=0)


def params():
    return pltpu.CompilerParams(vmem_limit_bytes=VMEM_BYTES)


SMEM = pl.BlockSpec(memory_space=pltpu.SMEM)
WHOLE = pl.BlockSpec(memory_space=pltpu.VMEM)
IDLE = pl.BlockSpec(memory_space=pl.ANY)
LENGTH, CORE, PART, LAYER = range(4)


def call_with(kernel, inputs, after, **options):
    specs = options.pop("in_specs") + [IDLE] * len(after)

    def run(*refs):
        kernel(*refs[: len(inputs)], *refs[len(inputs) + len(after) :])

    return pl.pallas_call(run, in_specs=specs, compiler_params=params(), **options)(*inputs, *after)


def pack_first_kernel(info_ref, wq_ref, wk_ref, wv_ref, *refs):
    small_refs, out_ref = refs[:9], refs[9]
    lines = [ref[...].astype(F32).reshape(1, BLOCK) for ref in small_refs[:8]]
    up_line = small_refs[8][...].astype(F32).reshape(1, -1)
    lines += [up_line[:, i * BLOCK : (i + 1) * BLOCK] for i in range(QUARTERS)]
    small = jnp.concatenate(lines + [jnp.zeros((PAIR - 12, BLOCK), F32)], axis=0).T
    place = pl.ds(pl.multiple_of((info_ref[PART] + 1) * PAIR, PAIR), PAIR)
    for i, ref in enumerate((wq_ref, wk_ref, wv_ref)):
        out_ref[:, i * PAIR : (i + 1) * PAIR] = ref[:, :PAIR]
        out_ref[:, (i + 4) * PAIR : (i + 5) * PAIR] = ref[:, place]
    out_ref[:, 3 * PAIR : 4 * PAIR] = small.astype(BF)


def pack_wide_kernel(info_ref, up_ref, wo_ref, out_ref):
    part = info_ref[PART]

    @pl.when(part < QUARTERS - 1)
    def _():
        out_ref[...] = up_ref[:, pl.ds(pl.multiple_of(part * UP_PART, UP_PART), UP_PART)]

    @pl.when(part == QUARTERS - 1)
    def _():
        out_ref[...] = wo_ref[...]


def pack(kernel, info, arrays, shape, after=()):
    return call_with(
        kernel, (info, *arrays), after,
        in_specs=[SMEM] + [WHOLE] * len(arrays),
        out_specs=WHOLE,
        out_shape=jax.ShapeDtypeStruct(shape, BF),
        cost_estimate=cost(2),
    )


def repeat_kernel(*refs):
    for i, ref in enumerate(refs[:-1]):
        for copy in range(QUARTERS):
            refs[-1][copy, i] = ref[...]


def repeat(parts, after=()):
    return call_with(
        repeat_kernel, tuple(parts), after,
        in_specs=[WHOLE] * len(parts),
        out_specs=WHOLE,
        out_shape=jax.ShapeDtypeStruct((QUARTERS, len(parts)) + parts[0].shape, BF),
        cost_estimate=cost(30),
    )


def turn_kernel(source_ref, out_ref):
    out_ref[:WIDTH, :] = source_ref[...].T
    out_ref[WIDTH:, :] = jnp.zeros((BLOCKS * BLOCK - WIDTH, source_ref.shape[0]), BF)


def turn(tokens, after=()):
    return call_with(
        turn_kernel, (tokens,), after,
        in_specs=[WHOLE],
        out_specs=WHOLE,
        out_shape=jax.ShapeDtypeStruct((BLOCKS * BLOCK, tokens.shape[0]), BF),
        cost_estimate=cost(3),
    )


def cut(down, after=()):
    return call_with(
        cut_kernel, (down,), after,
        in_specs=[WHOLE],
        out_specs=WHOLE,
        out_shape=jax.ShapeDtypeStruct((down.shape[0], WIDTH), BF),
        cost_estimate=cost(1),
    )


def cut_kernel(down_ref, out_ref):
    out_ref[...] = down_ref[:, :WIDTH]


def lay_line(info_ref, target, own_ref, twin_ref, came_ref, twins_ref):
    core, layer = info_ref[CORE], info_ref[LAYER]
    width = target.shape[1]
    target[rows_of(2 * layer + core), :] = own_ref[:, :width]
    target[rows_of(2 * layer + 1 - core), :] = twin_ref[:, :width]
    for step in range(1, LAYERS):
        source = (layer + LAYERS - step) % LAYERS
        target[rows_of(2 * source + core), :] = came_ref[step - 1, :, :width]
        target[rows_of(2 * source + 1 - core), :] = twins_ref[step - 1, :, :width]


def lay(info_ref, target, width, mine_ref, other_ref):
    core, layer = info_ref[CORE], info_ref[LAYER]
    for quarter in range(QUARTERS):
        columns = slice(quarter * width, (quarter + 1) * width)
        for slot in range(LAYERS):
            source = (layer + LAYERS - slot) % LAYERS
            target[rows_of(2 * source + core), columns] = mine_ref[quarter, slot]
            target[rows_of(2 * source + 1 - core), columns] = other_ref[quarter, slot]


def attend_kernel(shift, info_ref, token_ref, *refs):
    first = shift is None
    count = 4 if first else 2
    sources, refs = refs[:count], refs[count:]
    if first:
        vectors_ref = refs[-2]
        refs = refs[:-2] + refs[-1:]
    else:
        vectors_ref = refs[0]
        refs = refs[1:]
    (
        exp_ref, context_ref, context_t_ref, wide_ref, inverse_ref, query_t_ref, key_ref,
        value_t_ref, weight_ref,
    ) = refs
    rows = token_ref.shape[0]
    if first:
        lay_line(info_ref, weight_ref, *sources)
        vectors_ref[...] = weight_ref[:, 3 * PAIR :].astype(F32).T[:16]
        bq = vectors_ref[0:1, :PAIR]
        bv = vectors_ref[1:2, :PAIR]
        weights = weight_ref[:WIDTH, : 3 * PAIR]
    else:
        @pl.when(pl.program_id(0) == 0)
        def _():
            lay(info_ref, weight_ref, 3 * PAIR, *sources)

        pair = pl.program_id(0) + shift
        place = pl.ds(pl.multiple_of(pair * PAIR, PAIR), PAIR)
        bq = vectors_ref[0:1, place]
        bv = vectors_ref[1:2, place]
        place = pl.ds(pl.multiple_of((pair - 1) * 3 * PAIR, 3 * PAIR), 3 * PAIR)
        weights = weight_ref[:WIDTH, place]
    product = dot(token_ref[...], weights, 1, 0)
    query = (product[:, :PAIR] + bq).astype(BF)
    key = product[:, PAIR : 2 * PAIR].astype(BF)
    value = (product[:, 2 * PAIR :] + bv).astype(BF)
    key_t = key.T
    query_t_ref[...] = query.T
    key_ref[...] = key
    value_t_ref[...] = value.T
    key_place = lax.broadcasted_iota(jnp.int32, (1, rows), 1)
    bias = jnp.where(key_place < info_ref[LENGTH], 0.0, MASKED)
    scaled = query.astype(F32) * HEAD_DIM**-0.5
    key_wide = key_t.astype(F32)
    value_wide = value.astype(F32)
    block = 128
    results = []
    for half in range(2):
        left = side((rows, PAIR), 1, half, scaled, 1.0).astype(BF)
        place = lax.broadcasted_iota(jnp.int32, (PAIR, rows), 0)
        right = jnp.where(place == (HEAD_DIM if half == 0 else 0), bias, key_wide).astype(BF)
        for start in range(0, rows, block):
            scores = dot(left[start : start + block], right, 1, 0)
            highest = jnp.max(scores, 1, keepdims=True)
            exp_ref[half, start : start + block, :] = jnp.exp(scores - highest).astype(BF)
        values = side((rows, PAIR), 1, half, value_wide, 1.0).astype(BF)
        total = dot(exp_ref[half], values, 1, 0)
        flag = HEAD_DIM if half == 0 else 0
        inverse = 1.0 / total[:, flag : flag + 1]
        results.append((total * inverse, inverse))
    low = lax.broadcasted_iota(jnp.int32, (rows, PAIR), 1) < HEAD_DIM
    context = jnp.where(low, results[0][0], results[1][0])
    wide_ref[...] = context
    context_low = context.astype(BF)
    context_ref[...] = context_low
    context_t_ref[...] = context_low.T
    inverse_ref[...] = jnp.where(low, results[0][1], results[1][1])


def attend(info, tokens, sources, start, pairs, weight, vectors=None, after=()):
    rows = tokens.shape[0]
    first = vectors is None
    width = (4 if first else 12) * PAIR
    tall = lambda: pl.BlockSpec((rows, PAIR), lambda p: (0, p))
    flat = lambda: pl.BlockSpec((PAIR, rows), lambda p: (p, 0))
    array = lambda kind: jax.ShapeDtypeStruct((rows, pairs * PAIR), kind)
    turned = jax.ShapeDtypeStruct((pairs * PAIR, rows), BF)
    table = (16, BLOCKS * BLOCK)
    fixed = pl.BlockSpec(table, lambda p: (0, 0))
    return call_with(
        functools.partial(attend_kernel, None if first else start),
        (info, tokens, *sources, *(() if first else (vectors,))),
        after,
        grid=(pairs,),
        in_specs=[SMEM, WHOLE] + [WHOLE] * len(sources) + ([] if first else [fixed]),
        out_specs=[
            pl.BlockSpec((2, rows, rows), lambda p: (p, 0, 0)),
            tall(), flat(), tall(), tall(), flat(), tall(), flat(),
        ]
        + ([fixed] if first else []),
        out_shape=[
            jax.ShapeDtypeStruct((2 * pairs, rows, rows), BF),
            array(BF), turned, array(F32), array(F32), turned, array(BF), turned,
        ]
        + ([jax.ShapeDtypeStruct(table, F32)] if first else []),
        scratch_shapes=[pltpu.VMEM((BLOCKS * BLOCK, width), BF)],
        cost_estimate=cost(weight),
    )


def gelu_pair(values):
    t = 1.0 / (1.0 + (0.3275911 * 0.5**0.5) * jnp.abs(values))
    bell = jnp.exp(-0.5 * values * values)
    tail = t * (0.5 * 0.254829592 + t * (0.5 * -0.284496736 + t * (0.5 * 1.421413741 + t * (
        0.5 * -1.453152027 + t * (0.5 * 1.061405429)))))
    tail = tail * bell
    share = jnp.where(values >= 0.0, 1.0 - tail, tail)
    return values * share, share + values * bell * 0.3989422804014327


def row_mean(values):
    return jnp.sum(values, 1, keepdims=True) * (1.0 / WIDTH)


def column_sum(values):
    return jnp.sum(values, 0, keepdims=True)


def row_mean(values):
    return jnp.sum(values, 1, keepdims=True) * (1.0 / WIDTH)


def column_sum(values):
    return jnp.sum(values, 0, keepdims=True)


def up_places():
    for block in range(HIDDEN_PAD // (QUARTERS * BLOCK)):
        for quarter in range(QUARTERS):
            start = (block * QUARTERS + quarter) * BLOCK
            row = slice(8 + quarter, 9 + quarter)
            yield slice(start, start + BLOCK), row, slice(block * BLOCK, (block + 1) * BLOCK)


def feed_kernel(
    info_ref, context_0_ref, context_1_ref, context_2_ref, token_ref, cotangent_ref,
    *refs
):
    sources, refs = refs[:2], refs[2:]
    (
        down_ref, vector_ref,
        output_ref, normed_t_ref, active_ref, hidden_ref, feed_ref, first_ref, branch_ref,
        grad_context_ref, sums_ref, b1_sum_ref, w1_ref, w2_ref, b1_ref,
    ) = refs
    step = pl.program_id(0)
    rows = token_ref.shape[0]

    @pl.when(step == 0)
    def _():
        lay(info_ref, w1_ref, UP_PART, *sources)
        last = slice(HIDDEN_PAD - PAIR, HIDDEN_PAD)
        lane = lax.broadcasted_iota(jnp.int32, (BLOCKS * BLOCK, PAIR), 1)
        kept = lane < HIDDEN_SIZE - (HIDDEN_PAD - PAIR)
        w1_ref[:, last] = jnp.where(kept, w1_ref[:, last].astype(F32), 0.0).astype(BF)
        w2_ref[:HIDDEN_SIZE, :] = down_ref[:HIDDEN_SIZE, :]
        for place, row, columns in up_places():
            b1_ref[:, place] = vector_ref[row, columns]
        lane = lax.broadcasted_iota(jnp.int32, (1, HIDDEN_PAD), 1)
        b1_ref[...] = jnp.where(lane < HIDDEN_SIZE, b1_ref[...], 0.0)
        w2_ref[HIDDEN_SIZE:, :] = jnp.zeros((HIDDEN_PAD - HIDDEN_SIZE, WIDTH), BF)

    wo = w1_ref[:WIDTH, HIDDEN_PAD : HIDDEN_PAD + WIDTH]
    w1, w2 = w1_ref[:WIDTH, :HIDDEN_PAD], w2_ref[...]
    place = lax.broadcasted_iota(jnp.int32, (rows, 1), 0) + step * rows
    live = jnp.where(place < info_ref[LENGTH], 1.0, 0.0)
    vector = lambda i: vector_ref[i : i + 1, :WIDTH]
    out_add, down_add = vector(2), vector(3)
    gain_one, shift_one, gain_two, shift_two = vector(4), vector(5), vector(6), vector(7)
    context = jnp.concatenate([context_0_ref[...], context_1_ref[...], context_2_ref[...]], axis=1)
    first_sum = token_ref[...].astype(F32) + dot(context, wo, 1, 0) + out_add
    center = first_sum - row_mean(first_sum)
    rate_one = lax.rsqrt(row_mean(center * center) + EPSILON)
    unit_one = center * rate_one
    normed = (unit_one * gain_one + shift_one).astype(BF)
    normed_t_ref[:WIDTH, :] = normed.T
    normed_t_ref[WIDTH:, :] = jnp.zeros((BLOCKS * BLOCK - WIDTH, rows), BF)
    pre = dot(normed, w1, 1, 0) + b1_ref[...]
    active_full, slope = gelu_pair(pre)
    active = active_full.astype(BF)
    active_ref[...] = active
    second_sum = normed.astype(F32) + dot(active, w2, 1, 0) + down_add
    center = second_sum - row_mean(second_sum)
    rate_two = lax.rsqrt(row_mean(center * center) + EPSILON)
    unit_two = center * rate_two
    output_ref[...] = ((unit_two * gain_two + shift_two) * live).astype(BF)
    cotangent = cotangent_ref[...].astype(F32) * live
    inner = cotangent * gain_two
    grad_second = rate_two * (inner - row_mean(inner) - unit_two * row_mean(inner * unit_two))
    grad_feed = grad_second.astype(BF)
    feed_ref[...] = grad_feed
    grad_hidden = (dot(grad_feed, w2, 1, 1) * slope).astype(BF)
    hidden_ref[...] = grad_hidden
    grad_normed = grad_second + dot(grad_hidden, w1, 1, 1)
    inner = grad_normed * gain_one
    grad_first = rate_one * (inner - row_mean(inner) - unit_one * row_mean(inner * unit_one))
    first_ref[...] = grad_first
    grad_branch = grad_first.astype(BF)
    branch_ref[...] = grad_branch
    grad_context_ref[...] = dot(grad_branch, wo, 1, 1).astype(BF)
    sums = jnp.concatenate(
        [
            column_sum(grad_branch.astype(F32)),
            column_sum(grad_feed.astype(F32)),
            column_sum(grad_normed * unit_one),
            column_sum(grad_normed),
            column_sum(cotangent * unit_two),
            column_sum(cotangent),
            jnp.zeros((2, WIDTH), F32),
        ],
        axis=0,
    )
    b1_sum = column_sum(grad_hidden.astype(F32))

    @pl.when(step == 0)
    def _():
        sums_ref[...] = sums
        b1_sum_ref[...] = b1_sum

    @pl.when(step > 0)
    def _():
        sums_ref[...] += sums
        b1_sum_ref[...] += b1_sum


def feed(info, contexts, tokens, cotangent, wide, down, vectors):
    rows = tokens.shape[0]
    tile = 256
    part = lambda width: pl.BlockSpec((tile, width), lambda i: (i, 0))
    whole = lambda *shape: pl.BlockSpec(shape, lambda i: (0, 0))
    array = lambda width, kind: jax.ShapeDtypeStruct((rows, width), kind)
    return pl.pallas_call(
        feed_kernel,
        grid=(rows // tile,),
        in_specs=[SMEM]
        + [part(context.shape[1]) for context in contexts]
        + [part(WIDTH), part(WIDTH)]
        + [WHOLE] * len(wide)
        + [WHOLE]
        + [whole(*vectors.shape)],
        out_specs=[
            part(WIDTH), pl.BlockSpec((BLOCKS * BLOCK, tile), lambda i: (0, i)),
            part(HIDDEN_PAD), part(HIDDEN_PAD), part(WIDTH),
            part(WIDTH), part(WIDTH), part(WIDTH), whole(8, WIDTH), whole(1, HIDDEN_PAD),
        ],
        out_shape=[
            array(WIDTH, BF), jax.ShapeDtypeStruct((BLOCKS * BLOCK, rows), BF),
            array(HIDDEN_PAD, BF), array(HIDDEN_PAD, BF),
            array(WIDTH, BF), array(WIDTH, F32), array(WIDTH, BF), array(WIDTH, BF),
            jax.ShapeDtypeStruct((8, WIDTH), F32),
            jax.ShapeDtypeStruct((1, HIDDEN_PAD), F32),
        ],
        scratch_shapes=[
            pltpu.VMEM((BLOCKS * BLOCK, QUARTERS * UP_PART), BF),
            pltpu.VMEM((HIDDEN_PAD, WIDTH), BF),
            pltpu.VMEM((1, HIDDEN_PAD), F32),
        ],
        compiler_params=params(),
        cost_estimate=cost(40),
    )(info, *contexts, tokens, cotangent, *wide, down, vectors)


def down_grad_kernel(active_ref, feed_ref, out_ref):
    out_ref[...] = dot(active_ref[...], feed_ref[...], 0, 0).astype(BF)


def down_grad(active, grad_feed, super_hidden, after=()):
    rows = active.shape[0]
    deep = UP_PART
    return call_with(
        down_grad_kernel, (active, grad_feed), after,
        grid=(HIDDEN_PAD // deep,),
        in_specs=[
            pl.BlockSpec((rows, deep), lambda i: (0, i)),
            pl.BlockSpec((rows, WIDTH), lambda i: (0, 0)),
        ],
        out_specs=pl.BlockSpec((deep, WIDTH), lambda i: (i, 0)),
        out_shape=jax.ShapeDtypeStruct((super_hidden, WIDTH), BF),
        cost_estimate=cost(8),
    )


def deal(info_ref, product_ref, keep_ref, send_ref):
    core = info_ref[CORE]
    for layer in range(LAYERS):
        keep_ref[0, layer] = product_ref[rows_of(2 * layer + core), :].astype(BF)
        send_ref[0, layer] = product_ref[rows_of(2 * layer + 1 - core), :].astype(BF)


def up_grad_kernel(info_ref, normed_t_ref, hidden_ref, *refs):
    context_refs, branch_ref, keep_ref, send_ref, product_ref = refs[:3], *refs[3:]
    step = pl.program_id(0)

    @pl.when(step < QUARTERS - 1)
    def _():
        product_ref[...] = dot(normed_t_ref[...], hidden_ref[...], 1, 0)

    @pl.when(step == QUARTERS - 1)
    def _():
        start = 0
        for ref in context_refs:
            product_ref[start : start + ref.shape[0], :WIDTH] = dot(ref[...], branch_ref[...], 1, 0)
            start += ref.shape[0]

    deal(info_ref, product_ref, keep_ref, send_ref)


def up_grad(info, normed_t, grad_hidden, contexts_t, branch, after=()):
    rows = branch.shape[0]
    place = lambda: pl.BlockSpec((1, LAYERS, BLOCK, UP_PART), lambda d: (d, 0, 0, 0))
    array = jax.ShapeDtypeStruct((QUARTERS, LAYERS, BLOCK, UP_PART), BF)
    hidden = pl.BlockSpec((rows, UP_PART), lambda d: (0, jnp.minimum(d, QUARTERS - 2)))
    return call_with(
        up_grad_kernel, (info, normed_t, grad_hidden, *contexts_t, branch), after,
        grid=(QUARTERS,),
        in_specs=[SMEM, WHOLE, hidden] + [WHOLE] * (len(contexts_t) + 1),
        out_specs=[place(), place()],
        out_shape=[array, array],
        scratch_shapes=[pltpu.VMEM((BLOCKS * BLOCK, UP_PART), F32)],
        cost_estimate=cost(11),
    )


def head_grad_kernel(info_ref, token_t_ref, low_ref, high_ref, keep_ref, send_ref, product_ref):
    step = pl.program_id(0)
    half = low_ref.shape[0]

    @pl.when(step < half)
    def _():
        product_ref[...] = dot(token_t_ref[...], low_ref[jnp.minimum(step, half - 1)], 1, 0)

    @pl.when(step >= half)
    def _():
        product_ref[...] = dot(token_t_ref[...], high_ref[jnp.maximum(step - half, 0)], 1, 0)

    deal(info_ref, product_ref, keep_ref, send_ref)


def head_grad(info, token_t, low, high, after=()):
    place = lambda: pl.BlockSpec((1, LAYERS, BLOCK, 3 * PAIR), lambda d: (d, 0, 0, 0))
    array = jax.ShapeDtypeStruct((QUARTERS, LAYERS, BLOCK, 3 * PAIR), BF)
    return call_with(
        head_grad_kernel, (info, token_t, low, high), after,
        grid=(QUARTERS,),
        in_specs=[SMEM] + [WHOLE] * 3,
        out_specs=[place(), place()],
        out_shape=[array, array],
        scratch_shapes=[pltpu.VMEM((BLOCKS * BLOCK, 3 * PAIR), F32)],
        cost_estimate=cost(6),
    )


def first_grad_kernel(
    info_ref, token_t_ref, together_ref, sums_ref, up_sum_ref, pair_0_ref, pair_1_ref, pair_2_ref,
    keep_ref, send_ref, product_ref, table_ref,
):
    product_ref[:, : 3 * PAIR] = dot(token_t_ref[...], together_ref[0], 1, 0)
    table_ref[...] = jnp.zeros_like(table_ref)
    start = 0
    for ref in (pair_0_ref, pair_1_ref, pair_2_ref):
        table_ref[0:2, start : start + ref.shape[1]] = ref[0:2, :]
        start += ref.shape[1]
    table_ref[2:8, :WIDTH] = sums_ref[0:6, :]
    for place, row, columns in up_places():
        table_ref[row, columns] = up_sum_ref[:, place]
    product_ref[:, 3 * PAIR :] = table_ref[...].T
    core = info_ref[CORE]
    for layer in range(LAYERS):
        kept = product_ref[rows_of(2 * layer + core), :].astype(BF)
        sent = product_ref[rows_of(2 * layer + 1 - core), :].astype(BF)
        for part in range(QUARTERS):
            columns = slice(part * PAIR, (part + 1) * PAIR)
            keep_ref[part, layer] = kept[:, columns]
            send_ref[part, layer] = sent[:, columns]


def first_grad(info, token_t, together, sums, up_sum, pair_sums, after=()):
    array = jax.ShapeDtypeStruct((QUARTERS, LAYERS, BLOCK, PAIR), BF)
    return call_with(
        first_grad_kernel, (info, token_t, together, sums, up_sum, *pair_sums), after,
        in_specs=[SMEM] + [WHOLE] * 7,
        out_specs=[WHOLE] * 2,
        out_shape=[array, array],
        scratch_shapes=[
            pltpu.VMEM((BLOCKS * BLOCK, 4 * PAIR), F32),
            pltpu.VMEM((PAIR, BLOCKS * BLOCK), F32),
        ],
        cost_estimate=cost(3),
    )


def meet_kernel(info_ref, keep_ref, came_ref, *out_refs):
    for apart in range(QUARTERS):
        quarter = info_ref[PART] ^ apart
        out_refs[apart][0] = keep_ref[quarter, 0] + came_ref[quarter, 0]


def meet(info, keep, came, after=()):
    width = keep.shape[-1]
    block = lambda: pl.BlockSpec(
        (QUARTERS, 1, BLOCK, width), lambda s, info: (0, (info[LAYER] + s) % LAYERS, 0, 0)
    )

    def run(info_ref, keep_ref, came_ref, *refs):
        meet_kernel(info_ref, keep_ref, came_ref, *refs[len(after) :])

    return pl.pallas_call(
        run,
        grid_spec=pltpu.PrefetchScalarGridSpec(
            num_scalar_prefetch=1,
            grid=(LAYERS,),
            in_specs=[block(), block()] + [IDLE] * len(after),
            out_specs=[pl.BlockSpec((1, BLOCK, width), lambda s, info: (s, 0, 0))] * QUARTERS,
        ),
        out_shape=[jax.ShapeDtypeStruct((LAYERS, BLOCK, width), BF)] * QUARTERS,
        compiler_params=params(),
        cost_estimate=cost(3),
    )(info, keep, came, *after)


def attend_back_kernel(
    grad_ref, wide_ref, inverse_ref, exp_ref, query_t_ref, key_ref, value_t_ref,
    together_ref, sums_ref, score_ref,
):
    rows = grad_ref.shape[0]
    inverse = inverse_ref[...]
    grad = grad_ref[...].astype(F32)
    scaled = grad * inverse
    dots = scaled * wide_ref[...]
    scaled_t = scaled.T.astype(BF)
    value_wide = value_t_ref[...].astype(F32)
    lane = lax.broadcasted_iota(jnp.int32, (rows, PAIR), 1)
    place = lax.broadcasted_iota(jnp.int32, (PAIR, rows), 0)
    block = 128
    dq, dk_t, dv_t = [], [], []
    for half in range(2):
        mine = (lane < HEAD_DIM) if half == 0 else (lane >= HEAD_DIM)
        flag = HEAD_DIM if half == 0 else 0
        offset = jnp.sum(jnp.where(mine, -dots, 0.0), 1, keepdims=True)
        high = offset.astype(BF).astype(F32)
        rest = offset - high
        left = jnp.where(
            mine, scaled, jnp.where(lane == flag, high, jnp.where(lane == flag + 1, rest, 0.0))
        ).astype(BF)
        right = jnp.where((place == flag) | (place == flag + 1), 1.0, value_wide).astype(BF)
        for start in range(0, rows, block):
            grad_probs = dot(left[start : start + block], right, 1, 0)
            weight = exp_ref[half, start : start + block, :].astype(F32)
            score_ref[half, start : start + block, :] = (grad_probs * weight).astype(BF)
        own = slice(half * HEAD_DIM, (half + 1) * HEAD_DIM)
        dv_t.append(dot(scaled_t[own], exp_ref[half], 1, 0))
        dk_t.append(dot(query_t_ref[own, :], score_ref[half], 1, 0))
        dq.append(dot(score_ref[half], key_ref[...], 1, 0))
    factor = HEAD_DIM**-0.5
    dq_low = (jnp.where(lane < HEAD_DIM, dq[0], dq[1]) * factor).astype(BF)
    dk_low = (jnp.concatenate(dk_t, axis=0) * factor).T.astype(BF)
    dv_low = jnp.concatenate(dv_t, axis=0).T.astype(BF)
    together_ref[0] = jnp.concatenate([dq_low, dk_low, dv_low], axis=1)
    query_sum = column_sum(dq_low.astype(F32))
    value_sum = column_sum(dv_low.astype(F32))
    sums_ref[...] = jnp.concatenate([query_sum, value_sum, jnp.zeros((6, PAIR), F32)], axis=0)


def attend_back(grad_context, saved, start, pairs, weight, after=()):
    exps, wide, inverse, query_t, key, value_t = saved
    rows = grad_context.shape[0]
    tall = lambda first: pl.BlockSpec((rows, PAIR), lambda p: (0, first + p))
    flat = lambda: pl.BlockSpec((PAIR, rows), lambda p: (p, 0))
    return call_with(
        attend_back_kernel,
        (grad_context, wide, inverse, exps, query_t, key, value_t),
        after,
        grid=(pairs,),
        in_specs=[
            tall(start), tall(0), tall(0),
            pl.BlockSpec((2, rows, rows), lambda p: (p, 0, 0)),
            flat(), tall(0), flat(),
        ],
        out_specs=[
            pl.BlockSpec((1, rows, 3 * PAIR), lambda p: (p, 0, 0)),
            pl.BlockSpec((8, PAIR), lambda p: (0, p)),
        ],
        out_shape=[
            jax.ShapeDtypeStruct((pairs, rows, 3 * PAIR), BF),
            jax.ShapeDtypeStruct((8, pairs * PAIR), F32),
        ],
        scratch_shapes=[pltpu.VMEM((2, rows, rows), BF)],
        cost_estimate=cost(weight),
    )


def token_kernel(info_ref, grad_ref, together_0_ref, together_1_ref, together_2_ref, *refs):
    count = 4
    first_sources, rest_sources = refs[:count], refs[count : count + 2]
    out_ref, first_ref, rest_ref = refs[-3:]

    @pl.when(pl.program_id(0) == 0)
    def _():
        lay_line(info_ref, first_ref, *first_sources)
        lay(info_ref, rest_ref, 3 * PAIR, *rest_sources)

    pieces = [ref[i] for ref in (together_1_ref, together_2_ref) for i in range(ref.shape[0])]
    total = grad_ref[...] + dot(together_0_ref[0], first_ref[:WIDTH, : 3 * PAIR], 1, 1)
    total += dot(jnp.concatenate(pieces, axis=1), rest_ref[:WIDTH, :], 1, 1)
    out_ref[...] = total.astype(BF)


def token_back(info, grad_first, togethers, first, rest, after):
    rows = grad_first.shape[0]
    tile = 256
    part = pl.BlockSpec((tile, WIDTH), lambda i: (i, 0))
    piece = lambda array: pl.BlockSpec((array.shape[0], tile, 3 * PAIR), lambda i: (0, i, 0))
    return call_with(
        token_kernel, (info, grad_first, *togethers, *first, *rest), after,
        grid=(rows // tile,),
        in_specs=[SMEM, part]
        + [piece(array) for array in togethers]
        + [WHOLE] * (len(first) + len(rest)),
        out_specs=part,
        out_shape=jax.ShapeDtypeStruct((rows, WIDTH), BF),
        scratch_shapes=[
            pltpu.VMEM((BLOCKS * BLOCK, 4 * PAIR), BF),
            pltpu.VMEM((BLOCKS * BLOCK, 12 * PAIR), BF),
        ],
        cost_estimate=cost(7),
    )


def plane_kernel(groups, *refs):
    inputs, outputs = refs[: groups * QUARTERS], refs[groups * QUARTERS :]
    start = 0
    for group in range(groups):
        mine = inputs[group * QUARTERS : (group + 1) * QUARTERS]
        width = mine[0].shape[-1]
        for step in range(LAYERS):
            total = sum(ref[step].astype(F32) for ref in mine)
            outputs[step][:, start : start + width] = total.astype(BF)
        start += width


def plane(groups, after=()):
    width = sum(group[0].shape[-1] for group in groups)
    return call_with(
        functools.partial(plane_kernel, len(groups)),
        tuple(array for group in groups for array in group),
        after,
        in_specs=[WHOLE] * (len(groups) * QUARTERS),
        out_specs=[WHOLE] * LAYERS,
        out_shape=[jax.ShapeDtypeStruct((BLOCK, width), BF)] * LAYERS,
        cost_estimate=cost(2),
    )


def line_kernel(counts, *refs):
    inputs, out_ref = refs[:-1], refs[-1]
    start = 0
    for count in counts:
        mine, inputs = inputs[:count], inputs[count:]
        width = mine[0].shape[-1]
        parts = [ref[...] for ref in mine] if count > 1 else [mine[0][i] for i in range(QUARTERS)]
        total = sum(part.astype(F32) for part in parts).astype(BF)
        for copy in range(QUARTERS):
            out_ref[copy, :, start : start + width] = total
        start += width


def line(groups, after=()):
    width = sum(group[0].shape[-1] for group in groups)
    arrays = tuple(array for group in groups for array in group)
    return call_with(
        functools.partial(line_kernel, [len(group) for group in groups]), arrays, after,
        in_specs=[WHOLE] * len(arrays),
        out_specs=WHOLE,
        out_shape=jax.ShapeDtypeStruct((QUARTERS, BLOCK, width), BF),
        cost_estimate=cost(1),
    )


def finish_kernel(info_ref, wide_ref, heads_ref, *refs):
    wq_ref, wk_ref, wv_ref, wo_ref, up_ref, down_ref = refs[:6]
    line_refs, up_line_ref = refs[6:14], refs[14]
    extra = wq_ref.shape[1] - WIDTH
    blank = jnp.zeros((BLOCK, extra), F32)
    used = HIDDEN_PAD // (QUARTERS * BLOCK)
    owner = 2 * info_ref[LAYER] + info_ref[CORE]
    for quarter in range(QUARTERS):
        lines = slice(quarter * BLOCK, (quarter + 1) * BLOCK)
        down = wide_ref[quarter, :, UP_PART:].astype(F32)
        down_ref[lines, :WIDTH] = jnp.where(owner < used, down, 0.0)
        down_ref[lines, WIDTH:] = blank
    for quarter in range(QUARTERS - 1):
        columns = slice(quarter * UP_PART, (quarter + 1) * UP_PART)
        up_ref[:, columns] = wide_ref[quarter, :, :UP_PART].astype(F32)
    up_ref[:, HIDDEN_PAD:] = jnp.zeros((BLOCK, up_ref.shape[1] - HIDDEN_PAD), F32)
    wo_ref[:, :WIDTH] = wide_ref[QUARTERS - 1, :, :WIDTH].astype(F32)
    wo_ref[:, WIDTH:] = blank
    for i, ref in enumerate((wq_ref, wk_ref, wv_ref)):
        ref[:, :PAIR] = heads_ref[i, :, 3 * PAIR :].astype(F32)
        for pair in range(1, PAIRS):
            part = heads_ref[pair - 1, :, i * PAIR : (i + 1) * PAIR]
            ref[:, pair * PAIR : (pair + 1) * PAIR] = part.astype(F32)
        ref[:, WIDTH:] = blank
    lines = heads_ref[QUARTERS - 1, :, 3 * PAIR :].astype(F32).T
    for i, ref in enumerate(line_refs):
        ref[...] = lines[i]
    up_line_ref[...] = lines[8 : 8 + QUARTERS]


def finish(info, wide, heads, super_width, super_hidden):
    array = lambda *shape: jax.ShapeDtypeStruct(shape, F32)
    square = array(BLOCK, super_width)
    return pl.pallas_call(
        finish_kernel,
        in_specs=[SMEM] + [WHOLE] * 2,
        out_specs=[WHOLE] * 15,
        out_shape=[
            square, square, square, square, array(BLOCK, super_hidden),
            array(QUARTERS * BLOCK, super_width),
        ]
        + [array(BLOCK)] * 8
        + [array(QUARTERS, BLOCK)],
        compiler_params=params(),
        cost_estimate=cost(4),
    )(info, wide, heads)


SWAP = [(i, i ^ 1) for i in range(BLOCKS)]
STEPS = range(1, LAYERS)
DISTANCES = range(1, QUARTERS)


def twin(part):
    return lax.ppermute(part, "fsdp", SWAP)


def along(part, step):
    pairs = [(i, (i + 2 * step) % BLOCKS) for i in range(BLOCKS)]
    return lax.ppermute(part, "fsdp", pairs)


LINES = [[2 * layer + core for layer in range(LAYERS)] for core in range(2)]


def trade_plane(parts):
    return lax.all_to_all(parts, "dp", 0, 0)


def trade_line(parts):
    return lax.all_to_all(parts, "fsdp", 0, 0, axis_index_groups=LINES)


def copies(part):
    return jnp.broadcast_to(part[None], (QUARTERS,) + part.shape)


def across(part, apart):
    return lax.ppermute(part, "dp", [(i, i ^ apart) for i in range(QUARTERS)])


def drop(saved):
    return (saved[0],) + tuple(saved[3:])


def on_device(
    tokens, lengths, query_weight, key_weight, value_weight, out_weight, up_weight, down_weight,
    query_bias, value_bias, out_bias, up_bias, down_bias, first_gain, first_shift, second_gain,
    second_shift, cotangent,
):
    super_width, super_hidden = query_weight.shape[1], up_weight.shape[1]
    index = lax.axis_index("fsdp").astype(jnp.int32)
    part = lax.axis_index("dp").astype(jnp.int32)
    info = jnp.stack([lengths[0], index % 2, part, index // 2])
    qkv = (query_weight, key_weight, value_weight)
    small = (
        query_bias, value_bias, out_bias, down_bias,
        first_gain, first_shift, second_gain, second_shift, up_bias,
    )
    first_own = pack(pack_first_kernel, info, qkv + small, (BLOCK, 7 * PAIR))
    first_came = [along(first_own, step) for step in STEPS]
    token_t = turn(tokens, after=(first_own,))
    wide_own = pack(
        pack_wide_kernel, info, (up_weight, out_weight), (BLOCK, UP_PART), after=(token_t,)
    )
    first_line = jnp.stack(first_came)
    first = (first_own, twin(first_own), first_line, twin(first_line))
    rest_line = jnp.concatenate([first_own[None], first_line])[:, :, 4 * PAIR :]
    rest_mine = trade_plane(copies(rest_line))
    down_cut = cut(down_weight, after=(wide_own, *first))
    wide_line = [wide_own] + [along(wide_own, step) for step in STEPS]
    down = lax.all_gather(down_cut, "fsdp", axis=0, tiled=True)
    *saved_0, vectors = attend(info, tokens, first, 0, 1, 8, after=(down_cut,))
    rest = (rest_mine, twin(rest_mine))
    wide_mine = trade_plane(repeat(wide_line, after=(saved_0[1],)))
    saved_1 = attend(info, tokens, rest, 1, 3, 50, vectors, after=wide_line)
    wide = (wide_mine, twin(wide_mine))
    saved_2 = attend(info, tokens, rest, 4, 1, 50, vectors, after=(saved_1[1], wide_mine))
    all_saved = (saved_0, saved_1, saved_2)
    contexts = [saved[1] for saved in all_saved]
    contexts_t = [saved[2] for saved in all_saved]
    (
        output, normed_t, active, grad_hidden, grad_feed, grad_first, branch, grad_context, sums, up_sum
    ) = feed(info, contexts, tokens, cotangent, wide, down, vectors)

    terms = (info, normed_t, grad_hidden, contexts_t, branch)
    up_keep, up_send = up_grad(*terms)
    down_term = down_grad(active, grad_feed, super_hidden, after=(up_keep,))
    down_total = lax.psum_scatter(down_term, "fsdp", scatter_dimension=0, tiled=True)
    up_near = meet(info, up_keep, twin(up_send), after=(down_term,))
    send = lambda near: [near[0]] + [across(near[apart], apart) for apart in DISTANCES]
    pass_on = lambda layers: [layers[0]] + [along(layers[step], step) for step in STEPS]
    up_plane = send(up_near)
    together_1, sums_1 = attend_back(grad_context, drop(saved_1), 1, 3, 1, after=(up_near[0],))
    up_layers = plane([up_plane], after=(together_1,))
    up_line = pass_on(up_layers)
    together_2, sums_2 = attend_back(grad_context, drop(saved_2), 4, 1, 50, after=(up_layers[0],))
    head_keep, head_send = head_grad(info, token_t, together_1, together_2, after=up_line[1:])
    down_plane = trade_plane(down_total.reshape(QUARTERS, BLOCK, WIDTH))
    head_near = meet(info, head_keep, twin(head_send), after=(down_total,))
    head_plane = send(head_near)
    together_0, sums_0 = attend_back(
        grad_context, drop(saved_0), 0, 1, 8, after=(head_near[0],)
    )
    first_keep, first_send = first_grad(
        info, token_t, together_0, sums, up_sum, (sums_0, sums_1, sums_2),
        after=(down_plane, *head_plane[1:]),
    )
    wide_copies = line([up_line, [down_plane]], after=(first_keep,))
    wide_total = trade_plane(wide_copies)
    first_near = meet(info, first_keep, twin(first_send), after=(wide_copies,))
    first_plane = send(first_near)
    layers = plane([head_plane, first_plane])
    token_grad = token_back(
        info, grad_first, (together_0, together_1, together_2), first, rest, (layers[0],)
    )
    head_total = trade_plane(line([pass_on(layers)], after=(token_grad, wide_total)))
    *results, up_lines = finish(info, wide_total, head_total, super_width, super_hidden)
    matrices, lines = results[:6], results[6:]
    order = lines[:3] + [up_lines.reshape(-1)] + lines[3:]
    return (output, token_grad, *matrices, *order)


def widen(matrix, row_count, column_count):
    return jnp.pad(matrix, ((0, row_count - matrix.shape[0]), (0, column_count - matrix.shape[1])))


def on_device_elsewhere(
    tokens, lengths, query_weight, key_weight, value_weight, out_weight, up_weight, down_weight,
    query_bias, value_bias, out_bias, up_bias, down_bias, first_gain, first_shift, second_gain,
    second_shift, cotangent,
):
    owned, super_width = query_weight.shape
    super_hidden = up_weight.shape[1]
    info = jnp.stack([lengths[0]] + [jnp.zeros((), jnp.int32)] * 3)
    gather = lambda array: lax.all_gather(array, "fsdp", axis=0, tiled=True)
    qkv = [gather(array) for array in (query_weight, key_weight, value_weight)]
    lines = [
        gather(array)
        for array in (
            query_bias, value_bias, out_bias, down_bias,
            first_gain, first_shift, second_gain, second_shift,
        )
    ]
    up_lines = gather(up_bias).reshape(BLOCKS, QUARTERS, BLOCK).transpose(1, 0, 2)
    lines = jnp.concatenate([jnp.stack(lines), up_lines.reshape(QUARTERS, -1)], axis=0)
    columns = jnp.pad(lines, ((0, PAIR - lines.shape[0]), (0, 0))).T
    first_full = jnp.concatenate([array[:, :PAIR] for array in qkv] + [columns], axis=1)
    places = [slice(pair * PAIR, (pair + 1) * PAIR) for pair in range(1, PAIRS)]
    rest_full = jnp.concatenate([array[:, place] for place in places for array in qkv], axis=1)
    wide_full = jnp.concatenate([gather(up_weight)[:, :HIDDEN_PAD], gather(out_weight)], axis=1)
    down = gather(down_weight)[:, :WIDTH]

    back = [(LAYERS - slot) % LAYERS for slot in range(LAYERS)]

    def pieces(full):
        blocks = full.reshape(LAYERS, 2, BLOCK, QUARTERS, -1).transpose(0, 1, 3, 2, 4)
        blocks = jnp.stack([blocks[layer] for layer in back], axis=2)
        return blocks[0], blocks[1]

    blocks = first_full.reshape(LAYERS, 2, BLOCK, -1)
    blocks = jnp.stack([blocks[layer] for layer in back])
    first = (blocks[0, 0], blocks[0, 1], blocks[1:, 0], blocks[1:, 1])
    rest, wide = pieces(rest_full), pieces(wide_full)
    token_t = turn(tokens)
    *saved_0, vectors = attend(info, tokens, first, 0, 1, 8)
    saved_1 = attend(info, tokens, rest, 1, 3, 50, vectors)
    saved_2 = attend(info, tokens, rest, 4, 1, 50, vectors)
    all_saved = (saved_0, saved_1, saved_2)
    contexts = [saved[1] for saved in all_saved]
    contexts_t = [saved[2] for saved in all_saved]
    (
        output, normed_t, active, grad_hidden, grad_feed, grad_first, branch, grad_context, sums, up_sum
    ) = feed(info, contexts, tokens, cotangent, wide, down, vectors)
    deep = lax.broadcasted_iota(jnp.int32, (super_hidden, 1), 0)
    down_term = jnp.where(deep < HIDDEN_PAD, down_grad(active, grad_feed, super_hidden), 0.0)
    terms = (info, normed_t, grad_hidden, contexts_t, branch)
    together_1, sums_1 = attend_back(grad_context, drop(saved_1), 1, 3, 1)
    together_2, sums_2 = attend_back(grad_context, drop(saved_2), 4, 1, 1)
    together_0, sums_0 = attend_back(grad_context, drop(saved_0), 0, 1, 1)
    heads = (info, token_t, together_1, together_2)
    firsts = (info, token_t, together_0, sums, up_sum, (sums_0, sums_1, sums_2))

    def both(parts):
        return jnp.stack(parts, axis=2).transpose(1, 2, 3, 0, 4).reshape(super_width, -1)

    def total(array):
        array = lax.psum_scatter(array, "fsdp", scatter_dimension=0, tiled=True)
        return lax.psum(array, "dp").astype(F32)

    wide_total = total(both(up_grad(*terms)))
    heads_total = total(both(head_grad(*heads))).reshape(owned, PAIRS - 1, 3, PAIR)
    first_total = total(both(first_grad(*firsts)))
    down_total = total(down_term)
    token_grad = token_back(
        info, grad_first, (together_0, together_1, together_2), first, rest, ()
    )
    full = lambda matrix: widen(matrix, owned, super_width)
    heads = [
        full(
            jnp.concatenate(
                [first_total[:, i * PAIR : (i + 1) * PAIR], heads_total[:, :, i].reshape(owned, -1)],
                axis=1,
            )
        )
        for i in range(3)
    ]
    lines = gather(first_total[:, 3 * PAIR :]).T
    up_lines = lines[8:12].reshape(QUARTERS, BLOCKS, BLOCK).transpose(1, 0, 2).reshape(-1)
    place = lax.axis_index("fsdp")
    mine = lambda array: lax.dynamic_slice_in_dim(array, place * owned, owned)
    deep = up_bias.shape[0]
    return (
        output, token_grad, *heads,
        full(wide_total[:, HIDDEN_PAD : HIDDEN_PAD + WIDTH]),
        widen(wide_total[:, :HIDDEN_PAD], owned, super_hidden),
        widen(down_total, deep, super_width),
        mine(lines[0]), mine(lines[1]), mine(lines[2]),
        lax.dynamic_slice_in_dim(up_lines, place * deep, deep),
        mine(lines[3]), mine(lines[4]), mine(lines[5]), mine(lines[6]), mine(lines[7]),
    )


def solution(mesh):
    rows = P(("dp", "fsdp"), None)
    held = P("fsdp", None)
    line = P("fsdp")
    near = mesh.shape["dp"] == QUARTERS and mesh.shape["fsdp"] == BLOCKS
    return jax.shard_map(
        on_device if near else on_device_elsewhere,
        mesh=mesh,
        in_specs=(rows, P(("dp", "fsdp"))) + (held,) * 6 + (line,) * 9 + (rows,),
        out_specs=(rows, rows) + (held,) * 6 + (line,) * 9,
        check_vma=False,
    )
```

```python
import functools

import jax
import jax.numpy as jnp
from jax import lax
from jax.experimental import pallas as pl
from jax.experimental.pallas import tpu as pltpu
from jax.sharding import PartitionSpec as P

HEAD_DIM = 64
HIDDEN_SIZE = 2240
WIDTH = 640
EPSILON = 1e-05
MASKED = -1e30
PAIR = 2 * HEAD_DIM
PAIRS = WIDTH // PAIR
BF = jnp.bfloat16
F32 = jnp.float32
VMEM_BYTES = 60 * 2**20
BLOCKS = 8
BLOCK = 96
QUARTERS = 4
LAYERS = BLOCKS // 2
HIDDEN_PAD = 2304
UP_PART = 768
PEAK = 10**9


def dot(left, right, left_dim, right_dim):
    return lax.dot_general(
        left, right, (((left_dim,), (right_dim,)), ((), ())), preferred_element_type=F32
    )


def side(shape, axis, half, own, flag):
    place = lax.broadcasted_iota(jnp.int32, shape, axis)
    mine = (place < HEAD_DIM) if half == 0 else (place >= HEAD_DIM)
    first = place == (HEAD_DIM if half == 0 else 0)
    return jnp.where(mine, own, jnp.where(first, flag, 0.0))


def rows_of(step):
    return pl.ds(pl.multiple_of(step * BLOCK, BLOCK), BLOCK)


def cost(microseconds):
    return pl.CostEstimate(flops=microseconds * PEAK, bytes_accessed=0, transcendentals=0)


def params():
    return pltpu.CompilerParams(vmem_limit_bytes=VMEM_BYTES)


SMEM = pl.BlockSpec(memory_space=pltpu.SMEM)
WHOLE = pl.BlockSpec(memory_space=pltpu.VMEM)
IDLE = pl.BlockSpec(memory_space=pl.ANY)
LENGTH, CORE, PART, LAYER = range(4)


def call_with(kernel, inputs, after, **options):
    specs = options.pop("in_specs") + [IDLE] * len(after)

    def run(*refs):
        kernel(*refs[: len(inputs)], *refs[len(inputs) + len(after) :])

    return pl.pallas_call(run, in_specs=specs, compiler_params=params(), **options)(*inputs, *after)


def pack_first_kernel(info_ref, wq_ref, wk_ref, wv_ref, *refs):
    small_refs, out_ref = refs[:9], refs[9]
    lines = [ref[...].astype(F32).reshape(1, BLOCK) for ref in small_refs[:8]]
    up_line = small_refs[8][...].astype(F32).reshape(1, -1)
    lines += [up_line[:, i * BLOCK : (i + 1) * BLOCK] for i in range(QUARTERS)]
    small = jnp.concatenate(lines + [jnp.zeros((PAIR - 12, BLOCK), F32)], axis=0).T
    place = pl.ds(pl.multiple_of((info_ref[PART] + 1) * PAIR, PAIR), PAIR)
    for i, ref in enumerate((wq_ref, wk_ref, wv_ref)):
        out_ref[:, i * PAIR : (i + 1) * PAIR] = ref[:, :PAIR]
        out_ref[:, (i + 4) * PAIR : (i + 5) * PAIR] = ref[:, place]
    out_ref[:, 3 * PAIR : 4 * PAIR] = small.astype(BF)


def pack_wide_kernel(info_ref, up_ref, wo_ref, out_ref):
    part = info_ref[PART]

    @pl.when(part < QUARTERS - 1)
    def _():
        out_ref[...] = up_ref[:, pl.ds(pl.multiple_of(part * UP_PART, UP_PART), UP_PART)]

    @pl.when(part == QUARTERS - 1)
    def _():
        out_ref[...] = wo_ref[...]


def pack(kernel, info, arrays, shape, after=()):
    return call_with(
        kernel, (info, *arrays), after,
        in_specs=[SMEM] + [WHOLE] * len(arrays),
        out_specs=WHOLE,
        out_shape=jax.ShapeDtypeStruct(shape, BF),
        cost_estimate=cost(2),
    )


def repeat_kernel(*refs):
    for i, ref in enumerate(refs[:-1]):
        for copy in range(QUARTERS):
            refs[-1][copy, i] = ref[...]


def repeat(parts, after=()):
    return call_with(
        repeat_kernel, tuple(parts), after,
        in_specs=[WHOLE] * len(parts),
        out_specs=WHOLE,
        out_shape=jax.ShapeDtypeStruct((QUARTERS, len(parts)) + parts[0].shape, BF),
        cost_estimate=cost(30),
    )


def turn_kernel(source_ref, out_ref):
    out_ref[:WIDTH, :] = source_ref[...].T
    out_ref[WIDTH:, :] = jnp.zeros((BLOCKS * BLOCK - WIDTH, source_ref.shape[0]), BF)


def turn(tokens, after=()):
    return call_with(
        turn_kernel, (tokens,), after,
        in_specs=[WHOLE],
        out_specs=WHOLE,
        out_shape=jax.ShapeDtypeStruct((BLOCKS * BLOCK, tokens.shape[0]), BF),
        cost_estimate=cost(3),
    )


def cut(down, after=()):
    return call_with(
        cut_kernel, (down,), after,
        in_specs=[WHOLE],
        out_specs=WHOLE,
        out_shape=jax.ShapeDtypeStruct((down.shape[0], WIDTH), BF),
        cost_estimate=cost(1),
    )


def cut_kernel(down_ref, out_ref):
    out_ref[...] = down_ref[:, :WIDTH]


def lay_line(info_ref, target, own_ref, twin_ref, came_ref, twins_ref):
    core, layer = info_ref[CORE], info_ref[LAYER]
    width = target.shape[1]
    target[rows_of(2 * layer + core), :] = own_ref[:, :width]
    target[rows_of(2 * layer + 1 - core), :] = twin_ref[:, :width]
    for step in range(1, LAYERS):
        source = (layer + LAYERS - step) % LAYERS
        target[rows_of(2 * source + core), :] = came_ref[step - 1, :, :width]
        target[rows_of(2 * source + 1 - core), :] = twins_ref[step - 1, :, :width]


def lay(info_ref, target, width, mine_ref, other_ref):
    core, layer = info_ref[CORE], info_ref[LAYER]
    for quarter in range(QUARTERS):
        columns = slice(quarter * width, (quarter + 1) * width)
        for slot in range(LAYERS):
            source = (layer + LAYERS - slot) % LAYERS
            target[rows_of(2 * source + core), columns] = mine_ref[quarter, slot]
            target[rows_of(2 * source + 1 - core), columns] = other_ref[quarter, slot]


def attend_kernel(shift, info_ref, token_ref, *refs):
    first = shift is None
    count = 4 if first else 2
    sources, refs = refs[:count], refs[count:]
    if first:
        vectors_ref = refs[7]
        refs = refs[:7] + refs[8:]
    else:
        vectors_ref = refs[0]
        refs = refs[1:]
    (
        exp_ref, context_ref, wide_ref, inverse_ref, query_t_ref, key_ref,
        value_t_ref, weight_ref, held_ref, left_ref,
    ) = refs
    rows = token_ref.shape[0]
    if first:
        lay_line(info_ref, weight_ref, *sources)
        vectors_ref[...] = weight_ref[:, 3 * PAIR :].astype(F32).T[:16]
        bq = vectors_ref[0:1, :PAIR]
        bv = vectors_ref[1:2, :PAIR]
        weights = weight_ref[:WIDTH, : 3 * PAIR]
    else:
        @pl.when(pl.program_id(0) == 0)
        def _():
            lay(info_ref, weight_ref, 3 * PAIR, *sources)

        pair = pl.program_id(0) + shift
        place = pl.ds(pl.multiple_of(pair * PAIR, PAIR), PAIR)
        bq = vectors_ref[0:1, place]
        bv = vectors_ref[1:2, place]
        place = pl.ds(pl.multiple_of((pair - 1) * 3 * PAIR, 3 * PAIR), 3 * PAIR)
        weights = weight_ref[:WIDTH, place]
    product = dot(token_ref[...], weights, 1, 0)
    query = (product[:, :PAIR] + bq).astype(BF)
    key = product[:, PAIR : 2 * PAIR].astype(BF)
    value = (product[:, 2 * PAIR :] + bv).astype(BF)
    key_t = key.T
    query_t_ref[...] = query.T
    key_ref[...] = key
    value_t_ref[...] = value.T
    key_place = lax.broadcasted_iota(jnp.int32, (1, rows), 1)
    bias = jnp.where(key_place < info_ref[LENGTH], 0.0, MASKED)
    scaled = query.astype(F32) * HEAD_DIM**-0.5
    key_wide = key_t.astype(F32)
    value_wide = value.astype(F32)
    block = 128
    step = pl.program_id(0)

    def leave(half, start):
        lines = pl.ds(start, 2 * block)
        return pltpu.make_async_copy(
            held_ref.at[half, lines],
            exp_ref.at[2 * step + half, lines],
            left_ref.at[half, start // (2 * block)],
        )

    results = []
    for half in range(2):
        left = side((rows, PAIR), 1, half, scaled, 1.0).astype(BF)
        place = lax.broadcasted_iota(jnp.int32, (PAIR, rows), 0)
        right = jnp.where(place == (HEAD_DIM if half == 0 else 0), bias, key_wide).astype(BF)
        for start in range(0, rows, block):
            scores = dot(left[start : start + block], right, 1, 0)
            highest = jnp.max(scores, 1, keepdims=True)
            held_ref[half, start : start + block, :] = jnp.exp(scores - highest).astype(BF)
            if start % (2 * block):
                leave(half, start - block).start()
        values = side((rows, PAIR), 1, half, value_wide, 1.0).astype(BF)
        total = dot(held_ref[half], values, 1, 0)
        flag = HEAD_DIM if half == 0 else 0
        inverse = 1.0 / total[:, flag : flag + 1]
        results.append((total * inverse, inverse))
    low = lax.broadcasted_iota(jnp.int32, (rows, PAIR), 1) < HEAD_DIM
    context = jnp.where(low, results[0][0], results[1][0])
    wide_ref[...] = context
    context_ref[...] = context.astype(BF)
    inverse_ref[...] = jnp.where(low, results[0][1], results[1][1])
    for half in range(2):
        for start in range(0, rows, 2 * block):
            leave(half, start).wait()


def attend(info, tokens, sources, start, pairs, weight, vectors=None, after=()):
    rows = tokens.shape[0]
    first = vectors is None
    width = (4 if first else 12) * PAIR
    tall = lambda: pl.BlockSpec((rows, PAIR), lambda p: (0, p))
    flat = lambda: pl.BlockSpec((PAIR, rows), lambda p: (p, 0))
    array = lambda kind: jax.ShapeDtypeStruct((rows, pairs * PAIR), kind)
    turned = jax.ShapeDtypeStruct((pairs * PAIR, rows), BF)
    table = (16, BLOCKS * BLOCK)
    fixed = pl.BlockSpec(table, lambda p: (0, 0))
    return call_with(
        functools.partial(attend_kernel, None if first else start),
        (info, tokens, *sources, *(() if first else (vectors,))),
        after,
        grid=(pairs,),
        in_specs=[SMEM, WHOLE] + [WHOLE] * len(sources) + ([] if first else [fixed]),
        out_specs=[
            IDLE,
            tall(), tall(), tall(), flat(), tall(), flat(),
        ]
        + ([fixed] if first else []),
        out_shape=[
            jax.ShapeDtypeStruct((2 * pairs, rows, rows), BF),
            array(BF), array(F32), array(F32), turned, array(BF), turned,
        ]
        + ([jax.ShapeDtypeStruct(table, F32)] if first else []),
        scratch_shapes=[
            pltpu.VMEM((BLOCKS * BLOCK, width), BF),
            pltpu.VMEM((2, rows, rows), BF),
            pltpu.SemaphoreType.DMA((2, rows // 256)),
        ],
        cost_estimate=cost(weight),
    )


def gelu_pair(values):
    t = 1.0 / (1.0 + (0.3275911 * 0.5**0.5) * jnp.abs(values))
    bell = jnp.exp(-0.5 * values * values)
    tail = t * (0.5 * 0.254829592 + t * (0.5 * -0.284496736 + t * (0.5 * 1.421413741 + t * (
        0.5 * -1.453152027 + t * (0.5 * 1.061405429)))))
    tail = tail * bell
    share = jnp.where(values >= 0.0, 1.0 - tail, tail)
    return values * share, share + values * bell * 0.3989422804014327


def row_mean(values):
    return jnp.sum(values, 1, keepdims=True) * (1.0 / WIDTH)


def column_sum(values):
    return jnp.sum(values, 0, keepdims=True)


def row_mean(values):
    return jnp.sum(values, 1, keepdims=True) * (1.0 / WIDTH)


def column_sum(values):
    return jnp.sum(values, 0, keepdims=True)


def up_places():
    for block in range(HIDDEN_PAD // (QUARTERS * BLOCK)):
        for quarter in range(QUARTERS):
            start = (block * QUARTERS + quarter) * BLOCK
            row = slice(8 + quarter, 9 + quarter)
            yield slice(start, start + BLOCK), row, slice(block * BLOCK, (block + 1) * BLOCK)


def feed_kernel(
    info_ref, context_0_ref, context_1_ref, context_2_ref, token_ref, cotangent_ref,
    *refs
):
    sources, refs = refs[:2], refs[2:]
    (
        down_ref, vector_ref,
        output_ref, first_ref, grad_context_ref, sums_ref, b1_sum_ref, down_term_ref, keep_ref,
        send_ref, w1_ref, w2_ref, b1_ref, product_ref,
        context_ref, normed_ref, active_ref, hidden_ref, feed_ref, branch_ref,
    ) = refs
    step = pl.program_id(0)
    rows = token_ref.shape[0]

    @pl.when(step == 0)
    def _():
        lay(info_ref, w1_ref, UP_PART, *sources)
        last = slice(HIDDEN_PAD - PAIR, HIDDEN_PAD)
        lane = lax.broadcasted_iota(jnp.int32, (BLOCKS * BLOCK, PAIR), 1)
        kept = lane < HIDDEN_SIZE - (HIDDEN_PAD - PAIR)
        w1_ref[:, last] = jnp.where(kept, w1_ref[:, last].astype(F32), 0.0).astype(BF)
        w2_ref[:HIDDEN_SIZE, :] = down_ref[:HIDDEN_SIZE, :]
        for place, row, columns in up_places():
            b1_ref[:, place] = vector_ref[row, columns]
        lane = lax.broadcasted_iota(jnp.int32, (1, HIDDEN_PAD), 1)
        b1_ref[...] = jnp.where(lane < HIDDEN_SIZE, b1_ref[...], 0.0)
        w2_ref[HIDDEN_SIZE:, :] = jnp.zeros((HIDDEN_PAD - HIDDEN_SIZE, WIDTH), BF)

    steps = normed_ref.shape[0] // rows
    down_steps = HIDDEN_PAD // UP_PART

    @pl.when(step < steps)
    def _():
        here = pl.ds(pl.multiple_of(step * rows, rows), rows)
        wo = w1_ref[:WIDTH, HIDDEN_PAD : HIDDEN_PAD + WIDTH]
        w1, w2 = w1_ref[:WIDTH, :HIDDEN_PAD], w2_ref[...]
        place = lax.broadcasted_iota(jnp.int32, (rows, 1), 0) + step * rows
        live = jnp.where(place < info_ref[LENGTH], 1.0, 0.0)
        vector = lambda i: vector_ref[i : i + 1, :WIDTH]
        out_add, down_add = vector(2), vector(3)
        gain_one, shift_one, gain_two, shift_two = vector(4), vector(5), vector(6), vector(7)
        context = jnp.concatenate([context_0_ref[...], context_1_ref[...], context_2_ref[...]], axis=1)
        context_ref[here, :] = context
        first_sum = token_ref[...].astype(F32) + dot(context, wo, 1, 0) + out_add
        center = first_sum - row_mean(first_sum)
        rate_one = lax.rsqrt(row_mean(center * center) + EPSILON)
        unit_one = center * rate_one
        normed = (unit_one * gain_one + shift_one).astype(BF)
        normed_ref[here, :] = normed
        pre = dot(normed, w1, 1, 0) + b1_ref[...]
        active_full, slope = gelu_pair(pre)
        active = active_full.astype(BF)
        active_ref[here, :] = active
        second_sum = normed.astype(F32) + dot(active, w2, 1, 0) + down_add
        center = second_sum - row_mean(second_sum)
        rate_two = lax.rsqrt(row_mean(center * center) + EPSILON)
        unit_two = center * rate_two
        output_ref[...] = ((unit_two * gain_two + shift_two) * live).astype(BF)
        cotangent = cotangent_ref[...].astype(F32) * live
        inner = cotangent * gain_two
        grad_second = rate_two * (inner - row_mean(inner) - unit_two * row_mean(inner * unit_two))
        grad_feed = grad_second.astype(BF)
        feed_ref[here, :] = grad_feed
        grad_hidden = (dot(grad_feed, w2, 1, 1) * slope).astype(BF)
        hidden_ref[here, :] = grad_hidden
        grad_normed = grad_second + dot(grad_hidden, w1, 1, 1)
        inner = grad_normed * gain_one
        grad_first = rate_one * (inner - row_mean(inner) - unit_one * row_mean(inner * unit_one))
        first_ref[...] = grad_first
        grad_branch = grad_first.astype(BF)
        branch_ref[here, :] = grad_branch
        grad_context_ref[...] = dot(grad_branch, wo, 1, 1).astype(BF)
        sums = jnp.concatenate(
            [
                column_sum(grad_branch.astype(F32)),
                column_sum(grad_feed.astype(F32)),
                column_sum(grad_normed * unit_one),
                column_sum(grad_normed),
                column_sum(cotangent * unit_two),
                column_sum(cotangent),
                jnp.zeros((2, WIDTH), F32),
            ],
            axis=0,
        )
        b1_sum = column_sum(grad_hidden.astype(F32))

        @pl.when(step == 0)
        def _():
            sums_ref[...] = sums
            b1_sum_ref[...] = b1_sum

        @pl.when(step > 0)
        def _():
            sums_ref[...] += sums
            b1_sum_ref[...] += b1_sum

    @pl.when((step >= steps) & (step < steps + down_steps))
    def _():
        place = pl.ds(pl.multiple_of((step - steps) * UP_PART, UP_PART), UP_PART)
        down_term_ref[...] = dot(active_ref[:, place], feed_ref[...], 0, 0).astype(BF)

    @pl.when(step >= steps + down_steps)
    def _():
        part = step - steps - down_steps

        @pl.when(part == 0)
        def _():
            product_ref[WIDTH:, :] = jnp.zeros((BLOCKS * BLOCK - WIDTH, UP_PART), F32)

        @pl.when(part < QUARTERS - 1)
        def _():
            place = pl.ds(pl.multiple_of(part * UP_PART, UP_PART), UP_PART)
            product_ref[:WIDTH, :] = dot(normed_ref[...], hidden_ref[:, place], 0, 0)

        @pl.when(part == QUARTERS - 1)
        def _():
            product_ref[:WIDTH, :WIDTH] = dot(context_ref[...], branch_ref[...], 0, 0)

        deal(info_ref, product_ref, keep_ref, send_ref)


def feed(info, contexts, tokens, cotangent, wide, down, vectors):
    rows = tokens.shape[0]
    tile = 256
    steps = rows // tile
    down_steps = HIDDEN_PAD // UP_PART
    part = lambda width: pl.BlockSpec((tile, width), lambda i: (jnp.minimum(i, steps - 1), 0))
    whole = lambda *shape: pl.BlockSpec(shape, lambda i: (0, 0))
    array = lambda width, kind: jax.ShapeDtypeStruct((rows, width), kind)
    held = lambda width: pltpu.VMEM((rows, width), BF)
    place = lambda: pl.BlockSpec(
        (1, LAYERS, BLOCK, UP_PART),
        lambda i: (jnp.clip(i - steps - down_steps, 0, QUARTERS - 1), 0, 0, 0),
    )
    shared = jax.ShapeDtypeStruct((QUARTERS, LAYERS, BLOCK, UP_PART), BF)
    return pl.pallas_call(
        feed_kernel,
        grid=(steps + down_steps + QUARTERS,),
        in_specs=[SMEM]
        + [part(context.shape[1]) for context in contexts]
        + [part(WIDTH), part(WIDTH)]
        + [WHOLE] * len(wide)
        + [WHOLE]
        + [whole(*vectors.shape)],
        out_specs=[
            part(WIDTH), part(WIDTH), part(WIDTH), whole(8, WIDTH), whole(1, HIDDEN_PAD),
            pl.BlockSpec((UP_PART, WIDTH), lambda i: (jnp.clip(i - steps, 0, down_steps - 1), 0)),
            place(), place(),
        ],
        out_shape=[
            array(WIDTH, BF), array(WIDTH, F32), array(WIDTH, BF),
            jax.ShapeDtypeStruct((8, WIDTH), F32),
            jax.ShapeDtypeStruct((1, HIDDEN_PAD), F32),
            jax.ShapeDtypeStruct((down.shape[0], WIDTH), BF),
            shared, shared,
        ],
        scratch_shapes=[
            pltpu.VMEM((BLOCKS * BLOCK, QUARTERS * UP_PART), BF),
            pltpu.VMEM((HIDDEN_PAD, WIDTH), BF),
            pltpu.VMEM((1, HIDDEN_PAD), F32),
            pltpu.VMEM((BLOCKS * BLOCK, UP_PART), F32),
            held(WIDTH), held(WIDTH), held(HIDDEN_PAD), held(HIDDEN_PAD), held(WIDTH), held(WIDTH),
        ],
        compiler_params=params(),
        cost_estimate=cost(50),
    )(info, *contexts, tokens, cotangent, *wide, down, vectors)


def deal(info_ref, product_ref, keep_ref, send_ref):
    core = info_ref[CORE]
    for layer in range(LAYERS):
        keep_ref[0, layer] = product_ref[rows_of(2 * layer + core), :].astype(BF)
        send_ref[0, layer] = product_ref[rows_of(2 * layer + 1 - core), :].astype(BF)


def head_grad_kernel(info_ref, token_t_ref, low_ref, high_ref, keep_ref, send_ref, product_ref):
    step = pl.program_id(0)
    half = low_ref.shape[0]

    @pl.when(step < half)
    def _():
        product_ref[...] = dot(token_t_ref[...], low_ref[jnp.minimum(step, half - 1)], 1, 0)

    @pl.when(step >= half)
    def _():
        product_ref[...] = dot(token_t_ref[...], high_ref[jnp.maximum(step - half, 0)], 1, 0)

    deal(info_ref, product_ref, keep_ref, send_ref)


def head_grad(info, token_t, low, high, after=()):
    place = lambda: pl.BlockSpec((1, LAYERS, BLOCK, 3 * PAIR), lambda d: (d, 0, 0, 0))
    array = jax.ShapeDtypeStruct((QUARTERS, LAYERS, BLOCK, 3 * PAIR), BF)
    return call_with(
        head_grad_kernel, (info, token_t, low, high), after,
        grid=(QUARTERS,),
        in_specs=[SMEM] + [WHOLE] * 3,
        out_specs=[place(), place()],
        out_shape=[array, array],
        scratch_shapes=[pltpu.VMEM((BLOCKS * BLOCK, 3 * PAIR), F32)],
        cost_estimate=cost(6),
    )


def first_grad_kernel(
    info_ref, token_t_ref, together_ref, sums_ref, up_sum_ref, pair_0_ref, pair_1_ref, pair_2_ref,
    keep_ref, send_ref, product_ref, table_ref,
):
    product_ref[:, : 3 * PAIR] = dot(token_t_ref[...], together_ref[0], 1, 0)
    table_ref[...] = jnp.zeros_like(table_ref)
    start = 0
    for ref in (pair_0_ref, pair_1_ref, pair_2_ref):
        table_ref[0:2, start : start + ref.shape[1]] = ref[0:2, :]
        start += ref.shape[1]
    table_ref[2:8, :WIDTH] = sums_ref[0:6, :]
    for place, row, columns in up_places():
        table_ref[row, columns] = up_sum_ref[:, place]
    product_ref[:, 3 * PAIR :] = table_ref[...].T
    core = info_ref[CORE]
    for layer in range(LAYERS):
        kept = product_ref[rows_of(2 * layer + core), :].astype(BF)
        sent = product_ref[rows_of(2 * layer + 1 - core), :].astype(BF)
        for part in range(QUARTERS):
            columns = slice(part * PAIR, (part + 1) * PAIR)
            keep_ref[part, layer] = kept[:, columns]
            send_ref[part, layer] = sent[:, columns]


def first_grad(info, token_t, together, sums, up_sum, pair_sums, after=()):
    array = jax.ShapeDtypeStruct((QUARTERS, LAYERS, BLOCK, PAIR), BF)
    return call_with(
        first_grad_kernel, (info, token_t, together, sums, up_sum, *pair_sums), after,
        in_specs=[SMEM] + [WHOLE] * 7,
        out_specs=[WHOLE] * 2,
        out_shape=[array, array],
        scratch_shapes=[
            pltpu.VMEM((BLOCKS * BLOCK, 4 * PAIR), F32),
            pltpu.VMEM((PAIR, BLOCKS * BLOCK), F32),
        ],
        cost_estimate=cost(3),
    )


def meet_kernel(info_ref, keep_ref, came_ref, *out_refs):
    for apart in range(QUARTERS):
        quarter = info_ref[PART] ^ apart
        out_refs[apart][0] = keep_ref[quarter, 0] + came_ref[quarter, 0]


def meet(info, keep, came, after=()):
    width = keep.shape[-1]
    block = lambda: pl.BlockSpec(
        (QUARTERS, 1, BLOCK, width), lambda s, info: (0, (info[LAYER] + s) % LAYERS, 0, 0)
    )

    def run(info_ref, keep_ref, came_ref, *refs):
        meet_kernel(info_ref, keep_ref, came_ref, *refs[len(after) :])

    return pl.pallas_call(
        run,
        grid_spec=pltpu.PrefetchScalarGridSpec(
            num_scalar_prefetch=1,
            grid=(LAYERS,),
            in_specs=[block(), block()] + [IDLE] * len(after),
            out_specs=[pl.BlockSpec((1, BLOCK, width), lambda s, info: (s, 0, 0))] * QUARTERS,
        ),
        out_shape=[jax.ShapeDtypeStruct((LAYERS, BLOCK, width), BF)] * QUARTERS,
        compiler_params=params(),
        cost_estimate=cost(3),
    )(info, keep, came, *after)


def attend_back_kernel(
    grad_ref, wide_ref, inverse_ref, exp_ref, query_t_ref, key_ref, value_t_ref,
    together_ref, sums_ref, score_ref,
):
    rows = grad_ref.shape[0]
    inverse = inverse_ref[...]
    grad = grad_ref[...].astype(F32)
    scaled = grad * inverse
    dots = scaled * wide_ref[...]
    scaled_t = scaled.T.astype(BF)
    value_wide = value_t_ref[...].astype(F32)
    lane = lax.broadcasted_iota(jnp.int32, (rows, PAIR), 1)
    place = lax.broadcasted_iota(jnp.int32, (PAIR, rows), 0)
    block = 128
    dq, dk_t, dv_t = [], [], []
    for half in range(2):
        mine = (lane < HEAD_DIM) if half == 0 else (lane >= HEAD_DIM)
        flag = HEAD_DIM if half == 0 else 0
        offset = jnp.sum(jnp.where(mine, -dots, 0.0), 1, keepdims=True)
        high = offset.astype(BF).astype(F32)
        rest = offset - high
        left = jnp.where(
            mine, scaled, jnp.where(lane == flag, high, jnp.where(lane == flag + 1, rest, 0.0))
        ).astype(BF)
        right = jnp.where((place == flag) | (place == flag + 1), 1.0, value_wide).astype(BF)
        for start in range(0, rows, block):
            grad_probs = dot(left[start : start + block], right, 1, 0)
            weight = exp_ref[half, start : start + block, :].astype(F32)
            score_ref[half, start : start + block, :] = (grad_probs * weight).astype(BF)
        own = slice(half * HEAD_DIM, (half + 1) * HEAD_DIM)
        dv_t.append(dot(scaled_t[own], exp_ref[half], 1, 0))
        dk_t.append(dot(query_t_ref[own, :], score_ref[half], 1, 0))
        dq.append(dot(score_ref[half], key_ref[...], 1, 0))
    factor = HEAD_DIM**-0.5
    dq_low = (jnp.where(lane < HEAD_DIM, dq[0], dq[1]) * factor).astype(BF)
    dk_low = (jnp.concatenate(dk_t, axis=0) * factor).T.astype(BF)
    dv_low = jnp.concatenate(dv_t, axis=0).T.astype(BF)
    together_ref[0] = jnp.concatenate([dq_low, dk_low, dv_low], axis=1)
    query_sum = column_sum(dq_low.astype(F32))
    value_sum = column_sum(dv_low.astype(F32))
    sums_ref[...] = jnp.concatenate([query_sum, value_sum, jnp.zeros((6, PAIR), F32)], axis=0)


def attend_back(grad_context, saved, start, pairs, weight, after=()):
    exps, wide, inverse, query_t, key, value_t = saved
    rows = grad_context.shape[0]
    tall = lambda first: pl.BlockSpec((rows, PAIR), lambda p: (0, first + p))
    flat = lambda: pl.BlockSpec((PAIR, rows), lambda p: (p, 0))
    return call_with(
        attend_back_kernel,
        (grad_context, wide, inverse, exps, query_t, key, value_t),
        after,
        grid=(pairs,),
        in_specs=[
            tall(start), tall(0), tall(0),
            pl.BlockSpec((2, rows, rows), lambda p: (p, 0, 0)),
            flat(), tall(0), flat(),
        ],
        out_specs=[
            pl.BlockSpec((1, rows, 3 * PAIR), lambda p: (p, 0, 0)),
            pl.BlockSpec((8, PAIR), lambda p: (0, p)),
        ],
        out_shape=[
            jax.ShapeDtypeStruct((pairs, rows, 3 * PAIR), BF),
            jax.ShapeDtypeStruct((8, pairs * PAIR), F32),
        ],
        scratch_shapes=[pltpu.VMEM((2, rows, rows), BF)],
        cost_estimate=cost(weight),
    )


def token_kernel(info_ref, grad_ref, together_0_ref, together_1_ref, together_2_ref, *refs):
    count = 4
    first_sources, rest_sources = refs[:count], refs[count : count + 2]
    out_ref, first_ref, rest_ref = refs[-3:]

    @pl.when(pl.program_id(0) == 0)
    def _():
        lay_line(info_ref, first_ref, *first_sources)
        lay(info_ref, rest_ref, 3 * PAIR, *rest_sources)

    pieces = [ref[i] for ref in (together_1_ref, together_2_ref) for i in range(ref.shape[0])]
    total = grad_ref[...] + dot(together_0_ref[0], first_ref[:WIDTH, : 3 * PAIR], 1, 1)
    total += dot(jnp.concatenate(pieces, axis=1), rest_ref[:WIDTH, :], 1, 1)
    out_ref[...] = total.astype(BF)


def token_back(info, grad_first, togethers, first, rest, after):
    rows = grad_first.shape[0]
    tile = 256
    part = pl.BlockSpec((tile, WIDTH), lambda i: (i, 0))
    piece = lambda array: pl.BlockSpec((array.shape[0], tile, 3 * PAIR), lambda i: (0, i, 0))
    return call_with(
        token_kernel, (info, grad_first, *togethers, *first, *rest), after,
        grid=(rows // tile,),
        in_specs=[SMEM, part]
        + [piece(array) for array in togethers]
        + [WHOLE] * (len(first) + len(rest)),
        out_specs=part,
        out_shape=jax.ShapeDtypeStruct((rows, WIDTH), BF),
        scratch_shapes=[
            pltpu.VMEM((BLOCKS * BLOCK, 4 * PAIR), BF),
            pltpu.VMEM((BLOCKS * BLOCK, 12 * PAIR), BF),
        ],
        cost_estimate=cost(7),
    )


def plane_kernel(groups, *refs):
    inputs, outputs = refs[: groups * QUARTERS], refs[groups * QUARTERS :]
    start = 0
    for group in range(groups):
        mine = inputs[group * QUARTERS : (group + 1) * QUARTERS]
        width = mine[0].shape[-1]
        for step in range(LAYERS):
            total = sum(ref[step].astype(F32) for ref in mine)
            outputs[step][:, start : start + width] = total.astype(BF)
        start += width


def plane(groups, after=()):
    width = sum(group[0].shape[-1] for group in groups)
    return call_with(
        functools.partial(plane_kernel, len(groups)),
        tuple(array for group in groups for array in group),
        after,
        in_specs=[WHOLE] * (len(groups) * QUARTERS),
        out_specs=[WHOLE] * LAYERS,
        out_shape=[jax.ShapeDtypeStruct((BLOCK, width), BF)] * LAYERS,
        cost_estimate=cost(2),
    )


def line_kernel(counts, *refs):
    inputs, out_ref = refs[:-1], refs[-1]
    start = 0
    for count in counts:
        mine, inputs = inputs[:count], inputs[count:]
        width = mine[0].shape[-1]
        parts = [ref[...] for ref in mine] if count > 1 else [mine[0][i] for i in range(QUARTERS)]
        total = sum(part.astype(F32) for part in parts).astype(BF)
        for copy in range(QUARTERS):
            out_ref[copy, :, start : start + width] = total
        start += width


def line(groups, after=()):
    width = sum(group[0].shape[-1] for group in groups)
    arrays = tuple(array for group in groups for array in group)
    return call_with(
        functools.partial(line_kernel, [len(group) for group in groups]), arrays, after,
        in_specs=[WHOLE] * len(arrays),
        out_specs=WHOLE,
        out_shape=jax.ShapeDtypeStruct((QUARTERS, BLOCK, width), BF),
        cost_estimate=cost(1),
    )


def finish_kernel(info_ref, wide_ref, heads_ref, *refs):
    wq_ref, wk_ref, wv_ref, wo_ref, up_ref, down_ref = refs[:6]
    line_refs, up_line_ref = refs[6:14], refs[14]
    extra = wq_ref.shape[1] - WIDTH
    blank = jnp.zeros((BLOCK, extra), F32)
    used = HIDDEN_PAD // (QUARTERS * BLOCK)
    owner = 2 * info_ref[LAYER] + info_ref[CORE]
    for quarter in range(QUARTERS):
        lines = slice(quarter * BLOCK, (quarter + 1) * BLOCK)
        down = wide_ref[quarter, :, UP_PART:].astype(F32)
        down_ref[lines, :WIDTH] = jnp.where(owner < used, down, 0.0)
        down_ref[lines, WIDTH:] = blank
    for quarter in range(QUARTERS - 1):
        columns = slice(quarter * UP_PART, (quarter + 1) * UP_PART)
        up_ref[:, columns] = wide_ref[quarter, :, :UP_PART].astype(F32)
    up_ref[:, HIDDEN_PAD:] = jnp.zeros((BLOCK, up_ref.shape[1] - HIDDEN_PAD), F32)
    wo_ref[:, :WIDTH] = wide_ref[QUARTERS - 1, :, :WIDTH].astype(F32)
    wo_ref[:, WIDTH:] = blank
    for i, ref in enumerate((wq_ref, wk_ref, wv_ref)):
        ref[:, :PAIR] = heads_ref[i, :, 3 * PAIR :].astype(F32)
        for pair in range(1, PAIRS):
            part = heads_ref[pair - 1, :, i * PAIR : (i + 1) * PAIR]
            ref[:, pair * PAIR : (pair + 1) * PAIR] = part.astype(F32)
        ref[:, WIDTH:] = blank
    lines = heads_ref[QUARTERS - 1, :, 3 * PAIR :].astype(F32).T
    for i, ref in enumerate(line_refs):
        ref[...] = lines[i]
    up_line_ref[...] = lines[8 : 8 + QUARTERS]


def finish(info, wide, heads, super_width, super_hidden):
    array = lambda *shape: jax.ShapeDtypeStruct(shape, F32)
    square = array(BLOCK, super_width)
    return pl.pallas_call(
        finish_kernel,
        in_specs=[SMEM] + [WHOLE] * 2,
        out_specs=[WHOLE] * 15,
        out_shape=[
            square, square, square, square, array(BLOCK, super_hidden),
            array(QUARTERS * BLOCK, super_width),
        ]
        + [array(BLOCK)] * 8
        + [array(QUARTERS, BLOCK)],
        compiler_params=params(),
        cost_estimate=cost(4),
    )(info, wide, heads)


SWAP = [(i, i ^ 1) for i in range(BLOCKS)]
STEPS = range(1, LAYERS)
DISTANCES = range(1, QUARTERS)


def twin(part):
    return lax.ppermute(part, "fsdp", SWAP)


def along(part, step):
    pairs = [(i, (i + 2 * step) % BLOCKS) for i in range(BLOCKS)]
    return lax.ppermute(part, "fsdp", pairs)


LINES = [[2 * layer + core for layer in range(LAYERS)] for core in range(2)]


def trade_plane(parts):
    return lax.all_to_all(parts, "dp", 0, 0)


def trade_line(parts):
    return lax.all_to_all(parts, "fsdp", 0, 0, axis_index_groups=LINES)


def copies(part):
    return jnp.broadcast_to(part[None], (QUARTERS,) + part.shape)


def across(part, apart):
    return lax.ppermute(part, "dp", [(i, i ^ apart) for i in range(QUARTERS)])


def drop(saved):
    return (saved[0],) + tuple(saved[2:])


def on_device(
    tokens, lengths, query_weight, key_weight, value_weight, out_weight, up_weight, down_weight,
    query_bias, value_bias, out_bias, up_bias, down_bias, first_gain, first_shift, second_gain,
    second_shift, cotangent,
):
    super_width, super_hidden = query_weight.shape[1], up_weight.shape[1]
    index = lax.axis_index("fsdp").astype(jnp.int32)
    part = lax.axis_index("dp").astype(jnp.int32)
    info = jnp.stack([lengths[0], index % 2, part, index // 2])
    qkv = (query_weight, key_weight, value_weight)
    small = (
        query_bias, value_bias, out_bias, down_bias,
        first_gain, first_shift, second_gain, second_shift, up_bias,
    )
    first_own = pack(pack_first_kernel, info, qkv + small, (BLOCK, 7 * PAIR))
    first_came = [along(first_own, step) for step in STEPS]
    token_t = turn(tokens, after=(first_own,))
    wide_own = pack(
        pack_wide_kernel, info, (up_weight, out_weight), (BLOCK, UP_PART), after=(token_t,)
    )
    first_line = jnp.stack(first_came)
    first = (first_own, twin(first_own), first_line, twin(first_line))
    rest_line = jnp.concatenate([first_own[None], first_line])[:, :, 4 * PAIR :]
    rest_mine = trade_plane(copies(rest_line))
    down_cut = cut(down_weight, after=(wide_own, *first))
    wide_line = [wide_own] + [along(wide_own, step) for step in STEPS]
    down = lax.all_gather(down_cut, "fsdp", axis=0, tiled=True)
    *saved_0, vectors = attend(info, tokens, first, 0, 1, 8, after=(down_cut,))
    rest = (rest_mine, twin(rest_mine))
    wide_mine = trade_plane(repeat(wide_line, after=(saved_0[1],)))
    saved_1 = attend(info, tokens, rest, 1, 3, 50, vectors, after=wide_line)
    wide = (wide_mine, twin(wide_mine))
    saved_2 = attend(info, tokens, rest, 4, 1, 50, vectors, after=(saved_1[1], wide_mine))
    all_saved = (saved_0, saved_1, saved_2)
    contexts = [saved[1] for saved in all_saved]
    (
        output, grad_first, grad_context, sums, up_sum, down_term, up_keep, up_send
    ) = feed(info, contexts, tokens, cotangent, wide, down, vectors)
    down_total = lax.psum_scatter(down_term, "fsdp", scatter_dimension=0, tiled=True)
    up_near = meet(info, up_keep, twin(up_send))
    send = lambda near: [near[0]] + [across(near[apart], apart) for apart in DISTANCES]
    pass_on = lambda layers: [layers[0]] + [along(layers[step], step) for step in STEPS]
    up_plane = send(up_near)
    together_1, sums_1 = attend_back(grad_context, drop(saved_1), 1, 3, 1, after=(up_near[0],))
    up_layers = plane([up_plane], after=(together_1,))
    up_line = pass_on(up_layers)
    together_2, sums_2 = attend_back(grad_context, drop(saved_2), 4, 1, 50, after=(up_layers[0],))
    head_keep, head_send = head_grad(info, token_t, together_1, together_2, after=up_line[1:])
    down_plane = trade_plane(down_total.reshape(QUARTERS, BLOCK, WIDTH))
    head_near = meet(info, head_keep, twin(head_send), after=(down_total,))
    head_plane = send(head_near)
    together_0, sums_0 = attend_back(
        grad_context, drop(saved_0), 0, 1, 8, after=(head_near[0],)
    )
    first_keep, first_send = first_grad(
        info, token_t, together_0, sums, up_sum, (sums_0, sums_1, sums_2),
        after=(down_plane, *head_plane[1:]),
    )
    wide_copies = line([up_line, [down_plane]], after=(first_keep,))
    wide_total = trade_plane(wide_copies)
    first_near = meet(info, first_keep, twin(first_send), after=(wide_copies,))
    first_plane = send(first_near)
    layers = plane([head_plane, first_plane])
    token_grad = token_back(
        info, grad_first, (together_0, together_1, together_2), first, rest, (layers[0],)
    )
    head_total = trade_plane(line([pass_on(layers)], after=(token_grad, wide_total)))
    *results, up_lines = finish(info, wide_total, head_total, super_width, super_hidden)
    matrices, lines = results[:6], results[6:]
    order = lines[:3] + [up_lines.reshape(-1)] + lines[3:]
    return (output, token_grad, *matrices, *order)


def widen(matrix, row_count, column_count):
    return jnp.pad(matrix, ((0, row_count - matrix.shape[0]), (0, column_count - matrix.shape[1])))


def on_device_elsewhere(
    tokens, lengths, query_weight, key_weight, value_weight, out_weight, up_weight, down_weight,
    query_bias, value_bias, out_bias, up_bias, down_bias, first_gain, first_shift, second_gain,
    second_shift, cotangent,
):
    owned, super_width = query_weight.shape
    super_hidden = up_weight.shape[1]
    info = jnp.stack([lengths[0]] + [jnp.zeros((), jnp.int32)] * 3)
    gather = lambda array: lax.all_gather(array, "fsdp", axis=0, tiled=True)
    qkv = [gather(array) for array in (query_weight, key_weight, value_weight)]
    lines = [
        gather(array)
        for array in (
            query_bias, value_bias, out_bias, down_bias,
            first_gain, first_shift, second_gain, second_shift,
        )
    ]
    up_lines = gather(up_bias).reshape(BLOCKS, QUARTERS, BLOCK).transpose(1, 0, 2)
    lines = jnp.concatenate([jnp.stack(lines), up_lines.reshape(QUARTERS, -1)], axis=0)
    columns = jnp.pad(lines, ((0, PAIR - lines.shape[0]), (0, 0))).T
    first_full = jnp.concatenate([array[:, :PAIR] for array in qkv] + [columns], axis=1)
    places = [slice(pair * PAIR, (pair + 1) * PAIR) for pair in range(1, PAIRS)]
    rest_full = jnp.concatenate([array[:, place] for place in places for array in qkv], axis=1)
    wide_full = jnp.concatenate([gather(up_weight)[:, :HIDDEN_PAD], gather(out_weight)], axis=1)
    down = gather(down_weight)[:, :WIDTH]

    back = [(LAYERS - slot) % LAYERS for slot in range(LAYERS)]

    def pieces(full):
        blocks = full.reshape(LAYERS, 2, BLOCK, QUARTERS, -1).transpose(0, 1, 3, 2, 4)
        blocks = jnp.stack([blocks[layer] for layer in back], axis=2)
        return blocks[0], blocks[1]

    blocks = first_full.reshape(LAYERS, 2, BLOCK, -1)
    blocks = jnp.stack([blocks[layer] for layer in back])
    first = (blocks[0, 0], blocks[0, 1], blocks[1:, 0], blocks[1:, 1])
    rest, wide = pieces(rest_full), pieces(wide_full)
    token_t = turn(tokens)
    *saved_0, vectors = attend(info, tokens, first, 0, 1, 8)
    saved_1 = attend(info, tokens, rest, 1, 3, 50, vectors)
    saved_2 = attend(info, tokens, rest, 4, 1, 50, vectors)
    all_saved = (saved_0, saved_1, saved_2)
    contexts = [saved[1] for saved in all_saved]
    (
        output, grad_first, grad_context, sums, up_sum, down_term, *up_parts
    ) = feed(info, contexts, tokens, cotangent, wide, down, vectors)
    deep = lax.broadcasted_iota(jnp.int32, (super_hidden, 1), 0)
    down_term = jnp.where(deep < HIDDEN_PAD, down_term, 0.0)
    together_1, sums_1 = attend_back(grad_context, drop(saved_1), 1, 3, 1)
    together_2, sums_2 = attend_back(grad_context, drop(saved_2), 4, 1, 1)
    together_0, sums_0 = attend_back(grad_context, drop(saved_0), 0, 1, 1)
    heads = (info, token_t, together_1, together_2)
    firsts = (info, token_t, together_0, sums, up_sum, (sums_0, sums_1, sums_2))

    def both(parts):
        return jnp.stack(parts, axis=2).transpose(1, 2, 3, 0, 4).reshape(super_width, -1)

    def total(array):
        array = lax.psum_scatter(array, "fsdp", scatter_dimension=0, tiled=True)
        return lax.psum(array, "dp").astype(F32)

    wide_total = total(both(up_parts))
    heads_total = total(both(head_grad(*heads))).reshape(owned, PAIRS - 1, 3, PAIR)
    first_total = total(both(first_grad(*firsts)))
    down_total = total(down_term)
    token_grad = token_back(
        info, grad_first, (together_0, together_1, together_2), first, rest, ()
    )
    full = lambda matrix: widen(matrix, owned, super_width)
    heads = [
        full(
            jnp.concatenate(
                [first_total[:, i * PAIR : (i + 1) * PAIR], heads_total[:, :, i].reshape(owned, -1)],
                axis=1,
            )
        )
        for i in range(3)
    ]
    lines = gather(first_total[:, 3 * PAIR :]).T
    up_lines = lines[8:12].reshape(QUARTERS, BLOCKS, BLOCK).transpose(1, 0, 2).reshape(-1)
    place = lax.axis_index("fsdp")
    mine = lambda array: lax.dynamic_slice_in_dim(array, place * owned, owned)
    deep = up_bias.shape[0]
    return (
        output, token_grad, *heads,
        full(wide_total[:, HIDDEN_PAD : HIDDEN_PAD + WIDTH]),
        widen(wide_total[:, :HIDDEN_PAD], owned, super_hidden),
        widen(down_total, deep, super_width),
        mine(lines[0]), mine(lines[1]), mine(lines[2]),
        lax.dynamic_slice_in_dim(up_lines, place * deep, deep),
        mine(lines[3]), mine(lines[4]), mine(lines[5]), mine(lines[6]), mine(lines[7]),
    )


def solution(mesh):
    rows = P(("dp", "fsdp"), None)
    held = P("fsdp", None)
    line = P("fsdp")
    near = mesh.shape["dp"] == QUARTERS and mesh.shape["fsdp"] == BLOCKS
    return jax.shard_map(
        on_device if near else on_device_elsewhere,
        mesh=mesh,
        in_specs=(rows, P(("dp", "fsdp"))) + (held,) * 6 + (line,) * 9 + (rows,),
        out_specs=(rows, rows) + (held,) * 6 + (line,) * 9,
        check_vma=False,
    )
```

```python
import functools

import jax
import jax.numpy as jnp
from jax import lax
from jax.experimental import pallas as pl
from jax.experimental.pallas import tpu as pltpu
from jax.sharding import PartitionSpec as P

HEAD_DIM = 64
HIDDEN_SIZE = 2240
WIDTH = 640
EPSILON = 1e-05
MASKED = -1e30
PAIR = 2 * HEAD_DIM
PAIRS = WIDTH // PAIR
BF = jnp.bfloat16
F32 = jnp.float32
VMEM_BYTES = 127 * 2**19
BLOCKS = 8
BLOCK = 96
QUARTERS = 4
LAYERS = BLOCKS // 2
HIDDEN_PAD = 2304
UP_PART = 768
PEAK = 10**9


def dot(left, right, left_dim, right_dim):
    return lax.dot_general(
        left, right, (((left_dim,), (right_dim,)), ((), ())), preferred_element_type=F32
    )


def side(shape, axis, half, own, flag):
    place = lax.broadcasted_iota(jnp.int32, shape, axis)
    mine = (place < HEAD_DIM) if half == 0 else (place >= HEAD_DIM)
    first = place == (HEAD_DIM if half == 0 else 0)
    return jnp.where(mine, own, jnp.where(first, flag, 0.0))


def rows_of(step):
    return pl.ds(pl.multiple_of(step * BLOCK, BLOCK), BLOCK)


def cost(microseconds):
    return pl.CostEstimate(flops=microseconds * PEAK, bytes_accessed=0, transcendentals=0)


def params():
    return pltpu.CompilerParams(vmem_limit_bytes=VMEM_BYTES)


SMEM = pl.BlockSpec(memory_space=pltpu.SMEM)
WHOLE = pl.BlockSpec(memory_space=pltpu.VMEM)
IDLE = pl.BlockSpec(memory_space=pl.ANY)
LENGTH, CORE, PART, LAYER = range(4)


def call_with(kernel, inputs, after, **options):
    specs = options.pop("in_specs") + [IDLE] * len(after)

    def run(*refs):
        kernel(*refs[: len(inputs)], *refs[len(inputs) + len(after) :])

    return pl.pallas_call(run, in_specs=specs, compiler_params=params(), **options)(*inputs, *after)


def pack_first_kernel(info_ref, wq_ref, wk_ref, wv_ref, *refs):
    small_refs, out_ref = refs[:9], refs[9]
    lines = [ref[...].astype(F32).reshape(1, BLOCK) for ref in small_refs[:8]]
    up_line = small_refs[8][...].astype(F32).reshape(1, -1)
    lines += [up_line[:, i * BLOCK : (i + 1) * BLOCK] for i in range(QUARTERS)]
    small = jnp.concatenate(lines + [jnp.zeros((PAIR - 12, BLOCK), F32)], axis=0).T
    place = pl.ds(pl.multiple_of((info_ref[PART] + 1) * PAIR, PAIR), PAIR)
    for i, ref in enumerate((wq_ref, wk_ref, wv_ref)):
        out_ref[:, i * PAIR : (i + 1) * PAIR] = ref[:, :PAIR]
        out_ref[:, (i + 4) * PAIR : (i + 5) * PAIR] = ref[:, place]
    out_ref[:, 3 * PAIR : 4 * PAIR] = small.astype(BF)


def pack_wide_kernel(info_ref, up_ref, wo_ref, out_ref):
    part = info_ref[PART]

    @pl.when(part < QUARTERS - 1)
    def _():
        out_ref[...] = up_ref[:, pl.ds(pl.multiple_of(part * UP_PART, UP_PART), UP_PART)]

    @pl.when(part == QUARTERS - 1)
    def _():
        out_ref[...] = wo_ref[...]


def pack(kernel, info, arrays, shape, after=()):
    return call_with(
        kernel, (info, *arrays), after,
        in_specs=[SMEM] + [WHOLE] * len(arrays),
        out_specs=WHOLE,
        out_shape=jax.ShapeDtypeStruct(shape, BF),
        cost_estimate=cost(2),
    )


def join_kernel(own_ref, *refs):
    came_refs, (line_ref, out_ref) = refs[:-2], refs[-2:]
    width = line_ref.shape[-1]
    for i, ref in enumerate(came_refs):
        line_ref[i] = ref[:, :width]
    for i, ref in enumerate((own_ref, *came_refs)):
        for copy in range(QUARTERS):
            out_ref[copy, i] = ref[:, width:]


def join(own, came, after=()):
    arrays = (own, *came)
    shape = lambda *lead: jax.ShapeDtypeStruct(lead, BF)
    return call_with(
        join_kernel, arrays, after,
        in_specs=[WHOLE] * len(arrays),
        out_specs=[WHOLE] * 2,
        out_shape=[
            shape(len(came), BLOCK, 4 * PAIR), shape(QUARTERS, len(arrays), BLOCK, 3 * PAIR),
        ],
        cost_estimate=cost(2),
    )


def repeat_kernel(*refs):
    for i, ref in enumerate(refs[:-1]):
        for copy in range(QUARTERS):
            refs[-1][copy, i] = ref[...]


def repeat(parts, after=()):
    return call_with(
        repeat_kernel, tuple(parts), after,
        in_specs=[WHOLE] * len(parts),
        out_specs=WHOLE,
        out_shape=jax.ShapeDtypeStruct((QUARTERS, len(parts)) + parts[0].shape, BF),
        cost_estimate=cost(30),
    )


def turn_kernel(source_ref, out_ref):
    out_ref[:WIDTH, :] = source_ref[...].T
    out_ref[WIDTH:, :] = jnp.zeros((BLOCKS * BLOCK - WIDTH, source_ref.shape[0]), BF)


def turn(tokens, after=()):
    return call_with(
        turn_kernel, (tokens,), after,
        in_specs=[WHOLE],
        out_specs=WHOLE,
        out_shape=jax.ShapeDtypeStruct((BLOCKS * BLOCK, tokens.shape[0]), BF),
        cost_estimate=cost(50),
    )


def cut(down, after=()):
    return call_with(
        cut_kernel, (down,), after,
        in_specs=[WHOLE],
        out_specs=WHOLE,
        out_shape=jax.ShapeDtypeStruct((down.shape[0], WIDTH), BF),
        cost_estimate=cost(1),
    )


def cut_kernel(down_ref, out_ref):
    out_ref[...] = down_ref[:, :WIDTH]


def lay_line(info_ref, target, own_ref, twin_ref, came_ref, twins_ref):
    core, layer = info_ref[CORE], info_ref[LAYER]
    width = target.shape[1]
    target[rows_of(2 * layer + core), :] = own_ref[:, :width]
    target[rows_of(2 * layer + 1 - core), :] = twin_ref[:, :width]
    for step in range(1, LAYERS):
        source = (layer + LAYERS - step) % LAYERS
        target[rows_of(2 * source + core), :] = came_ref[step - 1, :, :width]
        target[rows_of(2 * source + 1 - core), :] = twins_ref[step - 1, :, :width]


def lay(info_ref, target, width, mine_ref, other_ref):
    core, layer = info_ref[CORE], info_ref[LAYER]
    for quarter in range(QUARTERS):
        columns = slice(quarter * width, (quarter + 1) * width)
        for slot in range(LAYERS):
            source = (layer + LAYERS - slot) % LAYERS
            target[rows_of(2 * source + core), columns] = mine_ref[quarter, slot]
            target[rows_of(2 * source + 1 - core), columns] = other_ref[quarter, slot]


def attend_kernel(shift, info_ref, token_ref, *refs):
    first = shift is None
    count = 4 if first else 2
    sources, refs = refs[:count], refs[count:]
    if first:
        vectors_ref = refs[7]
        refs = refs[:7] + refs[8:]
    else:
        vectors_ref = refs[0]
        refs = refs[1:]
    (
        exp_ref, context_ref, wide_ref, inverse_ref, query_t_ref, key_ref,
        value_t_ref, weight_ref, held_ref, left_ref,
    ) = refs
    rows = token_ref.shape[0]
    if first:
        lay_line(info_ref, weight_ref, *sources)
        vectors_ref[...] = weight_ref[:, 3 * PAIR :].astype(F32).T[:16]
        bq = vectors_ref[0:1, :PAIR]
        bv = vectors_ref[1:2, :PAIR]
        weights = weight_ref[:WIDTH, : 3 * PAIR]
    else:
        @pl.when(pl.program_id(0) == 0)
        def _():
            lay(info_ref, weight_ref, 3 * PAIR, *sources)

        pair = pl.program_id(0) + shift
        place = pl.ds(pl.multiple_of(pair * PAIR, PAIR), PAIR)
        bq = vectors_ref[0:1, place]
        bv = vectors_ref[1:2, place]
        place = pl.ds(pl.multiple_of((pair - 1) * 3 * PAIR, 3 * PAIR), 3 * PAIR)
        weights = weight_ref[:WIDTH, place]
    product = dot(token_ref[...], weights, 1, 0)
    query = (product[:, :PAIR] + bq).astype(BF)
    key = product[:, PAIR : 2 * PAIR].astype(BF)
    value = (product[:, 2 * PAIR :] + bv).astype(BF)
    key_t = key.T
    query_t_ref[...] = query.T
    key_ref[...] = key
    value_t_ref[...] = value.T
    key_place = lax.broadcasted_iota(jnp.int32, (1, rows), 1)
    bias = jnp.where(key_place < info_ref[LENGTH], 0.0, MASKED)
    scaled = query.astype(F32) * HEAD_DIM**-0.5
    key_wide = key_t.astype(F32)
    value_wide = value.astype(F32)
    block = 128
    step = pl.program_id(0)

    def leave(half, start):
        lines = pl.ds(start, 2 * block)
        return pltpu.make_async_copy(
            held_ref.at[half, lines],
            exp_ref.at[2 * step + half, lines],
            left_ref.at[half, start // (2 * block)],
        )

    results = []
    for half in range(2):
        left = side((rows, PAIR), 1, half, scaled, 1.0).astype(BF)
        place = lax.broadcasted_iota(jnp.int32, (PAIR, rows), 0)
        right = jnp.where(place == (HEAD_DIM if half == 0 else 0), bias, key_wide).astype(BF)
        for start in range(0, rows, block):
            scores = dot(left[start : start + block], right, 1, 0)
            highest = jnp.max(scores, 1, keepdims=True)
            held_ref[half, start : start + block, :] = jnp.exp(scores - highest).astype(BF)
            if start % (2 * block):
                leave(half, start - block).start()
        values = side((rows, PAIR), 1, half, value_wide, 1.0).astype(BF)
        total = dot(held_ref[half], values, 1, 0)
        flag = HEAD_DIM if half == 0 else 0
        inverse = 1.0 / total[:, flag : flag + 1]
        results.append((total * inverse, inverse))
    low = lax.broadcasted_iota(jnp.int32, (rows, PAIR), 1) < HEAD_DIM
    context = jnp.where(low, results[0][0], results[1][0])
    wide_ref[...] = context
    context_ref[...] = context.astype(BF)
    inverse_ref[...] = jnp.where(low, results[0][1], results[1][1])
    for half in range(2):
        for start in range(0, rows, 2 * block):
            leave(half, start).wait()


def attend(info, tokens, sources, start, pairs, weight, vectors=None, after=()):
    rows = tokens.shape[0]
    first = vectors is None
    width = (4 if first else 12) * PAIR
    tall = lambda: pl.BlockSpec((rows, PAIR), lambda p: (0, p))
    flat = lambda: pl.BlockSpec((PAIR, rows), lambda p: (p, 0))
    array = lambda kind: jax.ShapeDtypeStruct((rows, pairs * PAIR), kind)
    turned = jax.ShapeDtypeStruct((pairs * PAIR, rows), BF)
    table = (16, BLOCKS * BLOCK)
    fixed = pl.BlockSpec(table, lambda p: (0, 0))
    return call_with(
        functools.partial(attend_kernel, None if first else start),
        (info, tokens, *sources, *(() if first else (vectors,))),
        after,
        grid=(pairs,),
        in_specs=[SMEM, WHOLE] + [WHOLE] * len(sources) + ([] if first else [fixed]),
        out_specs=[
            IDLE,
            tall(), tall(), tall(), flat(), tall(), flat(),
        ]
        + ([fixed] if first else []),
        out_shape=[
            jax.ShapeDtypeStruct((2 * pairs, rows, rows), BF),
            array(BF), array(F32), array(F32), turned, array(BF), turned,
        ]
        + ([jax.ShapeDtypeStruct(table, F32)] if first else []),
        scratch_shapes=[
            pltpu.VMEM((BLOCKS * BLOCK, width), BF),
            pltpu.VMEM((2, rows, rows), BF),
            pltpu.SemaphoreType.DMA((2, rows // 256)),
        ],
        cost_estimate=cost(weight),
    )


def gelu_pair(values):
    t = 1.0 / (1.0 + (0.3275911 * 0.5**0.5) * jnp.abs(values))
    bell = jnp.exp(-0.5 * values * values)
    tail = t * (0.5 * 0.254829592 + t * (0.5 * -0.284496736 + t * (0.5 * 1.421413741 + t * (
        0.5 * -1.453152027 + t * (0.5 * 1.061405429)))))
    tail = tail * bell
    share = jnp.where(values >= 0.0, 1.0 - tail, tail)
    return values * share, share + values * bell * 0.3989422804014327


def row_mean(values):
    return jnp.sum(values, 1, keepdims=True) * (1.0 / WIDTH)


def column_sum(values):
    return jnp.sum(values, 0, keepdims=True)


def row_mean(values):
    return jnp.sum(values, 1, keepdims=True) * (1.0 / WIDTH)


def column_sum(values):
    return jnp.sum(values, 0, keepdims=True)


def up_places():
    for block in range(HIDDEN_PAD // (QUARTERS * BLOCK)):
        for quarter in range(QUARTERS):
            start = (block * QUARTERS + quarter) * BLOCK
            row = slice(8 + quarter, 9 + quarter)
            yield slice(start, start + BLOCK), row, slice(block * BLOCK, (block + 1) * BLOCK)


def feed_kernel(
    info_ref, context_0_ref, context_1_ref, context_2_ref, token_ref, cotangent_ref, *refs
):
    sources, refs = refs[:2], refs[2:]
    (
        down_ref, vector_ref,
        output_ref, first_ref, grad_context_ref, sums_ref, b1_sum_ref, down_term_ref, keep_ref,
        send_ref, w1_ref, w2_ref, b1_ref, product_ref,
        context_ref, normed_ref, active_ref, hidden_ref, feed_ref, branch_ref,
    ) = refs
    step = pl.program_id(0)
    rows = token_ref.shape[0]

    @pl.when(step == 0)
    def _():
        lay(info_ref, w1_ref, UP_PART, *sources)
        last = slice(HIDDEN_PAD - PAIR, HIDDEN_PAD)
        lane = lax.broadcasted_iota(jnp.int32, (BLOCKS * BLOCK, PAIR), 1)
        kept = lane < HIDDEN_SIZE - (HIDDEN_PAD - PAIR)
        w1_ref[:, last] = jnp.where(kept, w1_ref[:, last].astype(F32), 0.0).astype(BF)
        w2_ref[:HIDDEN_SIZE, :] = down_ref[:HIDDEN_SIZE, :]
        for place, row, columns in up_places():
            b1_ref[:, place] = vector_ref[row, columns]
        lane = lax.broadcasted_iota(jnp.int32, (1, HIDDEN_PAD), 1)
        b1_ref[...] = jnp.where(lane < HIDDEN_SIZE, b1_ref[...], 0.0)
        w2_ref[HIDDEN_SIZE:, :] = jnp.zeros((HIDDEN_PAD - HIDDEN_SIZE, WIDTH), BF)

    steps = normed_ref.shape[0] // rows
    down_steps = HIDDEN_PAD // UP_PART

    @pl.when(step < steps)
    def _():
        here = pl.ds(pl.multiple_of(step * rows, rows), rows)
        wo = w1_ref[:WIDTH, HIDDEN_PAD : HIDDEN_PAD + WIDTH]
        w1, w2 = w1_ref[:WIDTH, :HIDDEN_PAD], w2_ref[...]
        place = lax.broadcasted_iota(jnp.int32, (rows, 1), 0) + step * rows
        live = jnp.where(place < info_ref[LENGTH], 1.0, 0.0)
        vector = lambda i: vector_ref[i : i + 1, :WIDTH]
        out_add, down_add = vector(2), vector(3)
        gain_one, shift_one, gain_two, shift_two = vector(4), vector(5), vector(6), vector(7)
        context = jnp.concatenate([context_0_ref[...], context_1_ref[...], context_2_ref[...]], axis=1)
        context_ref[here, :] = context
        first_sum = token_ref[...].astype(F32) + dot(context, wo, 1, 0) + out_add
        center = first_sum - row_mean(first_sum)
        rate_one = lax.rsqrt(row_mean(center * center) + EPSILON)
        unit_one = center * rate_one
        normed = (unit_one * gain_one + shift_one).astype(BF)
        normed_ref[here, :] = normed
        pre = dot(normed, w1, 1, 0) + b1_ref[...]
        active_full, slope = gelu_pair(pre)
        active = active_full.astype(BF)
        active_ref[here, :] = active
        second_sum = normed.astype(F32) + dot(active, w2, 1, 0) + down_add
        center = second_sum - row_mean(second_sum)
        rate_two = lax.rsqrt(row_mean(center * center) + EPSILON)
        unit_two = center * rate_two
        output_ref[...] = ((unit_two * gain_two + shift_two) * live).astype(BF)
        cotangent = cotangent_ref[...].astype(F32) * live
        inner = cotangent * gain_two
        grad_second = rate_two * (inner - row_mean(inner) - unit_two * row_mean(inner * unit_two))
        grad_feed = grad_second.astype(BF)
        feed_ref[here, :] = grad_feed
        grad_hidden = (dot(grad_feed, w2, 1, 1) * slope).astype(BF)
        hidden_ref[here, :] = grad_hidden
        grad_normed = grad_second + dot(grad_hidden, w1, 1, 1)
        inner = grad_normed * gain_one
        grad_first = rate_one * (inner - row_mean(inner) - unit_one * row_mean(inner * unit_one))
        first_ref[...] = grad_first
        grad_branch = grad_first.astype(BF)
        branch_ref[here, :] = grad_branch
        grad_context_ref[...] = dot(grad_branch, wo, 1, 1).astype(BF)
        sums = jnp.concatenate(
            [
                column_sum(grad_branch.astype(F32)),
                column_sum(grad_feed.astype(F32)),
                column_sum(grad_normed * unit_one),
                column_sum(grad_normed),
                column_sum(cotangent * unit_two),
                column_sum(cotangent),
                jnp.zeros((2, WIDTH), F32),
            ],
            axis=0,
        )
        b1_sum = column_sum(grad_hidden.astype(F32))

        @pl.when(step == 0)
        def _():
            sums_ref[...] = sums
            b1_sum_ref[...] = b1_sum

        @pl.when(step > 0)
        def _():
            sums_ref[...] += sums
            b1_sum_ref[...] += b1_sum

    @pl.when((step >= steps) & (step < steps + down_steps))
    def _():
        place = pl.ds(pl.multiple_of((step - steps) * UP_PART, UP_PART), UP_PART)
        down_term_ref[...] = dot(active_ref[:, place], feed_ref[...], 0, 0).astype(BF)

    @pl.when(step >= steps + down_steps)
    def _():
        part = step - steps - down_steps

        @pl.when(part == 0)
        def _():
            product_ref[WIDTH:, :] = jnp.zeros((BLOCKS * BLOCK - WIDTH, UP_PART), F32)

        @pl.when(part < QUARTERS - 1)
        def _():
            place = pl.ds(pl.multiple_of(part * UP_PART, UP_PART), UP_PART)
            product_ref[:WIDTH, :] = dot(normed_ref[...], hidden_ref[:, place], 0, 0)

        @pl.when(part == QUARTERS - 1)
        def _():
            product_ref[:WIDTH, :WIDTH] = dot(context_ref[...], branch_ref[...], 0, 0)

        deal(info_ref, product_ref, keep_ref, send_ref)


def feed(info, contexts, tokens, cotangent, wide, down, vectors, after=()):
    rows = tokens.shape[0]
    tile = 256
    steps = rows // tile
    down_steps = HIDDEN_PAD // UP_PART
    part = lambda width: pl.BlockSpec((tile, width), lambda i: (jnp.minimum(i, steps - 1), 0))
    whole = lambda *shape: pl.BlockSpec(shape, lambda i: (0, 0))
    array = lambda width, kind: jax.ShapeDtypeStruct((rows, width), kind)
    held = lambda width: pltpu.VMEM((rows, width), BF)
    place = lambda: pl.BlockSpec(
        (1, LAYERS, BLOCK, UP_PART),
        lambda i: (jnp.clip(i - steps - down_steps, 0, QUARTERS - 1), 0, 0, 0),
    )
    shared = jax.ShapeDtypeStruct((QUARTERS, LAYERS, BLOCK, UP_PART), BF)
    return call_with(
        feed_kernel, (info, *contexts, tokens, cotangent, *wide, down, vectors), after,
        grid=(steps + down_steps + QUARTERS,),
        in_specs=[SMEM]
        + [part(context.shape[1]) for context in contexts]
        + [part(WIDTH), part(WIDTH)]
        + [WHOLE] * len(wide)
        + [WHOLE]
        + [whole(*vectors.shape)],
        out_specs=[
            part(WIDTH), part(WIDTH), part(WIDTH), whole(8, WIDTH), whole(1, HIDDEN_PAD),
            pl.BlockSpec((UP_PART, WIDTH), lambda i: (jnp.clip(i - steps, 0, down_steps - 1), 0)),
            place(), place(),
        ],
        out_shape=[
            array(WIDTH, BF), array(WIDTH, F32), array(WIDTH, BF),
            jax.ShapeDtypeStruct((8, WIDTH), F32),
            jax.ShapeDtypeStruct((1, HIDDEN_PAD), F32),
            jax.ShapeDtypeStruct((down.shape[0], WIDTH), BF),
            shared, shared,
        ],
        scratch_shapes=[
            pltpu.VMEM((BLOCKS * BLOCK, QUARTERS * UP_PART), BF),
            pltpu.VMEM((HIDDEN_PAD, WIDTH), BF),
            pltpu.VMEM((1, HIDDEN_PAD), F32),
            pltpu.VMEM((BLOCKS * BLOCK, UP_PART), F32),
            held(WIDTH), held(WIDTH), held(HIDDEN_PAD), held(HIDDEN_PAD), held(WIDTH), held(WIDTH),
        ],
        cost_estimate=cost(50),
    )


def deal(info_ref, product_ref, keep_ref, send_ref):
    core = info_ref[CORE]
    for layer in range(LAYERS):
        keep_ref[0, layer] = product_ref[rows_of(2 * layer + core), :].astype(BF)
        send_ref[0, layer] = product_ref[rows_of(2 * layer + 1 - core), :].astype(BF)


def head_grad_kernel(info_ref, token_t_ref, low_ref, high_ref, keep_ref, send_ref, product_ref):
    step = pl.program_id(0)
    half = low_ref.shape[0]

    @pl.when(step < half)
    def _():
        product_ref[...] = dot(token_t_ref[...], low_ref[jnp.minimum(step, half - 1)], 1, 0)

    @pl.when(step >= half)
    def _():
        product_ref[...] = dot(token_t_ref[...], high_ref[jnp.maximum(step - half, 0)], 1, 0)

    deal(info_ref, product_ref, keep_ref, send_ref)


def head_grad(info, token_t, low, high, after=()):
    place = lambda: pl.BlockSpec((1, LAYERS, BLOCK, 3 * PAIR), lambda d: (d, 0, 0, 0))
    array = jax.ShapeDtypeStruct((QUARTERS, LAYERS, BLOCK, 3 * PAIR), BF)
    return call_with(
        head_grad_kernel, (info, token_t, low, high), after,
        grid=(QUARTERS,),
        in_specs=[SMEM] + [WHOLE] * 3,
        out_specs=[place(), place()],
        out_shape=[array, array],
        scratch_shapes=[pltpu.VMEM((BLOCKS * BLOCK, 3 * PAIR), F32)],
        cost_estimate=cost(6),
    )


def first_grad_kernel(
    info_ref, token_t_ref, together_ref, sums_ref, up_sum_ref, pair_0_ref, pair_1_ref, pair_2_ref,
    keep_ref, send_ref, product_ref, table_ref,
):
    product_ref[:, : 3 * PAIR] = dot(token_t_ref[...], together_ref[0], 1, 0)
    table_ref[...] = jnp.zeros_like(table_ref)
    start = 0
    for ref in (pair_0_ref, pair_1_ref, pair_2_ref):
        table_ref[0:2, start : start + ref.shape[1]] = ref[0:2, :]
        start += ref.shape[1]
    table_ref[2:8, :WIDTH] = sums_ref[0:6, :]
    for place, row, columns in up_places():
        table_ref[row, columns] = up_sum_ref[:, place]
    product_ref[:, 3 * PAIR :] = table_ref[...].T
    core = info_ref[CORE]
    for layer in range(LAYERS):
        kept = product_ref[rows_of(2 * layer + core), :].astype(BF)
        sent = product_ref[rows_of(2 * layer + 1 - core), :].astype(BF)
        for part in range(QUARTERS):
            columns = slice(part * PAIR, (part + 1) * PAIR)
            keep_ref[part, layer] = kept[:, columns]
            send_ref[part, layer] = sent[:, columns]


def first_grad(info, token_t, together, sums, up_sum, pair_sums, after=()):
    array = jax.ShapeDtypeStruct((QUARTERS, LAYERS, BLOCK, PAIR), BF)
    return call_with(
        first_grad_kernel, (info, token_t, together, sums, up_sum, *pair_sums), after,
        in_specs=[SMEM] + [WHOLE] * 7,
        out_specs=[WHOLE] * 2,
        out_shape=[array, array],
        scratch_shapes=[
            pltpu.VMEM((BLOCKS * BLOCK, 4 * PAIR), F32),
            pltpu.VMEM((PAIR, BLOCKS * BLOCK), F32),
        ],
        cost_estimate=cost(3),
    )


def meet_kernel(info_ref, keep_ref, came_ref, *out_refs):
    for apart in range(QUARTERS):
        quarter = info_ref[PART] ^ apart
        out_refs[apart][0] = keep_ref[quarter, 0] + came_ref[quarter, 0]


def meet_small_kernel(info_ref, keep_ref, came_ref, *out_refs):
    for apart in range(QUARTERS):
        quarter = info_ref[PART] ^ apart
        for step in range(LAYERS):
            source = (info_ref[LAYER] + step) % LAYERS
            out_refs[apart][step] = keep_ref[quarter, source] + came_ref[quarter, source]


def meet(info, keep, came, after=()):
    width = keep.shape[-1]
    if width == PAIR:
        return call_with(
            meet_small_kernel, (info, keep, came), after,
            in_specs=[SMEM, WHOLE, WHOLE],
            out_specs=[WHOLE] * QUARTERS,
            out_shape=[jax.ShapeDtypeStruct((LAYERS, BLOCK, width), BF)] * QUARTERS,
            cost_estimate=cost(2),
        )
    block = lambda: pl.BlockSpec(
        (QUARTERS, 1, BLOCK, width), lambda s, info: (0, (info[LAYER] + s) % LAYERS, 0, 0)
    )

    def run(info_ref, keep_ref, came_ref, *refs):
        meet_kernel(info_ref, keep_ref, came_ref, *refs[len(after) :])

    return pl.pallas_call(
        run,
        grid_spec=pltpu.PrefetchScalarGridSpec(
            num_scalar_prefetch=1,
            grid=(LAYERS,),
            in_specs=[block(), block()] + [IDLE] * len(after),
            out_specs=[pl.BlockSpec((1, BLOCK, width), lambda s, info: (s, 0, 0))] * QUARTERS,
        ),
        out_shape=[jax.ShapeDtypeStruct((LAYERS, BLOCK, width), BF)] * QUARTERS,
        compiler_params=params(),
        cost_estimate=cost(3),
    )(info, keep, came, *after)


def attend_back_kernel(
    grad_ref, wide_ref, inverse_ref, exp_ref, query_t_ref, key_ref, value_t_ref,
    together_ref, sums_ref, score_ref,
):
    rows = grad_ref.shape[0]
    inverse = inverse_ref[...]
    grad = grad_ref[...].astype(F32)
    scaled = grad * inverse
    dots = scaled * wide_ref[...]
    scaled_t = scaled.T.astype(BF)
    value_wide = value_t_ref[...].astype(F32)
    lane = lax.broadcasted_iota(jnp.int32, (rows, PAIR), 1)
    place = lax.broadcasted_iota(jnp.int32, (PAIR, rows), 0)
    block = 128
    dq, dk_t, dv_t = [], [], []
    for half in range(2):
        mine = (lane < HEAD_DIM) if half == 0 else (lane >= HEAD_DIM)
        flag = HEAD_DIM if half == 0 else 0
        offset = jnp.sum(jnp.where(mine, -dots, 0.0), 1, keepdims=True)
        high = offset.astype(BF).astype(F32)
        rest = offset - high
        left = jnp.where(
            mine, scaled, jnp.where(lane == flag, high, jnp.where(lane == flag + 1, rest, 0.0))
        ).astype(BF)
        right = jnp.where((place == flag) | (place == flag + 1), 1.0, value_wide).astype(BF)
        for start in range(0, rows, block):
            grad_probs = dot(left[start : start + block], right, 1, 0)
            weight = exp_ref[half, start : start + block, :].astype(F32)
            score_ref[half, start : start + block, :] = (grad_probs * weight).astype(BF)
        own = slice(half * HEAD_DIM, (half + 1) * HEAD_DIM)
        dv_t.append(dot(scaled_t[own], exp_ref[half], 1, 0))
        dk_t.append(dot(query_t_ref[own, :], score_ref[half], 1, 0))
        dq.append(dot(score_ref[half], key_ref[...], 1, 0))
    factor = HEAD_DIM**-0.5
    dq_low = (jnp.where(lane < HEAD_DIM, dq[0], dq[1]) * factor).astype(BF)
    dk_low = (jnp.concatenate(dk_t, axis=0) * factor).T.astype(BF)
    dv_low = jnp.concatenate(dv_t, axis=0).T.astype(BF)
    together_ref[0] = jnp.concatenate([dq_low, dk_low, dv_low], axis=1)
    query_sum = column_sum(dq_low.astype(F32))
    value_sum = column_sum(dv_low.astype(F32))
    sums_ref[...] = jnp.concatenate([query_sum, value_sum, jnp.zeros((6, PAIR), F32)], axis=0)


def attend_back(grad_context, saved, start, offset, pairs, weight, after=()):
    exps, wide, inverse, query_t, key, value_t = saved
    rows = grad_context.shape[0]
    tall = lambda first: pl.BlockSpec((rows, PAIR), lambda p: (0, first + p))
    flat = lambda: pl.BlockSpec((PAIR, rows), lambda p: (offset + p, 0))
    return call_with(
        attend_back_kernel,
        (grad_context, wide, inverse, exps, query_t, key, value_t),
        after,
        grid=(pairs,),
        in_specs=[
            tall(start), tall(offset), tall(offset),
            pl.BlockSpec((2, rows, rows), lambda p: (offset + p, 0, 0)),
            flat(), tall(offset), flat(),
        ],
        out_specs=[
            pl.BlockSpec((1, rows, 3 * PAIR), lambda p: (p, 0, 0)),
            pl.BlockSpec((8, PAIR), lambda p: (0, p)),
        ],
        out_shape=[
            jax.ShapeDtypeStruct((pairs, rows, 3 * PAIR), BF),
            jax.ShapeDtypeStruct((8, pairs * PAIR), F32),
        ],
        scratch_shapes=[pltpu.VMEM((2, rows, rows), BF)],
        cost_estimate=cost(weight),
    )


def token_kernel(info_ref, grad_ref, together_0_ref, together_1_ref, together_2_ref, *refs):
    count = 4
    first_sources, rest_sources = refs[:count], refs[count : count + 2]
    out_ref, first_ref, rest_ref = refs[-3:]

    @pl.when(pl.program_id(0) == 0)
    def _():
        lay_line(info_ref, first_ref, *first_sources)
        lay(info_ref, rest_ref, 3 * PAIR, *rest_sources)

    pieces = [ref[i] for ref in (together_1_ref, together_2_ref) for i in range(ref.shape[0])]
    total = grad_ref[...] + dot(together_0_ref[0], first_ref[:WIDTH, : 3 * PAIR], 1, 1)
    total += dot(jnp.concatenate(pieces, axis=1), rest_ref[:WIDTH, :], 1, 1)
    out_ref[...] = total.astype(BF)


def token_back(info, grad_first, togethers, first, rest, after):
    rows = grad_first.shape[0]
    tile = 256
    part = pl.BlockSpec((tile, WIDTH), lambda i: (i, 0))
    piece = lambda array: pl.BlockSpec((array.shape[0], tile, 3 * PAIR), lambda i: (0, i, 0))
    return call_with(
        token_kernel, (info, grad_first, *togethers, *first, *rest), after,
        grid=(rows // tile,),
        in_specs=[SMEM, part]
        + [piece(array) for array in togethers]
        + [WHOLE] * (len(first) + len(rest)),
        out_specs=part,
        out_shape=jax.ShapeDtypeStruct((rows, WIDTH), BF),
        scratch_shapes=[
            pltpu.VMEM((BLOCKS * BLOCK, 4 * PAIR), BF),
            pltpu.VMEM((BLOCKS * BLOCK, 12 * PAIR), BF),
        ],
        cost_estimate=cost(7),
    )


def plane_kernel(groups, *refs):
    inputs, outputs = refs[: groups * QUARTERS], refs[groups * QUARTERS :]
    start = 0
    for group in range(groups):
        mine = inputs[group * QUARTERS : (group + 1) * QUARTERS]
        width = mine[0].shape[-1]
        for step in range(LAYERS):
            total = sum(ref[step].astype(F32) for ref in mine)
            outputs[step][:, start : start + width] = total.astype(BF)
        start += width


def plane(groups, after=()):
    width = sum(group[0].shape[-1] for group in groups)
    return call_with(
        functools.partial(plane_kernel, len(groups)),
        tuple(array for group in groups for array in group),
        after,
        in_specs=[WHOLE] * (len(groups) * QUARTERS),
        out_specs=[WHOLE] * LAYERS,
        out_shape=[jax.ShapeDtypeStruct((BLOCK, width), BF)] * LAYERS,
        cost_estimate=cost(2),
    )


def line_kernel(counts, *refs):
    inputs, out_ref = refs[:-1], refs[-1]
    start = 0
    for count in counts:
        mine, inputs = inputs[:count], inputs[count:]
        width = mine[0].shape[-1]
        parts = [ref[...] for ref in mine] if count > 1 else [mine[0][i] for i in range(QUARTERS)]
        total = sum(part.astype(F32) for part in parts).astype(BF)
        for copy in range(QUARTERS):
            out_ref[copy, :, start : start + width] = total
        start += width


def line(groups, after=()):
    width = sum(group[0].shape[-1] for group in groups)
    arrays = tuple(array for group in groups for array in group)
    return call_with(
        functools.partial(line_kernel, [len(group) for group in groups]), arrays, after,
        in_specs=[WHOLE] * len(arrays),
        out_specs=WHOLE,
        out_shape=jax.ShapeDtypeStruct((QUARTERS, BLOCK, width), BF),
        cost_estimate=cost(1),
    )


def finish_wide_kernel(info_ref, wide_ref, wo_ref, up_ref, down_ref):
    extra = wo_ref.shape[1] - WIDTH
    blank = jnp.zeros((BLOCK, extra), F32)
    used = HIDDEN_PAD // (QUARTERS * BLOCK)
    owner = 2 * info_ref[LAYER] + info_ref[CORE]
    for quarter in range(QUARTERS):
        lines = slice(quarter * BLOCK, (quarter + 1) * BLOCK)
        down = wide_ref[quarter, :, UP_PART:].astype(F32)
        down_ref[lines, :WIDTH] = jnp.where(owner < used, down, 0.0)
        down_ref[lines, WIDTH:] = blank
    for quarter in range(QUARTERS - 1):
        columns = slice(quarter * UP_PART, (quarter + 1) * UP_PART)
        up_ref[:, columns] = wide_ref[quarter, :, :UP_PART].astype(F32)
    up_ref[:, HIDDEN_PAD:] = jnp.zeros((BLOCK, up_ref.shape[1] - HIDDEN_PAD), F32)
    wo_ref[:, :WIDTH] = wide_ref[QUARTERS - 1, :, :WIDTH].astype(F32)
    wo_ref[:, WIDTH:] = blank


def finish_wide(info, wide, super_width, super_hidden, after=()):
    array = lambda *shape: jax.ShapeDtypeStruct(shape, F32)
    return call_with(
        finish_wide_kernel, (info, wide), after,
        in_specs=[SMEM, WHOLE],
        out_specs=[WHOLE] * 3,
        out_shape=[
            array(BLOCK, super_width), array(BLOCK, super_hidden),
            array(QUARTERS * BLOCK, super_width),
        ],
        cost_estimate=cost(3),
    )


def finish_heads_kernel(heads_ref, *refs):
    three, line_refs, up_line_ref = refs[:3], refs[3:11], refs[11]
    for i, ref in enumerate(three):
        ref[:, :PAIR] = heads_ref[i, :, 3 * PAIR :].astype(F32)
        for pair in range(1, PAIRS):
            part = heads_ref[pair - 1, :, i * PAIR : (i + 1) * PAIR]
            ref[:, pair * PAIR : (pair + 1) * PAIR] = part.astype(F32)
        ref[:, WIDTH:] = jnp.zeros((BLOCK, ref.shape[1] - WIDTH), F32)
    lines = heads_ref[QUARTERS - 1, :, 3 * PAIR :].astype(F32).T
    for i, ref in enumerate(line_refs):
        ref[...] = lines[i]
    up_line_ref[...] = lines[8 : 8 + QUARTERS]


def finish_heads(heads, super_width):
    array = lambda *shape: jax.ShapeDtypeStruct(shape, F32)
    return call_with(
        finish_heads_kernel, (heads,), (),
        in_specs=[WHOLE],
        out_specs=[WHOLE] * 12,
        out_shape=[array(BLOCK, super_width)] * 3
        + [array(BLOCK)] * 8
        + [array(QUARTERS, BLOCK)],
        cost_estimate=cost(2),
    )


SWAP = [(i, i ^ 1) for i in range(BLOCKS)]
STEPS = range(1, LAYERS)
DISTANCES = range(1, QUARTERS)


def twin(part):
    return lax.ppermute(part, "fsdp", SWAP)


def along(part, step):
    pairs = [(i, (i + 2 * step) % BLOCKS) for i in range(BLOCKS)]
    return lax.ppermute(part, "fsdp", pairs)


LINES = [[2 * layer + core for layer in range(LAYERS)] for core in range(2)]


def trade_plane(parts):
    return lax.all_to_all(parts, "dp", 0, 0)


def trade_line(parts):
    return lax.all_to_all(parts, "fsdp", 0, 0, axis_index_groups=LINES)


def copies(part):
    return jnp.broadcast_to(part[None], (QUARTERS,) + part.shape)


def across(part, apart):
    return lax.ppermute(part, "dp", [(i, i ^ apart) for i in range(QUARTERS)])


def drop(saved):
    return (saved[0],) + tuple(saved[2:])


def on_device(
    tokens, lengths, query_weight, key_weight, value_weight, out_weight, up_weight, down_weight,
    query_bias, value_bias, out_bias, up_bias, down_bias, first_gain, first_shift, second_gain,
    second_shift, cotangent,
):
    super_width, super_hidden = query_weight.shape[1], up_weight.shape[1]
    index = lax.axis_index("fsdp").astype(jnp.int32)
    part = lax.axis_index("dp").astype(jnp.int32)
    info = jnp.stack([lengths[0], index % 2, part, index // 2])
    qkv = (query_weight, key_weight, value_weight)
    small = (
        query_bias, value_bias, out_bias, down_bias,
        first_gain, first_shift, second_gain, second_shift, up_bias,
    )
    first_own = pack(pack_first_kernel, info, qkv + small, (BLOCK, 7 * PAIR))
    first_came = [along(first_own, step) for step in STEPS]
    wide_own = pack(
        pack_wide_kernel, info, (up_weight, out_weight), (BLOCK, UP_PART), after=(first_own,)
    )
    first_line, rest_copies = join(first_own, first_came, after=(wide_own,))
    first = (first_own, twin(first_own), first_line, twin(first_line))
    rest_mine = trade_plane(rest_copies)
    down_cut = cut(down_weight, after=(wide_own, *first))
    wide_line = [wide_own] + [along(wide_own, step) for step in STEPS]
    down = lax.all_gather(down_cut, "fsdp", axis=0, tiled=True)
    *saved_0, vectors = attend(info, tokens, first, 0, 1, 8, after=(down_cut,))
    rest = (rest_mine, twin(rest_mine))
    wide_mine = trade_plane(repeat(wide_line, after=(saved_0[1],)))
    saved_1 = attend(info, tokens, rest, 1, 3, 50, vectors, after=wide_line)
    wide = (wide_mine, twin(lax.optimization_barrier((wide_mine, saved_1[1]))[0]))
    saved_2 = attend(info, tokens, rest, 4, 1, 50, vectors, after=(saved_1[1], wide_mine))
    contexts = [saved[1] for saved in (saved_0, saved_1, saved_2)]
    (
        output, grad_first, grad_context, sums, up_sum, down_term, up_keep, up_send
    ) = feed(info, contexts, tokens, cotangent, wide, down, vectors)
    down_total = lax.psum_scatter(down_term, "fsdp", scatter_dimension=0, tiled=True)
    token_t = turn(tokens, after=(up_keep,))
    up_near = meet(info, up_keep, twin(up_send), after=(token_t,))
    send = lambda near: [near[0]] + [across(near[apart], apart) for apart in DISTANCES]
    pass_on = lambda layers: [layers[0]] + [along(layers[step], step) for step in STEPS]
    up_plane = send(up_near)
    together_1, sums_1 = attend_back(grad_context, drop(saved_1), 1, 0, 3, 1, after=(up_near[0],))
    up_layers = plane([up_plane], after=(together_1,))
    up_line = pass_on(up_layers)
    together_2, sums_2 = attend_back(grad_context, drop(saved_2), 4, 0, 1, 50, after=(up_layers[0],))
    head_keep, head_send = head_grad(info, token_t, together_1, together_2, after=up_line[1:])
    down_plane = trade_plane(down_total.reshape(QUARTERS, BLOCK, WIDTH))
    head_near = meet(info, head_keep, twin(head_send), after=(down_total,))
    head_plane = send(head_near)
    together_0, sums_0 = attend_back(
        grad_context, drop(saved_0), 0, 0, 1, 8, after=(head_near[0],)
    )
    first_keep, first_send = first_grad(
        info, token_t, together_0, sums, up_sum, (sums_0, sums_1, sums_2),
        after=(down_plane, *head_plane[1:]),
    )
    wide_copies = line([up_line, [down_plane]], after=(first_keep,))
    wide_total = trade_plane(wide_copies)
    first_near = meet(info, first_keep, twin(first_send), after=(wide_copies,))
    first_plane = send(first_near)
    layers = plane([head_plane, first_plane])
    token_grad = token_back(
        info, grad_first, (together_0, together_1, together_2), first, rest, (layers[0],)
    )
    head_copies = line([pass_on(layers)], after=(token_grad, wide_total))
    head_total = trade_plane(head_copies)
    wo, up, down = finish_wide(info, wide_total, super_width, super_hidden, after=(head_copies,))
    *results, up_lines = finish_heads(head_total, super_width)
    heads, lines = results[:3], results[3:]
    order = lines[:3] + [up_lines.reshape(-1)] + lines[3:]
    return (output, token_grad, *heads, wo, up, down, *order)


def widen(matrix, row_count, column_count):
    return jnp.pad(matrix, ((0, row_count - matrix.shape[0]), (0, column_count - matrix.shape[1])))


def on_device_elsewhere(
    tokens, lengths, query_weight, key_weight, value_weight, out_weight, up_weight, down_weight,
    query_bias, value_bias, out_bias, up_bias, down_bias, first_gain, first_shift, second_gain,
    second_shift, cotangent,
):
    owned, super_width = query_weight.shape
    super_hidden = up_weight.shape[1]
    info = jnp.stack([lengths[0]] + [jnp.zeros((), jnp.int32)] * 3)
    gather = lambda array: lax.all_gather(array, "fsdp", axis=0, tiled=True)
    qkv = [gather(array) for array in (query_weight, key_weight, value_weight)]
    lines = [
        gather(array)
        for array in (
            query_bias, value_bias, out_bias, down_bias,
            first_gain, first_shift, second_gain, second_shift,
        )
    ]
    up_lines = gather(up_bias).reshape(BLOCKS, QUARTERS, BLOCK).transpose(1, 0, 2)
    lines = jnp.concatenate([jnp.stack(lines), up_lines.reshape(QUARTERS, -1)], axis=0)
    columns = jnp.pad(lines, ((0, PAIR - lines.shape[0]), (0, 0))).T
    first_full = jnp.concatenate([array[:, :PAIR] for array in qkv] + [columns], axis=1)
    places = [slice(pair * PAIR, (pair + 1) * PAIR) for pair in range(1, PAIRS)]
    rest_full = jnp.concatenate([array[:, place] for place in places for array in qkv], axis=1)
    wide_full = jnp.concatenate([gather(up_weight)[:, :HIDDEN_PAD], gather(out_weight)], axis=1)
    down = gather(down_weight)[:, :WIDTH]

    back = [(LAYERS - slot) % LAYERS for slot in range(LAYERS)]

    def pieces(full):
        blocks = full.reshape(LAYERS, 2, BLOCK, QUARTERS, -1).transpose(0, 1, 3, 2, 4)
        blocks = jnp.stack([blocks[layer] for layer in back], axis=2)
        return blocks[0], blocks[1]

    blocks = first_full.reshape(LAYERS, 2, BLOCK, -1)
    blocks = jnp.stack([blocks[layer] for layer in back])
    first = (blocks[0, 0], blocks[0, 1], blocks[1:, 0], blocks[1:, 1])
    rest, wide = pieces(rest_full), pieces(wide_full)
    token_t = turn(tokens)
    *saved_0, vectors = attend(info, tokens, first, 0, 1, 8)
    saved_1 = attend(info, tokens, rest, 1, 3, 50, vectors)
    saved_2 = attend(info, tokens, rest, 4, 1, 50, vectors)
    contexts = [saved[1] for saved in (saved_0, saved_1, saved_2)]
    (
        output, grad_first, grad_context, sums, up_sum, down_term, *up_parts
    ) = feed(info, contexts, tokens, cotangent, wide, down, vectors)
    deep = lax.broadcasted_iota(jnp.int32, (super_hidden, 1), 0)
    down_term = jnp.where(deep < HIDDEN_PAD, down_term, 0.0)
    together_1, sums_1 = attend_back(grad_context, drop(saved_1), 1, 0, 3, 1)
    together_2, sums_2 = attend_back(grad_context, drop(saved_2), 4, 0, 1, 1)
    together_0, sums_0 = attend_back(grad_context, drop(saved_0), 0, 0, 1, 1)
    heads = (info, token_t, together_1, together_2)
    firsts = (info, token_t, together_0, sums, up_sum, (sums_0, sums_1, sums_2))

    def both(parts):
        return jnp.stack(parts, axis=2).transpose(1, 2, 3, 0, 4).reshape(super_width, -1)

    def total(array):
        array = lax.psum_scatter(array, "fsdp", scatter_dimension=0, tiled=True)
        return lax.psum(array, "dp").astype(F32)

    wide_total = total(both(up_parts))
    heads_total = total(both(head_grad(*heads))).reshape(owned, PAIRS - 1, 3, PAIR)
    first_total = total(both(first_grad(*firsts)))
    down_total = total(down_term)
    token_grad = token_back(
        info, grad_first, (together_0, together_1, together_2), first, rest, ()
    )
    full = lambda matrix: widen(matrix, owned, super_width)
    heads = [
        full(
            jnp.concatenate(
                [first_total[:, i * PAIR : (i + 1) * PAIR], heads_total[:, :, i].reshape(owned, -1)],
                axis=1,
            )
        )
        for i in range(3)
    ]
    lines = gather(first_total[:, 3 * PAIR :]).T
    up_lines = lines[8:12].reshape(QUARTERS, BLOCKS, BLOCK).transpose(1, 0, 2).reshape(-1)
    place = lax.axis_index("fsdp")
    mine = lambda array: lax.dynamic_slice_in_dim(array, place * owned, owned)
    deep = up_bias.shape[0]
    return (
        output, token_grad, *heads,
        full(wide_total[:, HIDDEN_PAD : HIDDEN_PAD + WIDTH]),
        widen(wide_total[:, :HIDDEN_PAD], owned, super_hidden),
        widen(down_total, deep, super_width),
        mine(lines[0]), mine(lines[1]), mine(lines[2]),
        lax.dynamic_slice_in_dim(up_lines, place * deep, deep),
        mine(lines[3]), mine(lines[4]), mine(lines[5]), mine(lines[6]), mine(lines[7]),
    )


def solution(mesh):
    rows = P(("dp", "fsdp"), None)
    held = P("fsdp", None)
    line = P("fsdp")
    near = mesh.shape["dp"] == QUARTERS and mesh.shape["fsdp"] == BLOCKS
    return jax.shard_map(
        on_device if near else on_device_elsewhere,
        mesh=mesh,
        in_specs=(rows, P(("dp", "fsdp"))) + (held,) * 6 + (line,) * 9 + (rows,),
        out_specs=(rows, rows) + (held,) * 6 + (line,) * 9,
        check_vma=False,
    )
```

```python
import functools

import jax
import jax.numpy as jnp
from jax import lax
from jax.experimental import pallas as pl
from jax.experimental.pallas import tpu as pltpu
from jax.sharding import PartitionSpec as P

HEAD_DIM = 64
HIDDEN_SIZE = 2240
WIDTH = 640
EPSILON = 1e-05
MASKED = -1e30
PAIR = 2 * HEAD_DIM
PAIRS = WIDTH // PAIR
BF = jnp.bfloat16
F32 = jnp.float32
VMEM_BYTES = 127 * 2**19
BLOCKS = 8
BLOCK = 96
QUARTERS = 4
LAYERS = BLOCKS // 2
HIDDEN_PAD = 2304
UP_PART = 768
PEAK = 10**9


def dot(left, right, left_dim, right_dim):
    return lax.dot_general(
        left, right, (((left_dim,), (right_dim,)), ((), ())), preferred_element_type=F32
    )


def side(shape, axis, half, own, flag):
    place = lax.broadcasted_iota(jnp.int32, shape, axis)
    mine = (place < HEAD_DIM) if half == 0 else (place >= HEAD_DIM)
    first = place == (HEAD_DIM if half == 0 else 0)
    return jnp.where(mine, own, jnp.where(first, flag, 0.0))


def rows_of(step):
    return pl.ds(pl.multiple_of(step * BLOCK, BLOCK), BLOCK)


def cost(microseconds):
    return pl.CostEstimate(flops=microseconds * PEAK, bytes_accessed=0, transcendentals=0)


def params():
    return pltpu.CompilerParams(vmem_limit_bytes=VMEM_BYTES)


SMEM = pl.BlockSpec(memory_space=pltpu.SMEM)
WHOLE = pl.BlockSpec(memory_space=pltpu.VMEM)
IDLE = pl.BlockSpec(memory_space=pl.ANY)
LENGTH, CORE, PART, LAYER = range(4)


def call_with(kernel, inputs, after, **options):
    specs = options.pop("in_specs") + [IDLE] * len(after)

    def run(*refs):
        kernel(*refs[: len(inputs)], *refs[len(inputs) + len(after) :])

    return pl.pallas_call(run, in_specs=specs, compiler_params=params(), **options)(*inputs, *after)


def pack_first_kernel(info_ref, wq_ref, wk_ref, wv_ref, *refs):
    small_refs, out_ref = refs[:9], refs[9]
    lines = [ref[...].astype(F32).reshape(1, BLOCK) for ref in small_refs[:8]]
    up_line = small_refs[8][...].astype(F32).reshape(1, -1)
    lines += [up_line[:, i * BLOCK : (i + 1) * BLOCK] for i in range(QUARTERS)]
    small = jnp.concatenate(lines + [jnp.zeros((PAIR - 12, BLOCK), F32)], axis=0).T
    place = pl.ds(pl.multiple_of((info_ref[PART] + 1) * PAIR, PAIR), PAIR)
    for i, ref in enumerate((wq_ref, wk_ref, wv_ref)):
        out_ref[:, i * PAIR : (i + 1) * PAIR] = ref[:, :PAIR]
        out_ref[:, (i + 4) * PAIR : (i + 5) * PAIR] = ref[:, place]
    out_ref[:, 3 * PAIR : 4 * PAIR] = small.astype(BF)


def pack_wide_kernel(info_ref, up_ref, wo_ref, out_ref):
    part = info_ref[PART]

    @pl.when(part < QUARTERS - 1)
    def _():
        out_ref[...] = up_ref[:, pl.ds(pl.multiple_of(part * UP_PART, UP_PART), UP_PART)]

    @pl.when(part == QUARTERS - 1)
    def _():
        out_ref[...] = wo_ref[...]


def pack(kernel, info, arrays, shape, after=()):
    return call_with(
        kernel, (info, *arrays), after,
        in_specs=[SMEM] + [WHOLE] * len(arrays),
        out_specs=WHOLE,
        out_shape=jax.ShapeDtypeStruct(shape, BF),
        cost_estimate=cost(2),
    )


def join_kernel(own_ref, *refs):
    came_refs, (line_ref, out_ref) = refs[:-2], refs[-2:]
    width = line_ref.shape[-1]
    for i, ref in enumerate(came_refs):
        line_ref[i] = ref[:, :width]
    for i, ref in enumerate((own_ref, *came_refs)):
        for copy in range(QUARTERS):
            out_ref[copy, i] = ref[:, width:]


def join(own, came, after=()):
    arrays = (own, *came)
    shape = lambda *lead: jax.ShapeDtypeStruct(lead, BF)
    return call_with(
        join_kernel, arrays, after,
        in_specs=[WHOLE] * len(arrays),
        out_specs=[WHOLE] * 2,
        out_shape=[
            shape(len(came), BLOCK, 4 * PAIR), shape(QUARTERS, len(arrays), BLOCK, 3 * PAIR),
        ],
        cost_estimate=cost(2),
    )


def repeat_kernel(*refs):
    for i, ref in enumerate(refs[:-1]):
        for copy in range(QUARTERS):
            refs[-1][copy, i] = ref[...]


def repeat(parts, after=()):
    return call_with(
        repeat_kernel, tuple(parts), after,
        in_specs=[WHOLE] * len(parts),
        out_specs=WHOLE,
        out_shape=jax.ShapeDtypeStruct((QUARTERS, len(parts)) + parts[0].shape, BF),
        cost_estimate=cost(30),
    )


def turn_kernel(source_ref, out_ref):
    out_ref[:WIDTH, :] = source_ref[...].T
    out_ref[WIDTH:, :] = jnp.zeros((BLOCKS * BLOCK - WIDTH, source_ref.shape[0]), BF)


def turn(tokens, after=()):
    return call_with(
        turn_kernel, (tokens,), after,
        in_specs=[WHOLE],
        out_specs=WHOLE,
        out_shape=jax.ShapeDtypeStruct((BLOCKS * BLOCK, tokens.shape[0]), BF),
        cost_estimate=cost(50),
    )


def cut(down, after=()):
    return call_with(
        cut_kernel, (down,), after,
        in_specs=[WHOLE],
        out_specs=WHOLE,
        out_shape=jax.ShapeDtypeStruct((down.shape[0], WIDTH), BF),
        cost_estimate=cost(1),
    )


def cut_kernel(down_ref, out_ref):
    out_ref[...] = down_ref[:, :WIDTH]


def lay_line(info_ref, target, own_ref, twin_ref, came_ref, twins_ref):
    core, layer = info_ref[CORE], info_ref[LAYER]
    width = target.shape[1]
    target[rows_of(2 * layer + core), :] = own_ref[:, :width]
    target[rows_of(2 * layer + 1 - core), :] = twin_ref[:, :width]
    for step in range(1, LAYERS):
        source = (layer + LAYERS - step) % LAYERS
        target[rows_of(2 * source + core), :] = came_ref[step - 1, :, :width]
        target[rows_of(2 * source + 1 - core), :] = twins_ref[step - 1, :, :width]


def lay(info_ref, target, width, mine_ref, other_ref):
    core, layer = info_ref[CORE], info_ref[LAYER]
    for quarter in range(QUARTERS):
        columns = slice(quarter * width, (quarter + 1) * width)
        for slot in range(LAYERS):
            source = (layer + LAYERS - slot) % LAYERS
            target[rows_of(2 * source + core), columns] = mine_ref[quarter, slot]
            target[rows_of(2 * source + 1 - core), columns] = other_ref[quarter, slot]


def attend_kernel(shift, info_ref, token_ref, *refs):
    first = shift is None
    count = 4 if first else 2
    sources, refs = refs[:count], refs[count:]
    if first:
        vectors_ref = refs[7]
        refs = refs[:7] + refs[8:]
    else:
        vectors_ref = refs[0]
        refs = refs[1:]
    (
        exp_ref, context_ref, wide_ref, inverse_ref, query_t_ref, key_ref,
        value_t_ref, mark_ref, weight_ref, held_ref, left_ref,
    ) = refs
    rows = token_ref.shape[0]
    if first:
        lay_line(info_ref, weight_ref, *sources)
        vectors_ref[...] = weight_ref[:, 3 * PAIR :].astype(F32).T[:16]
        bq = vectors_ref[0:1, :PAIR]
        bv = vectors_ref[1:2, :PAIR]
        weights = weight_ref[:WIDTH, : 3 * PAIR]
    else:
        @pl.when(pl.program_id(0) == 0)
        def _():
            lay(info_ref, weight_ref, 3 * PAIR, *sources)

        pair = pl.program_id(0) + shift
        place = pl.ds(pl.multiple_of(pair * PAIR, PAIR), PAIR)
        bq = vectors_ref[0:1, place]
        bv = vectors_ref[1:2, place]
        place = pl.ds(pl.multiple_of((pair - 1) * 3 * PAIR, 3 * PAIR), 3 * PAIR)
        weights = weight_ref[:WIDTH, place]
    product = dot(token_ref[...], weights, 1, 0)
    query = (product[:, :PAIR] + bq).astype(BF)
    key = product[:, PAIR : 2 * PAIR].astype(BF)
    value = (product[:, 2 * PAIR :] + bv).astype(BF)
    key_t = key.T
    query_t_ref[...] = query.T
    key_ref[...] = key
    value_t_ref[...] = value.T
    key_place = lax.broadcasted_iota(jnp.int32, (1, rows), 1)
    bias = jnp.where(key_place < info_ref[LENGTH], 0.0, MASKED)
    scaled = query.astype(F32) * HEAD_DIM**-0.5
    key_wide = key_t.astype(F32)
    value_wide = value.astype(F32)
    block = 128
    step = pl.program_id(0)

    def leave(half, start):
        lines = pl.ds(start, 2 * block)
        return pltpu.make_async_copy(
            held_ref.at[half, lines],
            exp_ref.at[2 * (step + (shift or 0)) + half, lines],
            left_ref.at[half, start // (2 * block)],
        )

    results = []
    for half in range(2):
        left = side((rows, PAIR), 1, half, scaled, 1.0).astype(BF)
        place = lax.broadcasted_iota(jnp.int32, (PAIR, rows), 0)
        right = jnp.where(place == (HEAD_DIM if half == 0 else 0), bias, key_wide).astype(BF)
        for start in range(0, rows, block):
            scores = dot(left[start : start + block], right, 1, 0)
            highest = jnp.max(scores, 1, keepdims=True)
            held_ref[half, start : start + block, :] = jnp.exp(scores - highest).astype(BF)
            if start % (2 * block):
                leave(half, start - block).start()
        values = side((rows, PAIR), 1, half, value_wide, 1.0).astype(BF)
        total = dot(held_ref[half], values, 1, 0)
        flag = HEAD_DIM if half == 0 else 0
        inverse = 1.0 / total[:, flag : flag + 1]
        results.append((total * inverse, inverse))
    low = lax.broadcasted_iota(jnp.int32, (rows, PAIR), 1) < HEAD_DIM
    context = jnp.where(low, results[0][0], results[1][0])
    mark_ref[...] = jnp.zeros_like(mark_ref)
    wide_ref[...] = context
    context_ref[...] = context.astype(BF)
    inverse_ref[...] = jnp.where(low, results[0][1], results[1][1])
    for half in range(2):
        for start in range(0, rows, 2 * block):
            leave(half, start).wait()


def attend(info, tokens, sources, start, pairs, vectors=None, held=(), after=()):
    rows = tokens.shape[0]
    first = vectors is None
    width = (4 if first else 12) * PAIR
    tall = lambda: pl.BlockSpec((rows, PAIR), lambda p: (0, start + p))
    flat = lambda: pl.BlockSpec((PAIR, rows), lambda p: (start + p, 0))
    array = lambda kind: jax.ShapeDtypeStruct((rows, WIDTH), kind)
    turned = jax.ShapeDtypeStruct((WIDTH, rows), BF)
    fixed = lambda *shape: pl.BlockSpec(shape, lambda p: (0, 0))
    table, mark = (16, BLOCKS * BLOCK), (8, 128)
    inputs = (info, tokens, *sources, *(() if first else (vectors,)))
    return call_with(
        functools.partial(attend_kernel, None if first else start),
        inputs,
        (*held, *after),
        grid=(pairs,),
        in_specs=[SMEM, WHOLE] + [WHOLE] * len(sources) + ([] if first else [fixed(*table)]),
        out_specs=[IDLE, tall(), tall(), tall(), flat(), tall(), flat()]
        + ([fixed(*table)] if first else [])
        + [fixed(*mark)],
        out_shape=[
            jax.ShapeDtypeStruct((2 * PAIRS, rows, rows), BF),
            array(BF), array(F32), array(F32), turned, array(BF), turned,
        ]
        + ([jax.ShapeDtypeStruct(table, F32)] if first else [])
        + [jax.ShapeDtypeStruct(mark, F32)],
        input_output_aliases={len(inputs) + i: i for i in range(len(held))},
        scratch_shapes=[
            pltpu.VMEM((BLOCKS * BLOCK, width), BF),
            pltpu.VMEM((2, rows, rows), BF),
            pltpu.SemaphoreType.DMA((2, rows // 256)),
        ],
        cost_estimate=cost(8 * pairs),
    )


def gelu_pair(values):
    t = 1.0 / (1.0 + (0.3275911 * 0.5**0.5) * jnp.abs(values))
    bell = jnp.exp(-0.5 * values * values)
    tail = t * (0.5 * 0.254829592 + t * (0.5 * -0.284496736 + t * (0.5 * 1.421413741 + t * (
        0.5 * -1.453152027 + t * (0.5 * 1.061405429)))))
    tail = tail * bell
    share = jnp.where(values >= 0.0, 1.0 - tail, tail)
    return values * share, share + values * bell * 0.3989422804014327


def row_mean(values):
    return jnp.sum(values, 1, keepdims=True) * (1.0 / WIDTH)


def column_sum(values):
    return jnp.sum(values, 0, keepdims=True)


def row_mean(values):
    return jnp.sum(values, 1, keepdims=True) * (1.0 / WIDTH)


def column_sum(values):
    return jnp.sum(values, 0, keepdims=True)


def up_places():
    for block in range(HIDDEN_PAD // (QUARTERS * BLOCK)):
        for quarter in range(QUARTERS):
            start = (block * QUARTERS + quarter) * BLOCK
            row = slice(8 + quarter, 9 + quarter)
            yield slice(start, start + BLOCK), row, slice(block * BLOCK, (block + 1) * BLOCK)


def feed_kernel(
    info_ref, context_in_ref, token_ref, cotangent_ref, *refs
):
    sources, refs = refs[:2], refs[2:]
    (
        down_ref, vector_ref,
        output_ref, first_ref, grad_context_ref, sums_ref, b1_sum_ref, down_term_ref, keep_ref,
        send_ref, w1_ref, w2_ref, b1_ref, product_ref,
        context_ref, normed_ref, active_ref, hidden_ref, feed_ref, branch_ref, came_ref,
    ) = refs
    step = pl.program_id(0)
    rows = token_ref.shape[0]

    @pl.when(step == 0)
    def _():
        core, layer = info_ref[CORE], info_ref[LAYER]
        copies = []
        for quarter in range(QUARTERS):
            columns = slice(quarter * UP_PART, (quarter + 1) * UP_PART)
            for slot in range(LAYERS):
                source = (layer + LAYERS - slot) % LAYERS
                for twin, ref in enumerate(sources):
                    block = 2 * source + (1 - core if twin else core)
                    target = w1_ref.at[rows_of(block), columns]
                    number = (quarter * LAYERS + slot) * 2 + twin
                    copies.append(
                        pltpu.make_async_copy(ref.at[quarter, slot], target, came_ref.at[number])
                    )
        lower = pltpu.make_async_copy(
            down_ref.at[:HIDDEN_PAD], w2_ref, came_ref.at[2 * QUARTERS * LAYERS]
        )
        copies.append(lower)
        for copy in copies:
            copy.start()
        for copy in copies:
            copy.wait()
        last = slice(HIDDEN_PAD - PAIR, HIDDEN_PAD)
        lane = lax.broadcasted_iota(jnp.int32, (BLOCKS * BLOCK, PAIR), 1)
        kept = lane < HIDDEN_SIZE - (HIDDEN_PAD - PAIR)
        w1_ref[:, last] = jnp.where(kept, w1_ref[:, last].astype(F32), 0.0).astype(BF)
        w2_ref[HIDDEN_SIZE:, :] = jnp.zeros((HIDDEN_PAD - HIDDEN_SIZE, WIDTH), BF)
        for place, row, columns in up_places():
            b1_ref[:, place] = vector_ref[row, columns]
        lane = lax.broadcasted_iota(jnp.int32, (1, HIDDEN_PAD), 1)
        b1_ref[...] = jnp.where(lane < HIDDEN_SIZE, b1_ref[...], 0.0)
        w2_ref[HIDDEN_SIZE:, :] = jnp.zeros((HIDDEN_PAD - HIDDEN_SIZE, WIDTH), BF)

    steps = normed_ref.shape[0] // rows
    down_steps = HIDDEN_PAD // UP_PART

    @pl.when(step < steps)
    def _():
        here = pl.ds(pl.multiple_of(step * rows, rows), rows)
        wo = w1_ref[:WIDTH, HIDDEN_PAD : HIDDEN_PAD + WIDTH]
        w1, w2 = w1_ref[:WIDTH, :HIDDEN_PAD], w2_ref[...]
        place = lax.broadcasted_iota(jnp.int32, (rows, 1), 0) + step * rows
        live = jnp.where(place < info_ref[LENGTH], 1.0, 0.0)
        vector = lambda i: vector_ref[i : i + 1, :WIDTH]
        out_add, down_add = vector(2), vector(3)
        gain_one, shift_one, gain_two, shift_two = vector(4), vector(5), vector(6), vector(7)
        context = context_in_ref[...]
        context_ref[here, :] = context
        first_sum = token_ref[...].astype(F32) + dot(context, wo, 1, 0) + out_add
        center = first_sum - row_mean(first_sum)
        rate_one = lax.rsqrt(row_mean(center * center) + EPSILON)
        unit_one = center * rate_one
        normed = (unit_one * gain_one + shift_one).astype(BF)
        normed_ref[here, :] = normed
        pre = dot(normed, w1, 1, 0) + b1_ref[...]
        active_full, slope = gelu_pair(pre)
        active = active_full.astype(BF)
        active_ref[here, :] = active
        second_sum = normed.astype(F32) + dot(active, w2, 1, 0) + down_add
        center = second_sum - row_mean(second_sum)
        rate_two = lax.rsqrt(row_mean(center * center) + EPSILON)
        unit_two = center * rate_two
        output_ref[...] = ((unit_two * gain_two + shift_two) * live).astype(BF)
        cotangent = cotangent_ref[...].astype(F32) * live
        inner = cotangent * gain_two
        grad_second = rate_two * (inner - row_mean(inner) - unit_two * row_mean(inner * unit_two))
        grad_feed = grad_second.astype(BF)
        feed_ref[here, :] = grad_feed
        grad_hidden = (dot(grad_feed, w2, 1, 1) * slope).astype(BF)
        hidden_ref[here, :] = grad_hidden
        grad_normed = grad_second + dot(grad_hidden, w1, 1, 1)
        inner = grad_normed * gain_one
        grad_first = rate_one * (inner - row_mean(inner) - unit_one * row_mean(inner * unit_one))
        first_ref[...] = grad_first
        grad_branch = grad_first.astype(BF)
        branch_ref[here, :] = grad_branch
        grad_context_ref[...] = dot(grad_branch, wo, 1, 1).astype(BF)
        sums = jnp.concatenate(
            [
                column_sum(grad_branch.astype(F32)),
                column_sum(grad_feed.astype(F32)),
                column_sum(grad_normed * unit_one),
                column_sum(grad_normed),
                column_sum(cotangent * unit_two),
                column_sum(cotangent),
                jnp.zeros((2, WIDTH), F32),
            ],
            axis=0,
        )
        b1_sum = column_sum(grad_hidden.astype(F32))

        @pl.when(step == 0)
        def _():
            sums_ref[...] = sums
            b1_sum_ref[...] = b1_sum

        @pl.when(step > 0)
        def _():
            sums_ref[...] += sums
            b1_sum_ref[...] += b1_sum

    @pl.when((step >= steps) & (step < steps + down_steps))
    def _():
        place = pl.ds(pl.multiple_of((step - steps) * UP_PART, UP_PART), UP_PART)
        down_term_ref[...] = dot(active_ref[:, place], feed_ref[...], 0, 0).astype(BF)

    @pl.when(step >= steps + down_steps)
    def _():
        part = step - steps - down_steps

        @pl.when(part == 0)
        def _():
            product_ref[WIDTH:, :] = jnp.zeros((BLOCKS * BLOCK - WIDTH, UP_PART), F32)

        @pl.when(part < QUARTERS - 1)
        def _():
            place = pl.ds(pl.multiple_of(part * UP_PART, UP_PART), UP_PART)
            product_ref[:WIDTH, :] = dot(normed_ref[...], hidden_ref[:, place], 0, 0)

        @pl.when(part == QUARTERS - 1)
        def _():
            product_ref[:WIDTH, :WIDTH] = dot(context_ref[...], branch_ref[...], 0, 0)

        deal(info_ref, product_ref, keep_ref, send_ref)


def feed(info, context, tokens, cotangent, wide, down, vectors, after=()):
    rows = tokens.shape[0]
    tile = rows // 4
    steps = rows // tile
    down_steps = HIDDEN_PAD // UP_PART
    part = lambda width: pl.BlockSpec((tile, width), lambda i: (jnp.minimum(i, steps - 1), 0))
    whole = lambda *shape: pl.BlockSpec(shape, lambda i: (0, 0))
    array = lambda width, kind: jax.ShapeDtypeStruct((rows, width), kind)
    held = lambda width: pltpu.VMEM((rows, width), BF)
    place = lambda: pl.BlockSpec(
        (1, LAYERS, BLOCK, UP_PART),
        lambda i: (jnp.clip(i - steps - down_steps, 0, QUARTERS - 1), 0, 0, 0),
    )
    shared = jax.ShapeDtypeStruct((QUARTERS, LAYERS, BLOCK, UP_PART), BF)
    return call_with(
        feed_kernel, (info, context, tokens, cotangent, *wide, down, vectors), after,
        grid=(steps + down_steps + QUARTERS,),
        in_specs=[SMEM]
        + [part(WIDTH), part(WIDTH), part(WIDTH)]
        + [IDLE] * (len(wide) + 1)
        + [whole(*vectors.shape)],
        out_specs=[
            part(WIDTH), part(WIDTH), part(WIDTH), whole(8, WIDTH), whole(1, HIDDEN_PAD),
            pl.BlockSpec((UP_PART, WIDTH), lambda i: (jnp.clip(i - steps, 0, down_steps - 1), 0)),
            place(), place(),
        ],
        out_shape=[
            array(WIDTH, BF), array(WIDTH, F32), array(WIDTH, BF),
            jax.ShapeDtypeStruct((8, WIDTH), F32),
            jax.ShapeDtypeStruct((1, HIDDEN_PAD), F32),
            jax.ShapeDtypeStruct((down.shape[0], WIDTH), BF),
            shared, shared,
        ],
        scratch_shapes=[
            pltpu.VMEM((BLOCKS * BLOCK, QUARTERS * UP_PART), BF),
            pltpu.VMEM((HIDDEN_PAD, WIDTH), BF),
            pltpu.VMEM((1, HIDDEN_PAD), F32),
            pltpu.VMEM((BLOCKS * BLOCK, UP_PART), F32),
            held(WIDTH), held(WIDTH), held(HIDDEN_PAD), held(HIDDEN_PAD), held(WIDTH), held(WIDTH),
            pltpu.SemaphoreType.DMA((2 * QUARTERS * LAYERS + 1,)),
        ],
        cost_estimate=cost(50),
    )


def deal(info_ref, product_ref, keep_ref, send_ref):
    core = info_ref[CORE]
    for layer in range(LAYERS):
        keep_ref[0, layer] = product_ref[rows_of(2 * layer + core), :].astype(BF)
        send_ref[0, layer] = product_ref[rows_of(2 * layer + 1 - core), :].astype(BF)


def head_grad_kernel(info_ref, token_t_ref, together_ref, keep_ref, send_ref, product_ref):
    product_ref[...] = dot(token_t_ref[...], together_ref[0], 1, 0)
    deal(info_ref, product_ref, keep_ref, send_ref)


def head_grad(info, token_t, together, after=()):
    rows = token_t.shape[1]
    place = lambda: pl.BlockSpec((1, LAYERS, BLOCK, 3 * PAIR), lambda d: (d, 0, 0, 0))
    array = jax.ShapeDtypeStruct((QUARTERS, LAYERS, BLOCK, 3 * PAIR), BF)
    return call_with(
        head_grad_kernel, (info, token_t, together), after,
        grid=(QUARTERS,),
        in_specs=[SMEM, WHOLE, pl.BlockSpec((1, rows, 3 * PAIR), lambda d: (d, 0, 0))],
        out_specs=[place(), place()],
        out_shape=[array, array],
        scratch_shapes=[pltpu.VMEM((BLOCKS * BLOCK, 3 * PAIR), F32)],
        cost_estimate=cost(6),
    )


def first_grad_kernel(
    info_ref, token_t_ref, together_ref, sums_ref, up_sum_ref, pair_0_ref, pair_1_ref,
    keep_ref, send_ref, product_ref, table_ref,
):
    product_ref[:, : 3 * PAIR] = dot(token_t_ref[...], together_ref[0], 1, 0)
    table_ref[...] = jnp.zeros_like(table_ref)
    start = 0
    for ref in (pair_0_ref, pair_1_ref):
        table_ref[0:2, start : start + ref.shape[1]] = ref[0:2, :]
        start += ref.shape[1]
    table_ref[2:8, :WIDTH] = sums_ref[0:6, :]
    for place, row, columns in up_places():
        table_ref[row, columns] = up_sum_ref[:, place]
    product_ref[:, 3 * PAIR :] = table_ref[...].T
    core = info_ref[CORE]
    for layer in range(LAYERS):
        kept = product_ref[rows_of(2 * layer + core), :].astype(BF)
        sent = product_ref[rows_of(2 * layer + 1 - core), :].astype(BF)
        for part in range(QUARTERS):
            columns = slice(part * PAIR, (part + 1) * PAIR)
            keep_ref[part, layer] = kept[:, columns]
            send_ref[part, layer] = sent[:, columns]


def first_grad(info, token_t, together, sums, up_sum, pair_sums, after=()):
    array = jax.ShapeDtypeStruct((QUARTERS, LAYERS, BLOCK, PAIR), BF)
    return call_with(
        first_grad_kernel, (info, token_t, together, sums, up_sum, *pair_sums), after,
        in_specs=[SMEM] + [WHOLE] * 6,
        out_specs=[WHOLE] * 2,
        out_shape=[array, array],
        scratch_shapes=[
            pltpu.VMEM((BLOCKS * BLOCK, 4 * PAIR), F32),
            pltpu.VMEM((PAIR, BLOCKS * BLOCK), F32),
        ],
        cost_estimate=cost(3),
    )


def meet_kernel(info_ref, keep_ref, came_ref, *out_refs):
    for apart in range(QUARTERS):
        quarter = info_ref[PART] ^ apart
        out_refs[apart][0] = keep_ref[quarter, 0] + came_ref[quarter, 0]


def meet_small_kernel(info_ref, keep_ref, came_ref, *out_refs):
    for apart in range(QUARTERS):
        quarter = info_ref[PART] ^ apart
        for step in range(LAYERS):
            source = (info_ref[LAYER] + step) % LAYERS
            out_refs[apart][step] = keep_ref[quarter, source] + came_ref[quarter, source]


def meet(info, keep, came, after=()):
    width = keep.shape[-1]
    if width == PAIR:
        return call_with(
            meet_small_kernel, (info, keep, came), after,
            in_specs=[SMEM, WHOLE, WHOLE],
            out_specs=[WHOLE] * QUARTERS,
            out_shape=[jax.ShapeDtypeStruct((LAYERS, BLOCK, width), BF)] * QUARTERS,
            cost_estimate=cost(2),
        )
    block = lambda: pl.BlockSpec(
        (QUARTERS, 1, BLOCK, width), lambda s, info: (0, (info[LAYER] + s) % LAYERS, 0, 0)
    )

    def run(info_ref, keep_ref, came_ref, *refs):
        meet_kernel(info_ref, keep_ref, came_ref, *refs[len(after) :])

    return pl.pallas_call(
        run,
        grid_spec=pltpu.PrefetchScalarGridSpec(
            num_scalar_prefetch=1,
            grid=(LAYERS,),
            in_specs=[block(), block()] + [IDLE] * len(after),
            out_specs=[pl.BlockSpec((1, BLOCK, width), lambda s, info: (s, 0, 0))] * QUARTERS,
        ),
        out_shape=[jax.ShapeDtypeStruct((LAYERS, BLOCK, width), BF)] * QUARTERS,
        compiler_params=params(),
        cost_estimate=cost(3),
    )(info, keep, came, *after)


def attend_back_kernel(
    grad_ref, wide_ref, inverse_ref, exp_ref, query_t_ref, key_ref, value_t_ref,
    together_ref, sums_ref, score_ref,
):
    rows = grad_ref.shape[0]
    inverse = inverse_ref[...]
    grad = grad_ref[...].astype(F32)
    scaled = grad * inverse
    dots = scaled * wide_ref[...]
    scaled_t = scaled.T.astype(BF)
    value_wide = value_t_ref[...].astype(F32)
    lane = lax.broadcasted_iota(jnp.int32, (rows, PAIR), 1)
    place = lax.broadcasted_iota(jnp.int32, (PAIR, rows), 0)
    block = 128
    dq, dk_t, dv_t = [], [], []
    for half in range(2):
        mine = (lane < HEAD_DIM) if half == 0 else (lane >= HEAD_DIM)
        flag = HEAD_DIM if half == 0 else 0
        offset = jnp.sum(jnp.where(mine, -dots, 0.0), 1, keepdims=True)
        high = offset.astype(BF).astype(F32)
        rest = offset - high
        left = jnp.where(
            mine, scaled, jnp.where(lane == flag, high, jnp.where(lane == flag + 1, rest, 0.0))
        ).astype(BF)
        right = jnp.where((place == flag) | (place == flag + 1), 1.0, value_wide).astype(BF)
        for start in range(0, rows, block):
            grad_probs = dot(left[start : start + block], right, 1, 0)
            weight = exp_ref[half, start : start + block, :].astype(F32)
            score_ref[half, start : start + block, :] = (grad_probs * weight).astype(BF)
        own = slice(half * HEAD_DIM, (half + 1) * HEAD_DIM)
        dv_t.append(dot(scaled_t[own], exp_ref[half], 1, 0))
        dk_t.append(dot(query_t_ref[own, :], score_ref[half], 1, 0))
        dq.append(dot(score_ref[half], key_ref[...], 1, 0))
    factor = HEAD_DIM**-0.5
    dq_low = (jnp.where(lane < HEAD_DIM, dq[0], dq[1]) * factor).astype(BF)
    dk_low = (jnp.concatenate(dk_t, axis=0) * factor).T.astype(BF)
    dv_low = jnp.concatenate(dv_t, axis=0).T.astype(BF)
    together_ref[0] = jnp.concatenate([dq_low, dk_low, dv_low], axis=1)
    query_sum = column_sum(dq_low.astype(F32))
    value_sum = column_sum(dv_low.astype(F32))
    sums_ref[...] = jnp.concatenate([query_sum, value_sum, jnp.zeros((6, PAIR), F32)], axis=0)


def attend_back(grad_context, saved, start, pairs, after=()):
    exps, wide, inverse, query_t, key, value_t = saved
    rows = grad_context.shape[0]
    tall = lambda: pl.BlockSpec((rows, PAIR), lambda p: (0, start + p))
    flat = lambda: pl.BlockSpec((PAIR, rows), lambda p: (start + p, 0))
    return call_with(
        attend_back_kernel,
        (grad_context, wide, inverse, exps, query_t, key, value_t),
        after,
        grid=(pairs,),
        in_specs=[
            tall(), tall(), tall(),
            pl.BlockSpec((2, rows, rows), lambda p: (start + p, 0, 0)),
            flat(), tall(), flat(),
        ],
        out_specs=[
            pl.BlockSpec((1, rows, 3 * PAIR), lambda p: (p, 0, 0)),
            pl.BlockSpec((8, PAIR), lambda p: (0, p)),
        ],
        out_shape=[
            jax.ShapeDtypeStruct((pairs, rows, 3 * PAIR), BF),
            jax.ShapeDtypeStruct((8, pairs * PAIR), F32),
        ],
        scratch_shapes=[pltpu.VMEM((2, rows, rows), BF)],
        cost_estimate=cost(8 * pairs),
    )


def token_kernel(info_ref, grad_ref, together_0_ref, together_1_ref, *refs):
    count = 4
    first_sources, rest_sources = refs[:count], refs[count : count + 2]
    out_ref, first_ref, rest_ref = refs[-3:]

    @pl.when(pl.program_id(0) == 0)
    def _():
        lay_line(info_ref, first_ref, *first_sources)
        lay(info_ref, rest_ref, 3 * PAIR, *rest_sources)

    pieces = [together_1_ref[i] for i in range(together_1_ref.shape[0])]
    total = grad_ref[...] + dot(together_0_ref[0], first_ref[:WIDTH, : 3 * PAIR], 1, 1)
    total += dot(jnp.concatenate(pieces, axis=1), rest_ref[:WIDTH, :], 1, 1)
    out_ref[...] = total.astype(BF)


def token_back(info, grad_first, togethers, first, rest, after):
    rows = grad_first.shape[0]
    tile = 256
    part = pl.BlockSpec((tile, WIDTH), lambda i: (i, 0))
    piece = lambda array: pl.BlockSpec((array.shape[0], tile, 3 * PAIR), lambda i: (0, i, 0))
    return call_with(
        token_kernel, (info, grad_first, *togethers, *first, *rest), after,
        grid=(rows // tile,),
        in_specs=[SMEM, part]
        + [piece(array) for array in togethers]
        + [WHOLE] * (len(first) + len(rest)),
        out_specs=part,
        out_shape=jax.ShapeDtypeStruct((rows, WIDTH), BF),
        scratch_shapes=[
            pltpu.VMEM((BLOCKS * BLOCK, 4 * PAIR), BF),
            pltpu.VMEM((BLOCKS * BLOCK, 12 * PAIR), BF),
        ],
        cost_estimate=cost(7),
    )


def plane_kernel(groups, *refs):
    inputs, outputs = refs[: groups * QUARTERS], refs[groups * QUARTERS :]
    start = 0
    for group in range(groups):
        mine = inputs[group * QUARTERS : (group + 1) * QUARTERS]
        width = mine[0].shape[-1]
        for step in range(LAYERS):
            total = sum(ref[step].astype(F32) for ref in mine)
            outputs[step][:, start : start + width] = total.astype(BF)
        start += width


def plane(groups, after=()):
    width = sum(group[0].shape[-1] for group in groups)
    return call_with(
        functools.partial(plane_kernel, len(groups)),
        tuple(array for group in groups for array in group),
        after,
        in_specs=[WHOLE] * (len(groups) * QUARTERS),
        out_specs=[WHOLE] * LAYERS,
        out_shape=[jax.ShapeDtypeStruct((BLOCK, width), BF)] * LAYERS,
        cost_estimate=cost(2),
    )


def plane_stack_kernel(info_ref, *refs):
    for step in range(LAYERS):
        total = sum(ref[step].astype(F32) for ref in refs[:-1])
        refs[-1][(info_ref[LAYER] + step) % LAYERS] = total.astype(BF)


def plane_stack(info, parts, after=()):
    return call_with(
        plane_stack_kernel, (info, *parts), after,
        in_specs=[SMEM] + [WHOLE] * len(parts),
        out_specs=WHOLE,
        out_shape=jax.ShapeDtypeStruct(parts[0].shape, BF),
        cost_estimate=cost(2),
    )


def line_kernel(counts, *refs):
    inputs, out_ref = refs[:-1], refs[-1]
    start = 0
    for count in counts:
        mine, inputs = inputs[:count], inputs[count:]
        width = mine[0].shape[-1]
        parts = [ref[...] for ref in mine] if count > 1 else [mine[0][i] for i in range(QUARTERS)]
        total = sum(part.astype(F32) for part in parts).astype(BF)
        for copy in range(QUARTERS):
            out_ref[copy, :, start : start + width] = total
        start += width


def line(groups, after=()):
    width = sum(group[0].shape[-1] for group in groups)
    arrays = tuple(array for group in groups for array in group)
    return call_with(
        functools.partial(line_kernel, [len(group) for group in groups]), arrays, after,
        in_specs=[WHOLE] * len(arrays),
        out_specs=WHOLE,
        out_shape=jax.ShapeDtypeStruct((QUARTERS, BLOCK, width), BF),
        cost_estimate=cost(1),
    )


def finish_wide_kernel(info_ref, wide_ref, wo_ref, up_ref, down_ref):
    extra = wo_ref.shape[1] - WIDTH
    blank = jnp.zeros((BLOCK, extra), F32)
    used = HIDDEN_PAD // (QUARTERS * BLOCK)
    owner = 2 * info_ref[LAYER] + info_ref[CORE]
    for quarter in range(QUARTERS):
        lines = slice(quarter * BLOCK, (quarter + 1) * BLOCK)
        down = wide_ref[quarter, :, UP_PART:].astype(F32)
        down_ref[lines, :WIDTH] = jnp.where(owner < used, down, 0.0)
        down_ref[lines, WIDTH:] = blank
    for quarter in range(QUARTERS - 1):
        columns = slice(quarter * UP_PART, (quarter + 1) * UP_PART)
        up_ref[:, columns] = wide_ref[quarter, :, :UP_PART].astype(F32)
    up_ref[:, HIDDEN_PAD:] = jnp.zeros((BLOCK, up_ref.shape[1] - HIDDEN_PAD), F32)
    wo_ref[:, :WIDTH] = wide_ref[QUARTERS - 1, :, :WIDTH].astype(F32)
    wo_ref[:, WIDTH:] = blank


def finish_wide(info, wide, super_width, super_hidden, after=()):
    array = lambda *shape: jax.ShapeDtypeStruct(shape, F32)
    return call_with(
        finish_wide_kernel, (info, wide), after,
        in_specs=[SMEM, WHOLE],
        out_specs=[WHOLE] * 3,
        out_shape=[
            array(BLOCK, super_width), array(BLOCK, super_hidden),
            array(QUARTERS * BLOCK, super_width),
        ],
        cost_estimate=cost(3),
    )


def finish_heads_kernel(heads_ref, *refs):
    three, line_refs, up_line_ref = refs[:3], refs[3:11], refs[11]
    for i, ref in enumerate(three):
        ref[:, :PAIR] = heads_ref[i, :, 3 * PAIR :].astype(F32)
        for pair in range(1, PAIRS):
            part = heads_ref[pair - 1, :, i * PAIR : (i + 1) * PAIR]
            ref[:, pair * PAIR : (pair + 1) * PAIR] = part.astype(F32)
        ref[:, WIDTH:] = jnp.zeros((BLOCK, ref.shape[1] - WIDTH), F32)
    lines = heads_ref[QUARTERS - 1, :, 3 * PAIR :].astype(F32).T
    for i, ref in enumerate(line_refs):
        ref[...] = lines[i]
    up_line_ref[...] = lines[8 : 8 + QUARTERS]


def finish_heads(heads, super_width):
    array = lambda *shape: jax.ShapeDtypeStruct(shape, F32)
    return call_with(
        finish_heads_kernel, (heads,), (),
        in_specs=[WHOLE],
        out_specs=[WHOLE] * 12,
        out_shape=[array(BLOCK, super_width)] * 3
        + [array(BLOCK)] * 8
        + [array(QUARTERS, BLOCK)],
        cost_estimate=cost(2),
    )


SWAP = [(i, i ^ 1) for i in range(BLOCKS)]
STEPS = range(1, LAYERS)
DISTANCES = range(1, QUARTERS)


def twin(part):
    return lax.ppermute(part, "fsdp", SWAP)


def along(part, step):
    pairs = [(i, (i + 2 * step) % BLOCKS) for i in range(BLOCKS)]
    return lax.ppermute(part, "fsdp", pairs)


LINES = [[2 * layer + core for layer in range(LAYERS)] for core in range(2)]


def trade_plane(parts):
    return lax.all_to_all(parts, "dp", 0, 0)


def trade_line(parts):
    return lax.all_to_all(parts, "fsdp", 0, 0, axis_index_groups=LINES)


def copies(part):
    return jnp.broadcast_to(part[None], (QUARTERS,) + part.shape)


def across(part, apart):
    return lax.ppermute(part, "dp", [(i, i ^ apart) for i in range(QUARTERS)])


def drop(saved):
    return (saved[0],) + tuple(saved[2:])


def on_device(
    tokens, lengths, query_weight, key_weight, value_weight, out_weight, up_weight, down_weight,
    query_bias, value_bias, out_bias, up_bias, down_bias, first_gain, first_shift, second_gain,
    second_shift, cotangent,
):
    super_width, super_hidden = query_weight.shape[1], up_weight.shape[1]
    index = lax.axis_index("fsdp").astype(jnp.int32)
    part = lax.axis_index("dp").astype(jnp.int32)
    info = jnp.stack([lengths[0], index % 2, part, index // 2])
    qkv = (query_weight, key_weight, value_weight)
    small = (
        query_bias, value_bias, out_bias, down_bias,
        first_gain, first_shift, second_gain, second_shift, up_bias,
    )
    first_own = pack(pack_first_kernel, info, qkv + small, (BLOCK, 7 * PAIR))
    first_came = [along(first_own, step) for step in STEPS]
    wide_own = pack(
        pack_wide_kernel, info, (up_weight, out_weight), (BLOCK, UP_PART), after=(first_own,)
    )
    first_line, rest_copies = join(first_own, first_came, after=(wide_own,))
    first = (first_own, twin(first_own), first_line, twin(first_line))
    rest_mine = trade_plane(rest_copies)
    down_cut = cut(down_weight, after=(wide_own, *first))
    wide_line = [wide_own] + [along(wide_own, step) for step in STEPS]
    down = lax.all_gather(down_cut, "fsdp", axis=0, tiled=True)
    *saved, vectors, mark = attend(info, tokens, first, 0, 1, after=(down_cut,))
    rest = (rest_mine, twin(rest_mine))
    wide_mine = trade_plane(repeat(wide_line, after=(mark,)))
    *saved, mark = attend(info, tokens, rest, 1, 3, vectors, saved, after=wide_line)
    wide_mine, mark = lax.optimization_barrier((wide_mine, mark))
    wide = (wide_mine, twin(wide_mine))
    *saved, mark = attend(info, tokens, rest, 4, 1, vectors, saved, after=(wide_mine, mark))
    (
        output, grad_first, grad_context, sums, up_sum, down_term, up_keep, up_send
    ) = feed(info, saved[1], tokens, cotangent, wide, down, vectors)
    down_total = lax.psum_scatter(down_term, "fsdp", scatter_dimension=0, tiled=True)
    token_t = turn(tokens, after=(up_keep,))
    up_near = meet(info, up_keep, twin(up_send), after=(token_t,))
    send = lambda near: [near[0]] + [across(near[apart], apart) for apart in DISTANCES]
    pass_on = lambda layers: [layers[0]] + [along(layers[step], step) for step in STEPS]
    up_plane = send(up_near)
    together_1, sums_1 = attend_back(grad_context, drop(saved), 1, 4, after=(up_near[0],))
    head_keep, head_send = head_grad(info, token_t, together_1, after=up_plane[1:])
    down_plane = trade_plane(down_total.reshape(QUARTERS, BLOCK, WIDTH))
    head_near = meet(info, head_keep, twin(head_send))
    up_layers = plane_stack(info, up_plane, after=(head_near[0], down_plane))
    up_line = trade_line(up_layers)
    head_plane = send(head_near)
    together_0, sums_0 = attend_back(grad_context, drop(saved), 0, 1, after=(up_layers,))
    first_keep, first_send = first_grad(
        info, token_t, together_0, sums, up_sum, (sums_0, sums_1),
        after=(up_line, *head_plane[1:]),
    )
    wide_copies = line([[up_line], [down_plane]], after=(first_keep,))
    wide_total = trade_plane(wide_copies)
    first_near = meet(info, first_keep, twin(first_send), after=(wide_copies,))
    first_plane = send(first_near)
    layers = plane([head_plane, first_plane])
    token_grad = token_back(
        info, grad_first, (together_0, together_1), first, rest, (layers[0],)
    )
    head_copies = line([pass_on(layers)], after=(token_grad, wide_total))
    head_total = trade_plane(head_copies)
    wo, up, down = finish_wide(info, wide_total, super_width, super_hidden, after=(head_copies,))
    *results, up_lines = finish_heads(head_total, super_width)
    heads, lines = results[:3], results[3:]
    order = lines[:3] + [up_lines.reshape(-1)] + lines[3:]
    return (output, token_grad, *heads, wo, up, down, *order)


def widen(matrix, row_count, column_count):
    return jnp.pad(matrix, ((0, row_count - matrix.shape[0]), (0, column_count - matrix.shape[1])))


def on_device_elsewhere(
    tokens, lengths, query_weight, key_weight, value_weight, out_weight, up_weight, down_weight,
    query_bias, value_bias, out_bias, up_bias, down_bias, first_gain, first_shift, second_gain,
    second_shift, cotangent,
):
    owned, super_width = query_weight.shape
    super_hidden = up_weight.shape[1]
    info = jnp.stack([lengths[0]] + [jnp.zeros((), jnp.int32)] * 3)
    gather = lambda array: lax.all_gather(array, "fsdp", axis=0, tiled=True)
    qkv = [gather(array) for array in (query_weight, key_weight, value_weight)]
    lines = [
        gather(array)
        for array in (
            query_bias, value_bias, out_bias, down_bias,
            first_gain, first_shift, second_gain, second_shift,
        )
    ]
    up_lines = gather(up_bias).reshape(BLOCKS, QUARTERS, BLOCK).transpose(1, 0, 2)
    lines = jnp.concatenate([jnp.stack(lines), up_lines.reshape(QUARTERS, -1)], axis=0)
    columns = jnp.pad(lines, ((0, PAIR - lines.shape[0]), (0, 0))).T
    first_full = jnp.concatenate([array[:, :PAIR] for array in qkv] + [columns], axis=1)
    places = [slice(pair * PAIR, (pair + 1) * PAIR) for pair in range(1, PAIRS)]
    rest_full = jnp.concatenate([array[:, place] for place in places for array in qkv], axis=1)
    wide_full = jnp.concatenate([gather(up_weight)[:, :HIDDEN_PAD], gather(out_weight)], axis=1)
    down = gather(down_weight)[:, :WIDTH]

    back = [(LAYERS - slot) % LAYERS for slot in range(LAYERS)]

    def pieces(full):
        blocks = full.reshape(LAYERS, 2, BLOCK, QUARTERS, -1).transpose(0, 1, 3, 2, 4)
        blocks = jnp.stack([blocks[layer] for layer in back], axis=2)
        return blocks[0], blocks[1]

    blocks = first_full.reshape(LAYERS, 2, BLOCK, -1)
    blocks = jnp.stack([blocks[layer] for layer in back])
    first = (blocks[0, 0], blocks[0, 1], blocks[1:, 0], blocks[1:, 1])
    rest, wide = pieces(rest_full), pieces(wide_full)
    token_t = turn(tokens)
    *saved, vectors, mark = attend(info, tokens, first, 0, 1)
    *saved, mark = attend(info, tokens, rest, 1, 4, vectors, saved)
    (
        output, grad_first, grad_context, sums, up_sum, down_term, *up_parts
    ) = feed(info, saved[1], tokens, cotangent, wide, down, vectors)
    deep = lax.broadcasted_iota(jnp.int32, (super_hidden, 1), 0)
    down_term = jnp.where(deep < HIDDEN_PAD, down_term, 0.0)
    together_1, sums_1 = attend_back(grad_context, drop(saved), 1, 4)
    together_0, sums_0 = attend_back(grad_context, drop(saved), 0, 1)
    heads = (info, token_t, together_1)
    firsts = (info, token_t, together_0, sums, up_sum, (sums_0, sums_1))

    def both(parts):
        return jnp.stack(parts, axis=2).transpose(1, 2, 3, 0, 4).reshape(super_width, -1)

    def total(array):
        array = lax.psum_scatter(array, "fsdp", scatter_dimension=0, tiled=True)
        return lax.psum(array, "dp").astype(F32)

    wide_total = total(both(up_parts))
    heads_total = total(both(head_grad(*heads))).reshape(owned, PAIRS - 1, 3, PAIR)
    first_total = total(both(first_grad(*firsts)))
    down_total = total(down_term)
    token_grad = token_back(
        info, grad_first, (together_0, together_1), first, rest, ()
    )
    full = lambda matrix: widen(matrix, owned, super_width)
    heads = [
        full(
            jnp.concatenate(
                [first_total[:, i * PAIR : (i + 1) * PAIR], heads_total[:, :, i].reshape(owned, -1)],
                axis=1,
            )
        )
        for i in range(3)
    ]
    lines = gather(first_total[:, 3 * PAIR :]).T
    up_lines = lines[8:12].reshape(QUARTERS, BLOCKS, BLOCK).transpose(1, 0, 2).reshape(-1)
    place = lax.axis_index("fsdp")
    mine = lambda array: lax.dynamic_slice_in_dim(array, place * owned, owned)
    deep = up_bias.shape[0]
    return (
        output, token_grad, *heads,
        full(wide_total[:, HIDDEN_PAD : HIDDEN_PAD + WIDTH]),
        widen(wide_total[:, :HIDDEN_PAD], owned, super_hidden),
        widen(down_total, deep, super_width),
        mine(lines[0]), mine(lines[1]), mine(lines[2]),
        lax.dynamic_slice_in_dim(up_lines, place * deep, deep),
        mine(lines[3]), mine(lines[4]), mine(lines[5]), mine(lines[6]), mine(lines[7]),
    )


def solution(mesh):
    rows = P(("dp", "fsdp"), None)
    held = P("fsdp", None)
    line = P("fsdp")
    near = mesh.shape["dp"] == QUARTERS and mesh.shape["fsdp"] == BLOCKS
    return jax.shard_map(
        on_device if near else on_device_elsewhere,
        mesh=mesh,
        in_specs=(rows, P(("dp", "fsdp"))) + (held,) * 6 + (line,) * 9 + (rows,),
        out_specs=(rows, rows) + (held,) * 6 + (line,) * 9,
        check_vma=False,
    )
```

```python
import functools

import jax
import jax.numpy as jnp
from jax import lax
from jax.experimental import pallas as pl
from jax.experimental.pallas import tpu as pltpu
from jax.sharding import PartitionSpec as P

HEAD_DIM = 64
HIDDEN_SIZE = 2240
WIDTH = 640
EPSILON = 1e-05
MASKED = -1e30
PAIR = 2 * HEAD_DIM
PAIRS = WIDTH // PAIR
BF = jnp.bfloat16
F32 = jnp.float32
VMEM_BYTES = 127 * 2**19
BLOCKS = 8
BLOCK = 96
QUARTERS = 4
LAYERS = BLOCKS // 2
HIDDEN_PAD = 2304
UP_PART = 768
PEAK = 10**9


def dot(left, right, left_dim, right_dim):
    return lax.dot_general(
        left, right, (((left_dim,), (right_dim,)), ((), ())), preferred_element_type=F32
    )


def side(shape, axis, half, own, flag):
    place = lax.broadcasted_iota(jnp.int32, shape, axis)
    mine = (place < HEAD_DIM) if half == 0 else (place >= HEAD_DIM)
    first = place == (HEAD_DIM if half == 0 else 0)
    return jnp.where(mine, own, jnp.where(first, flag, 0.0))


def rows_of(step):
    return pl.ds(pl.multiple_of(step * BLOCK, BLOCK), BLOCK)


def cost(microseconds):
    return pl.CostEstimate(flops=microseconds * PEAK, bytes_accessed=0, transcendentals=0)


def params():
    return pltpu.CompilerParams(vmem_limit_bytes=VMEM_BYTES)


SMEM = pl.BlockSpec(memory_space=pltpu.SMEM)
WHOLE = pl.BlockSpec(memory_space=pltpu.VMEM)
IDLE = pl.BlockSpec(memory_space=pl.ANY)
LENGTH, CORE, PART, LAYER = range(4)


def call_with(kernel, inputs, after, **options):
    specs = options.pop("in_specs") + [IDLE] * len(after)

    def run(*refs):
        kernel(*refs[: len(inputs)], *refs[len(inputs) + len(after) :])

    return pl.pallas_call(run, in_specs=specs, compiler_params=params(), **options)(*inputs, *after)


def pack_first_kernel(info_ref, wq_ref, wk_ref, wv_ref, *refs):
    small_refs, out_ref = refs[:9], refs[9]
    lines = [ref[...].astype(F32).reshape(1, BLOCK) for ref in small_refs[:8]]
    up_line = small_refs[8][...].astype(F32).reshape(1, -1)
    lines += [up_line[:, i * BLOCK : (i + 1) * BLOCK] for i in range(QUARTERS)]
    small = jnp.concatenate(lines + [jnp.zeros((PAIR - 12, BLOCK), F32)], axis=0).T
    place = pl.ds(pl.multiple_of((info_ref[PART] + 1) * PAIR, PAIR), PAIR)
    for i, ref in enumerate((wq_ref, wk_ref, wv_ref)):
        out_ref[:, i * PAIR : (i + 1) * PAIR] = ref[:, :PAIR]
        out_ref[:, (i + 4) * PAIR : (i + 5) * PAIR] = ref[:, place]
    out_ref[:, 3 * PAIR : 4 * PAIR] = small.astype(BF)


def pack_wide_kernel(info_ref, up_ref, wo_ref, out_ref):
    part = info_ref[PART]

    @pl.when(part < QUARTERS - 1)
    def _():
        out_ref[...] = up_ref[:, pl.ds(pl.multiple_of(part * UP_PART, UP_PART), UP_PART)]

    @pl.when(part == QUARTERS - 1)
    def _():
        out_ref[...] = wo_ref[...]


def pack(kernel, info, arrays, shape, after=()):
    return call_with(
        kernel, (info, *arrays), after,
        in_specs=[SMEM] + [WHOLE] * len(arrays),
        out_specs=WHOLE,
        out_shape=jax.ShapeDtypeStruct(shape, BF),
        cost_estimate=cost(2),
    )


def join_kernel(own_ref, *refs):
    came_refs, (line_ref, out_ref) = refs[:-2], refs[-2:]
    width = line_ref.shape[-1]
    for i, ref in enumerate(came_refs):
        line_ref[i] = ref[:, :width]
    for i, ref in enumerate((own_ref, *came_refs)):
        for copy in range(QUARTERS):
            out_ref[copy, i] = ref[:, width:]


def join(own, came, after=()):
    arrays = (own, *came)
    shape = lambda *lead: jax.ShapeDtypeStruct(lead, BF)
    return call_with(
        join_kernel, arrays, after,
        in_specs=[WHOLE] * len(arrays),
        out_specs=[WHOLE] * 2,
        out_shape=[
            shape(len(came), BLOCK, 4 * PAIR), shape(QUARTERS, len(arrays), BLOCK, 3 * PAIR),
        ],
        cost_estimate=cost(2),
    )


def repeat_kernel(*refs):
    for i, ref in enumerate(refs[:-1]):
        for copy in range(QUARTERS):
            refs[-1][copy, i] = ref[...]


def repeat(parts, after=()):
    return call_with(
        repeat_kernel, tuple(parts), after,
        in_specs=[WHOLE] * len(parts),
        out_specs=WHOLE,
        out_shape=jax.ShapeDtypeStruct((QUARTERS, len(parts)) + parts[0].shape, BF),
        cost_estimate=cost(30),
    )


def turn_kernel(source_ref, out_ref):
    out_ref[:WIDTH, :] = source_ref[...].T
    out_ref[WIDTH:, :] = jnp.zeros((BLOCKS * BLOCK - WIDTH, source_ref.shape[0]), BF)


def turn(tokens, after=()):
    return call_with(
        turn_kernel, (tokens,), after,
        in_specs=[WHOLE],
        out_specs=WHOLE,
        out_shape=jax.ShapeDtypeStruct((BLOCKS * BLOCK, tokens.shape[0]), BF),
        cost_estimate=cost(50),
    )


def cut(down, after=()):
    return call_with(
        cut_kernel, (down,), after,
        in_specs=[WHOLE],
        out_specs=WHOLE,
        out_shape=jax.ShapeDtypeStruct((down.shape[0], WIDTH), BF),
        cost_estimate=cost(1),
    )


def cut_kernel(down_ref, out_ref):
    out_ref[...] = down_ref[:, :WIDTH]


def lay_line(info_ref, target, own_ref, twin_ref, came_ref, twins_ref):
    core, layer = info_ref[CORE], info_ref[LAYER]
    width = target.shape[1]
    target[rows_of(2 * layer + core), :] = own_ref[:, :width]
    target[rows_of(2 * layer + 1 - core), :] = twin_ref[:, :width]
    for step in range(1, LAYERS):
        source = (layer + LAYERS - step) % LAYERS
        target[rows_of(2 * source + core), :] = came_ref[step - 1, :, :width]
        target[rows_of(2 * source + 1 - core), :] = twins_ref[step - 1, :, :width]


def lay(info_ref, target, width, mine_ref, other_ref):
    core, layer = info_ref[CORE], info_ref[LAYER]
    for quarter in range(QUARTERS):
        columns = slice(quarter * width, (quarter + 1) * width)
        for slot in range(LAYERS):
            source = (layer + LAYERS - slot) % LAYERS
            target[rows_of(2 * source + core), columns] = mine_ref[quarter, slot]
            target[rows_of(2 * source + 1 - core), columns] = other_ref[quarter, slot]


def attend_kernel(shift, info_ref, token_ref, *refs):
    first = shift is None
    count = 4 if first else 2
    sources, refs = refs[:count], refs[count:]
    if first:
        vectors_ref = refs[7]
        refs = refs[:7] + refs[8:]
    else:
        vectors_ref = refs[0]
        refs = refs[1:]
    (
        exp_ref, context_ref, wide_ref, inverse_ref, query_t_ref, key_ref,
        value_t_ref, mark_ref, weight_ref, held_ref, left_ref,
    ) = refs
    rows = token_ref.shape[0]
    if first:
        lay_line(info_ref, weight_ref, *sources)
        vectors_ref[...] = weight_ref[:, 3 * PAIR :].astype(F32).T[:16]
        bq = vectors_ref[0:1, :PAIR]
        bv = vectors_ref[1:2, :PAIR]
        weights = weight_ref[:WIDTH, : 3 * PAIR]
    else:
        @pl.when(pl.program_id(0) == 0)
        def _():
            lay(info_ref, weight_ref, 3 * PAIR, *sources)

        pair = pl.program_id(0) + shift
        place = pl.ds(pl.multiple_of(pair * PAIR, PAIR), PAIR)
        bq = vectors_ref[0:1, place]
        bv = vectors_ref[1:2, place]
        place = pl.ds(pl.multiple_of((pair - 1) * 3 * PAIR, 3 * PAIR), 3 * PAIR)
        weights = weight_ref[:WIDTH, place]
    product = dot(token_ref[...], weights, 1, 0)
    query = (product[:, :PAIR] + bq).astype(BF)
    key = product[:, PAIR : 2 * PAIR].astype(BF)
    value = (product[:, 2 * PAIR :] + bv).astype(BF)
    key_t = key.T
    query_t_ref[...] = query.T
    key_ref[...] = key
    value_t_ref[...] = value.T
    key_place = lax.broadcasted_iota(jnp.int32, (1, rows), 1)
    bias = jnp.where(key_place < info_ref[LENGTH], 0.0, MASKED)
    scaled = query.astype(F32) * HEAD_DIM**-0.5
    key_wide = key_t.astype(F32)
    value_wide = value.astype(F32)
    block = 128
    step = pl.program_id(0)

    def leave(half, start):
        lines = pl.ds(start, 2 * block)
        return pltpu.make_async_copy(
            held_ref.at[half, lines],
            exp_ref.at[2 * (step + (shift or 0)) + half, lines],
            left_ref.at[half, start // (2 * block)],
        )

    results = []
    for half in range(2):
        left = side((rows, PAIR), 1, half, scaled, 1.0).astype(BF)
        place = lax.broadcasted_iota(jnp.int32, (PAIR, rows), 0)
        right = jnp.where(place == (HEAD_DIM if half == 0 else 0), bias, key_wide).astype(BF)
        for start in range(0, rows, block):
            scores = dot(left[start : start + block], right, 1, 0)
            highest = jnp.max(scores, 1, keepdims=True)
            held_ref[half, start : start + block, :] = jnp.exp(scores - highest).astype(BF)
            if start % (2 * block):
                leave(half, start - block).start()
        values = side((rows, PAIR), 1, half, value_wide, 1.0).astype(BF)
        total = dot(held_ref[half], values, 1, 0)
        flag = HEAD_DIM if half == 0 else 0
        inverse = 1.0 / total[:, flag : flag + 1]
        results.append((total * inverse, inverse))
    low = lax.broadcasted_iota(jnp.int32, (rows, PAIR), 1) < HEAD_DIM
    context = jnp.where(low, results[0][0], results[1][0])
    mark_ref[...] = jnp.zeros_like(mark_ref)
    wide_ref[...] = context
    context_ref[...] = context.astype(BF)
    inverse_ref[...] = jnp.where(low, results[0][1], results[1][1])
    for half in range(2):
        for start in range(0, rows, 2 * block):
            leave(half, start).wait()


def attend(info, tokens, sources, start, pairs, vectors=None, held=(), after=()):
    rows = tokens.shape[0]
    first = vectors is None
    width = (4 if first else 12) * PAIR
    tall = lambda: pl.BlockSpec((rows, PAIR), lambda p: (0, start + p))
    flat = lambda: pl.BlockSpec((PAIR, rows), lambda p: (start + p, 0))
    array = lambda kind: jax.ShapeDtypeStruct((rows, WIDTH), kind)
    turned = jax.ShapeDtypeStruct((WIDTH, rows), BF)
    fixed = lambda *shape: pl.BlockSpec(shape, lambda p: (0, 0))
    table, mark = (16, BLOCKS * BLOCK), (8, 128)
    inputs = (info, tokens, *sources, *(() if first else (vectors,)))
    return call_with(
        functools.partial(attend_kernel, None if first else start),
        inputs,
        (*held, *after),
        grid=(pairs,),
        in_specs=[SMEM, WHOLE] + [WHOLE] * len(sources) + ([] if first else [fixed(*table)]),
        out_specs=[IDLE, tall(), tall(), tall(), flat(), tall(), flat()]
        + ([fixed(*table)] if first else [])
        + [fixed(*mark)],
        out_shape=[
            jax.ShapeDtypeStruct((2 * PAIRS, rows, rows), BF),
            array(BF), array(F32), array(F32), turned, array(BF), turned,
        ]
        + ([jax.ShapeDtypeStruct(table, F32)] if first else [])
        + [jax.ShapeDtypeStruct(mark, F32)],
        input_output_aliases={len(inputs) + i: i for i in range(len(held))},
        scratch_shapes=[
            pltpu.VMEM((BLOCKS * BLOCK, width), BF),
            pltpu.VMEM((2, rows, rows), BF),
            pltpu.SemaphoreType.DMA((2, rows // 256)),
        ],
        cost_estimate=cost(8 * pairs),
    )


def gelu_pair(values):
    t = 1.0 / (1.0 + (0.3275911 * 0.5**0.5) * jnp.abs(values))
    bell = jnp.exp(-0.5 * values * values)
    tail = t * (0.5 * 0.254829592 + t * (0.5 * -0.284496736 + t * (0.5 * 1.421413741 + t * (
        0.5 * -1.453152027 + t * (0.5 * 1.061405429)))))
    tail = tail * bell
    share = jnp.where(values >= 0.0, 1.0 - tail, tail)
    return values * share, share + values * bell * 0.3989422804014327


def row_mean(values):
    return jnp.sum(values, 1, keepdims=True) * (1.0 / WIDTH)


def column_sum(values):
    return jnp.sum(values, 0, keepdims=True)


def row_mean(values):
    return jnp.sum(values, 1, keepdims=True) * (1.0 / WIDTH)


def column_sum(values):
    return jnp.sum(values, 0, keepdims=True)


def up_places():
    for block in range(HIDDEN_PAD // (QUARTERS * BLOCK)):
        for quarter in range(QUARTERS):
            start = (block * QUARTERS + quarter) * BLOCK
            row = slice(8 + quarter, 9 + quarter)
            yield slice(start, start + BLOCK), row, slice(block * BLOCK, (block + 1) * BLOCK)


def feed_kernel(
    info_ref, context_in_ref, token_ref, cotangent_ref, *refs
):
    sources, refs = refs[:2], refs[2:]
    (
        down_ref, vector_ref,
        output_ref, first_ref, grad_context_ref, sums_ref, b1_sum_ref, down_term_ref, keep_ref,
        send_ref, w1_ref, w2_ref, b1_ref, product_ref,
        context_ref, normed_ref, active_ref, hidden_ref, feed_ref, branch_ref, came_ref,
    ) = refs
    step = pl.program_id(0)
    rows = token_ref.shape[0]

    @pl.when(step == 0)
    def _():
        core, layer = info_ref[CORE], info_ref[LAYER]
        copies = []
        for quarter in range(QUARTERS):
            columns = slice(quarter * UP_PART, (quarter + 1) * UP_PART)
            for slot in range(LAYERS):
                source = (layer + LAYERS - slot) % LAYERS
                for twin, ref in enumerate(sources):
                    block = 2 * source + (1 - core if twin else core)
                    target = w1_ref.at[rows_of(block), columns]
                    number = (quarter * LAYERS + slot) * 2 + twin
                    copies.append(
                        pltpu.make_async_copy(ref.at[quarter, slot], target, came_ref.at[number])
                    )
        lower = pltpu.make_async_copy(
            down_ref.at[:HIDDEN_PAD], w2_ref, came_ref.at[2 * QUARTERS * LAYERS]
        )
        copies.append(lower)
        for copy in copies:
            copy.start()
        for copy in copies:
            copy.wait()
        last = slice(HIDDEN_PAD - PAIR, HIDDEN_PAD)
        lane = lax.broadcasted_iota(jnp.int32, (BLOCKS * BLOCK, PAIR), 1)
        kept = lane < HIDDEN_SIZE - (HIDDEN_PAD - PAIR)
        w1_ref[:, last] = jnp.where(kept, w1_ref[:, last].astype(F32), 0.0).astype(BF)
        w2_ref[HIDDEN_SIZE:, :] = jnp.zeros((HIDDEN_PAD - HIDDEN_SIZE, WIDTH), BF)
        for place, row, columns in up_places():
            b1_ref[:, place] = vector_ref[row, columns]
        lane = lax.broadcasted_iota(jnp.int32, (1, HIDDEN_PAD), 1)
        b1_ref[...] = jnp.where(lane < HIDDEN_SIZE, b1_ref[...], 0.0)
        w2_ref[HIDDEN_SIZE:, :] = jnp.zeros((HIDDEN_PAD - HIDDEN_SIZE, WIDTH), BF)

    steps = normed_ref.shape[0] // rows
    down_steps = HIDDEN_PAD // UP_PART

    @pl.when(step < steps)
    def _():
        here = pl.ds(pl.multiple_of(step * rows, rows), rows)
        wo = w1_ref[:WIDTH, HIDDEN_PAD : HIDDEN_PAD + WIDTH]
        w1, w2 = w1_ref[:WIDTH, :HIDDEN_PAD], w2_ref[...]
        place = lax.broadcasted_iota(jnp.int32, (rows, 1), 0) + step * rows
        live = jnp.where(place < info_ref[LENGTH], 1.0, 0.0)
        vector = lambda i: vector_ref[i : i + 1, :WIDTH]
        out_add, down_add = vector(2), vector(3)
        gain_one, shift_one, gain_two, shift_two = vector(4), vector(5), vector(6), vector(7)
        context = context_in_ref[...]
        context_ref[here, :] = context
        first_sum = token_ref[...].astype(F32) + dot(context, wo, 1, 0) + out_add
        center = first_sum - row_mean(first_sum)
        rate_one = lax.rsqrt(row_mean(center * center) + EPSILON)
        unit_one = center * rate_one
        normed = (unit_one * gain_one + shift_one).astype(BF)
        normed_ref[here, :] = normed
        pre = dot(normed, w1, 1, 0) + b1_ref[...]
        active_full, slope = gelu_pair(pre)
        active = active_full.astype(BF)
        active_ref[here, :] = active
        second_sum = normed.astype(F32) + dot(active, w2, 1, 0) + down_add
        center = second_sum - row_mean(second_sum)
        rate_two = lax.rsqrt(row_mean(center * center) + EPSILON)
        unit_two = center * rate_two
        output_ref[...] = ((unit_two * gain_two + shift_two) * live).astype(BF)
        cotangent = cotangent_ref[...].astype(F32) * live
        inner = cotangent * gain_two
        grad_second = rate_two * (inner - row_mean(inner) - unit_two * row_mean(inner * unit_two))
        grad_feed = grad_second.astype(BF)
        feed_ref[here, :] = grad_feed
        grad_hidden = (dot(grad_feed, w2, 1, 1) * slope).astype(BF)
        hidden_ref[here, :] = grad_hidden
        grad_normed = grad_second + dot(grad_hidden, w1, 1, 1)
        inner = grad_normed * gain_one
        grad_first = rate_one * (inner - row_mean(inner) - unit_one * row_mean(inner * unit_one))
        first_ref[...] = grad_first
        grad_branch = grad_first.astype(BF)
        branch_ref[here, :] = grad_branch
        grad_context_ref[...] = dot(grad_branch, wo, 1, 1).astype(BF)
        sums = jnp.concatenate(
            [
                column_sum(grad_branch.astype(F32)),
                column_sum(grad_feed.astype(F32)),
                column_sum(grad_normed * unit_one),
                column_sum(grad_normed),
                column_sum(cotangent * unit_two),
                column_sum(cotangent),
                jnp.zeros((2, WIDTH), F32),
            ],
            axis=0,
        )
        b1_sum = column_sum(grad_hidden.astype(F32))

        @pl.when(step == 0)
        def _():
            sums_ref[...] = sums
            b1_sum_ref[...] = b1_sum

        @pl.when(step > 0)
        def _():
            sums_ref[...] += sums
            b1_sum_ref[...] += b1_sum

    @pl.when((step >= steps) & (step < steps + down_steps))
    def _():
        place = pl.ds(pl.multiple_of((step - steps) * UP_PART, UP_PART), UP_PART)
        down_term_ref[...] = dot(active_ref[:, place], feed_ref[...], 0, 0).astype(BF)

    @pl.when(step >= steps + down_steps)
    def _():
        part = step - steps - down_steps

        @pl.when(part == 0)
        def _():
            product_ref[WIDTH:, :] = jnp.zeros((BLOCKS * BLOCK - WIDTH, UP_PART), F32)

        @pl.when(part < QUARTERS - 1)
        def _():
            place = pl.ds(pl.multiple_of(part * UP_PART, UP_PART), UP_PART)
            product_ref[:WIDTH, :] = dot(normed_ref[...], hidden_ref[:, place], 0, 0)

        @pl.when(part == QUARTERS - 1)
        def _():
            product_ref[:WIDTH, :WIDTH] = dot(context_ref[...], branch_ref[...], 0, 0)

        deal(info_ref, product_ref, keep_ref, send_ref)


def feed(info, context, tokens, cotangent, wide, down, vectors, after=()):
    rows = tokens.shape[0]
    tile = rows // 4
    steps = rows // tile
    down_steps = HIDDEN_PAD // UP_PART
    part = lambda width: pl.BlockSpec((tile, width), lambda i: (jnp.minimum(i, steps - 1), 0))
    whole = lambda *shape: pl.BlockSpec(shape, lambda i: (0, 0))
    array = lambda width, kind: jax.ShapeDtypeStruct((rows, width), kind)
    held = lambda width: pltpu.VMEM((rows, width), BF)
    place = lambda: pl.BlockSpec(
        (1, LAYERS, BLOCK, UP_PART),
        lambda i: (jnp.clip(i - steps - down_steps, 0, QUARTERS - 1), 0, 0, 0),
    )
    shared = jax.ShapeDtypeStruct((QUARTERS, LAYERS, BLOCK, UP_PART), BF)
    return call_with(
        feed_kernel, (info, context, tokens, cotangent, *wide, down, vectors), after,
        grid=(steps + down_steps + QUARTERS,),
        in_specs=[SMEM]
        + [part(WIDTH), part(WIDTH), part(WIDTH)]
        + [IDLE] * (len(wide) + 1)
        + [whole(*vectors.shape)],
        out_specs=[
            part(WIDTH), part(WIDTH), part(WIDTH), whole(8, WIDTH), whole(1, HIDDEN_PAD),
            pl.BlockSpec((UP_PART, WIDTH), lambda i: (jnp.clip(i - steps, 0, down_steps - 1), 0)),
            place(), place(),
        ],
        out_shape=[
            array(WIDTH, BF), array(WIDTH, F32), array(WIDTH, BF),
            jax.ShapeDtypeStruct((8, WIDTH), F32),
            jax.ShapeDtypeStruct((1, HIDDEN_PAD), F32),
            jax.ShapeDtypeStruct((down.shape[0], WIDTH), BF),
            shared, shared,
        ],
        scratch_shapes=[
            pltpu.VMEM((BLOCKS * BLOCK, QUARTERS * UP_PART), BF),
            pltpu.VMEM((HIDDEN_PAD, WIDTH), BF),
            pltpu.VMEM((1, HIDDEN_PAD), F32),
            pltpu.VMEM((BLOCKS * BLOCK, UP_PART), F32),
            held(WIDTH), held(WIDTH), held(HIDDEN_PAD), held(HIDDEN_PAD), held(WIDTH), held(WIDTH),
            pltpu.SemaphoreType.DMA((2 * QUARTERS * LAYERS + 1,)),
        ],
        cost_estimate=cost(50),
    )


def deal(info_ref, product_ref, keep_ref, send_ref):
    core = info_ref[CORE]
    for layer in range(LAYERS):
        keep_ref[0, layer] = product_ref[rows_of(2 * layer + core), :].astype(BF)
        send_ref[0, layer] = product_ref[rows_of(2 * layer + 1 - core), :].astype(BF)


def head_grad_kernel(
    info_ref, token_t_ref, together_ref, first_ref, sums_ref, up_sum_ref, pair_ref,
    keep_ref, send_ref, product_ref, table_ref,
):
    step = pl.program_id(0)

    @pl.when(step < QUARTERS - 1)
    def _():
        part = first_ref[0, :, pl.ds(pl.multiple_of(step * PAIR, PAIR), PAIR)]
        both = jnp.concatenate([together_ref[0], part], axis=1)
        product_ref[...] = dot(token_t_ref[...], both, 1, 0)

    @pl.when(step == QUARTERS - 1)
    def _():
        product_ref[:, : 3 * PAIR] = dot(token_t_ref[...], together_ref[0], 1, 0)
        table_ref[...] = jnp.zeros_like(table_ref)
        table_ref[0:2, :WIDTH] = pair_ref[0:2, :]
        table_ref[2:8, :WIDTH] = sums_ref[0:6, :]
        for place, row, columns in up_places():
            table_ref[row, columns] = up_sum_ref[:, place]
        product_ref[:, 3 * PAIR :] = table_ref[...].T

    deal(info_ref, product_ref, keep_ref, send_ref)


def head_grad(info, token_t, together, sums, up_sum, pair_sums, after=()):
    rows = token_t.shape[1]
    place = lambda: pl.BlockSpec((1, LAYERS, BLOCK, 4 * PAIR), lambda d: (d, 0, 0, 0))
    array = jax.ShapeDtypeStruct((QUARTERS, LAYERS, BLOCK, 4 * PAIR), BF)
    return call_with(
        head_grad_kernel, (info, token_t, together, together, sums, up_sum, pair_sums), after,
        grid=(QUARTERS,),
        in_specs=[
            SMEM, WHOLE,
            pl.BlockSpec((1, rows, 3 * PAIR), lambda d: (d + 1, 0, 0)),
            pl.BlockSpec((1, rows, 3 * PAIR), lambda d: (0, 0, 0)),
            WHOLE, WHOLE, WHOLE,
        ],
        out_specs=[place(), place()],
        out_shape=[array, array],
        scratch_shapes=[
            pltpu.VMEM((BLOCKS * BLOCK, 4 * PAIR), F32),
            pltpu.VMEM((PAIR, BLOCKS * BLOCK), F32),
        ],
        cost_estimate=cost(8),
    )


def meet_kernel(info_ref, keep_ref, came_ref, *out_refs):
    for apart in range(QUARTERS):
        quarter = info_ref[PART] ^ apart
        out_refs[apart][0] = keep_ref[quarter, 0] + came_ref[quarter, 0]


def meet(info, keep, came, after=()):
    width = keep.shape[-1]
    block = lambda: pl.BlockSpec(
        (QUARTERS, 1, BLOCK, width), lambda s, info: (0, (info[LAYER] + s) % LAYERS, 0, 0)
    )

    def run(info_ref, keep_ref, came_ref, *refs):
        meet_kernel(info_ref, keep_ref, came_ref, *refs[len(after) :])

    return pl.pallas_call(
        run,
        grid_spec=pltpu.PrefetchScalarGridSpec(
            num_scalar_prefetch=1,
            grid=(LAYERS,),
            in_specs=[block(), block()] + [IDLE] * len(after),
            out_specs=[pl.BlockSpec((1, BLOCK, width), lambda s, info: (s, 0, 0))] * QUARTERS,
        ),
        out_shape=[jax.ShapeDtypeStruct((LAYERS, BLOCK, width), BF)] * QUARTERS,
        compiler_params=params(),
        cost_estimate=cost(3),
    )(info, keep, came, *after)


def attend_back_kernel(
    grad_ref, wide_ref, inverse_ref, exp_ref, query_t_ref, key_ref, value_t_ref,
    together_ref, sums_ref, score_ref,
):
    rows = grad_ref.shape[0]
    inverse = inverse_ref[...]
    grad = grad_ref[...].astype(F32)
    scaled = grad * inverse
    dots = scaled * wide_ref[...]
    scaled_t = scaled.T.astype(BF)
    value_wide = value_t_ref[...].astype(F32)
    lane = lax.broadcasted_iota(jnp.int32, (rows, PAIR), 1)
    place = lax.broadcasted_iota(jnp.int32, (PAIR, rows), 0)
    block = 128
    dq, dk_t, dv_t = [], [], []
    for half in range(2):
        mine = (lane < HEAD_DIM) if half == 0 else (lane >= HEAD_DIM)
        flag = HEAD_DIM if half == 0 else 0
        offset = jnp.sum(jnp.where(mine, -dots, 0.0), 1, keepdims=True)
        high = offset.astype(BF).astype(F32)
        rest = offset - high
        left = jnp.where(
            mine, scaled, jnp.where(lane == flag, high, jnp.where(lane == flag + 1, rest, 0.0))
        ).astype(BF)
        right = jnp.where((place == flag) | (place == flag + 1), 1.0, value_wide).astype(BF)
        for start in range(0, rows, block):
            grad_probs = dot(left[start : start + block], right, 1, 0)
            weight = exp_ref[half, start : start + block, :].astype(F32)
            score_ref[half, start : start + block, :] = (grad_probs * weight).astype(BF)
        own = slice(half * HEAD_DIM, (half + 1) * HEAD_DIM)
        dv_t.append(dot(scaled_t[own], exp_ref[half], 1, 0))
        dk_t.append(dot(query_t_ref[own, :], score_ref[half], 1, 0))
        dq.append(dot(score_ref[half], key_ref[...], 1, 0))
    factor = HEAD_DIM**-0.5
    dq_low = (jnp.where(lane < HEAD_DIM, dq[0], dq[1]) * factor).astype(BF)
    dk_low = (jnp.concatenate(dk_t, axis=0) * factor).T.astype(BF)
    dv_low = jnp.concatenate(dv_t, axis=0).T.astype(BF)
    together_ref[0] = jnp.concatenate([dq_low, dk_low, dv_low], axis=1)
    query_sum = column_sum(dq_low.astype(F32))
    value_sum = column_sum(dv_low.astype(F32))
    sums_ref[...] = jnp.concatenate([query_sum, value_sum, jnp.zeros((6, PAIR), F32)], axis=0)


def attend_back(grad_context, saved, start, pairs, after=()):
    exps, wide, inverse, query_t, key, value_t = saved
    rows = grad_context.shape[0]
    tall = lambda: pl.BlockSpec((rows, PAIR), lambda p: (0, start + p))
    flat = lambda: pl.BlockSpec((PAIR, rows), lambda p: (start + p, 0))
    return call_with(
        attend_back_kernel,
        (grad_context, wide, inverse, exps, query_t, key, value_t),
        after,
        grid=(pairs,),
        in_specs=[
            tall(), tall(), tall(),
            pl.BlockSpec((2, rows, rows), lambda p: (start + p, 0, 0)),
            flat(), tall(), flat(),
        ],
        out_specs=[
            pl.BlockSpec((1, rows, 3 * PAIR), lambda p: (p, 0, 0)),
            pl.BlockSpec((8, PAIR), lambda p: (0, p)),
        ],
        out_shape=[
            jax.ShapeDtypeStruct((pairs, rows, 3 * PAIR), BF),
            jax.ShapeDtypeStruct((8, pairs * PAIR), F32),
        ],
        scratch_shapes=[pltpu.VMEM((2, rows, rows), BF)],
        cost_estimate=cost(8 * pairs),
    )


def token_kernel(info_ref, grad_ref, together_ref, *refs):
    count = 4
    first_sources, rest_sources = refs[:count], refs[count : count + 2]
    out_ref, first_ref, rest_ref = refs[-3:]

    @pl.when(pl.program_id(0) == 0)
    def _():
        lay_line(info_ref, first_ref, *first_sources)
        lay(info_ref, rest_ref, 3 * PAIR, *rest_sources)

    pieces = [together_ref[i] for i in range(1, PAIRS)]
    total = grad_ref[...] + dot(together_ref[0], first_ref[:WIDTH, : 3 * PAIR], 1, 1)
    total += dot(jnp.concatenate(pieces, axis=1), rest_ref[:WIDTH, :], 1, 1)
    out_ref[...] = total.astype(BF)


def token_back(info, grad_first, together, first, rest, after):
    rows = grad_first.shape[0]
    tile = 256
    part = pl.BlockSpec((tile, WIDTH), lambda i: (i, 0))
    piece = pl.BlockSpec((PAIRS, tile, 3 * PAIR), lambda i: (0, i, 0))
    return call_with(
        token_kernel, (info, grad_first, together, *first, *rest), after,
        grid=(rows // tile,),
        in_specs=[SMEM, part, piece]
        + [WHOLE] * (len(first) + len(rest)),
        out_specs=part,
        out_shape=jax.ShapeDtypeStruct((rows, WIDTH), BF),
        scratch_shapes=[
            pltpu.VMEM((BLOCKS * BLOCK, 4 * PAIR), BF),
            pltpu.VMEM((BLOCKS * BLOCK, 12 * PAIR), BF),
        ],
        cost_estimate=cost(7),
    )


def plane_kernel(groups, *refs):
    inputs, outputs = refs[: groups * QUARTERS], refs[groups * QUARTERS :]
    start = 0
    for group in range(groups):
        mine = inputs[group * QUARTERS : (group + 1) * QUARTERS]
        width = mine[0].shape[-1]
        for step in range(LAYERS):
            total = sum(ref[step].astype(F32) for ref in mine)
            outputs[step][:, start : start + width] = total.astype(BF)
        start += width


def plane(groups, after=()):
    width = sum(group[0].shape[-1] for group in groups)
    return call_with(
        functools.partial(plane_kernel, len(groups)),
        tuple(array for group in groups for array in group),
        after,
        in_specs=[WHOLE] * (len(groups) * QUARTERS),
        out_specs=[WHOLE] * LAYERS,
        out_shape=[jax.ShapeDtypeStruct((BLOCK, width), BF)] * LAYERS,
        cost_estimate=cost(2),
    )


def plane_stack_kernel(info_ref, *refs):
    for step in range(LAYERS):
        total = sum(ref[step].astype(F32) for ref in refs[:-1])
        refs[-1][(info_ref[LAYER] + step) % LAYERS] = total.astype(BF)


def plane_stack(info, parts, after=()):
    return call_with(
        plane_stack_kernel, (info, *parts), after,
        in_specs=[SMEM] + [WHOLE] * len(parts),
        out_specs=WHOLE,
        out_shape=jax.ShapeDtypeStruct(parts[0].shape, BF),
        cost_estimate=cost(2),
    )


def line_kernel(counts, *refs):
    inputs, out_ref = refs[:-1], refs[-1]
    start = 0
    for count in counts:
        mine, inputs = inputs[:count], inputs[count:]
        width = mine[0].shape[-1]
        parts = [ref[...] for ref in mine] if count > 1 else [mine[0][i] for i in range(QUARTERS)]
        total = sum(part.astype(F32) for part in parts).astype(BF)
        for copy in range(out_ref.shape[0]):
            out_ref[copy, :, start : start + width] = total
        start += width


def line(groups, copies=QUARTERS, after=()):
    width = sum(group[0].shape[-1] for group in groups)
    arrays = tuple(array for group in groups for array in group)
    return call_with(
        functools.partial(line_kernel, [len(group) for group in groups]), arrays, after,
        in_specs=[WHOLE] * len(arrays),
        out_specs=WHOLE,
        out_shape=jax.ShapeDtypeStruct((copies, BLOCK, width), BF),
        cost_estimate=cost(1),
    )


def finish_wide_kernel(info_ref, wide_ref, wo_ref, up_ref, down_ref):
    extra = wo_ref.shape[1] - WIDTH
    blank = jnp.zeros((BLOCK, extra), F32)
    used = HIDDEN_PAD // (QUARTERS * BLOCK)
    owner = 2 * info_ref[LAYER] + info_ref[CORE]
    for quarter in range(QUARTERS):
        lines = slice(quarter * BLOCK, (quarter + 1) * BLOCK)
        down = wide_ref[quarter, :, UP_PART:].astype(F32)
        down_ref[lines, :WIDTH] = jnp.where(owner < used, down, 0.0)
        down_ref[lines, WIDTH:] = blank
    for quarter in range(QUARTERS - 1):
        columns = slice(quarter * UP_PART, (quarter + 1) * UP_PART)
        up_ref[:, columns] = wide_ref[quarter, :, :UP_PART].astype(F32)
    up_ref[:, HIDDEN_PAD:] = jnp.zeros((BLOCK, up_ref.shape[1] - HIDDEN_PAD), F32)
    wo_ref[:, :WIDTH] = wide_ref[QUARTERS - 1, :, :WIDTH].astype(F32)
    wo_ref[:, WIDTH:] = blank


def finish_wide(info, wide, super_width, super_hidden, after=()):
    array = lambda *shape: jax.ShapeDtypeStruct(shape, F32)
    return call_with(
        finish_wide_kernel, (info, wide), after,
        in_specs=[SMEM, WHOLE],
        out_specs=[WHOLE] * 3,
        out_shape=[
            array(BLOCK, super_width), array(BLOCK, super_hidden),
            array(QUARTERS * BLOCK, super_width),
        ],
        cost_estimate=cost(3),
    )


def finish_heads_kernel(info_ref, *refs):
    parts, three, line_refs = refs[:QUARTERS], refs[4:7], refs[7:15]
    up_line_ref, heads_ref = refs[15:]
    for apart, ref in enumerate(parts):
        heads_ref[info_ref[PART] ^ apart] = ref[...].astype(F32)
    for i, ref in enumerate(three):
        ref[:, :PAIR] = heads_ref[i, :, 3 * PAIR :]
        for pair in range(1, PAIRS):
            part = heads_ref[pair - 1, :, i * PAIR : (i + 1) * PAIR]
            ref[:, pair * PAIR : (pair + 1) * PAIR] = part
        ref[:, WIDTH:] = jnp.zeros((BLOCK, ref.shape[1] - WIDTH), F32)
    lines = heads_ref[QUARTERS - 1, :, 3 * PAIR :].T
    for i, ref in enumerate(line_refs):
        ref[...] = lines[i]
    for i in range(QUARTERS):
        up_line_ref[i * BLOCK : (i + 1) * BLOCK] = lines[8 + i]


def finish_heads(info, parts, super_width, after=()):
    array = lambda *shape: jax.ShapeDtypeStruct(shape, F32)
    return call_with(
        finish_heads_kernel, (info, *parts), after,
        in_specs=[SMEM] + [WHOLE] * QUARTERS,
        out_specs=[WHOLE] * 12,
        out_shape=[array(BLOCK, super_width)] * 3
        + [array(BLOCK)] * 8
        + [array(QUARTERS * BLOCK)],
        scratch_shapes=[pltpu.VMEM((QUARTERS, BLOCK, 4 * PAIR), F32)],
        cost_estimate=cost(2),
    )


SWAP = [(i, i ^ 1) for i in range(BLOCKS)]
STEPS = range(1, LAYERS)
DISTANCES = range(1, QUARTERS)


def twin(part):
    return lax.ppermute(part, "fsdp", SWAP)


def along(part, step):
    pairs = [(i, (i + 2 * step) % BLOCKS) for i in range(BLOCKS)]
    return lax.ppermute(part, "fsdp", pairs)


LINES = [[2 * layer + core for layer in range(LAYERS)] for core in range(2)]


def trade_plane(parts):
    return lax.all_to_all(parts, "dp", 0, 0)


def trade_line(parts):
    return lax.all_to_all(parts, "fsdp", 0, 0, axis_index_groups=LINES)


def copies(part):
    return jnp.broadcast_to(part[None], (QUARTERS,) + part.shape)


def across(part, apart):
    return lax.ppermute(part, "dp", [(i, i ^ apart) for i in range(QUARTERS)])


def drop(saved):
    return (saved[0],) + tuple(saved[2:])


def on_device(
    tokens, lengths, query_weight, key_weight, value_weight, out_weight, up_weight, down_weight,
    query_bias, value_bias, out_bias, up_bias, down_bias, first_gain, first_shift, second_gain,
    second_shift, cotangent,
):
    super_width, super_hidden = query_weight.shape[1], up_weight.shape[1]
    index = lax.axis_index("fsdp").astype(jnp.int32)
    part = lax.axis_index("dp").astype(jnp.int32)
    info = jnp.stack([lengths[0], index % 2, part, index // 2])
    qkv = (query_weight, key_weight, value_weight)
    small = (
        query_bias, value_bias, out_bias, down_bias,
        first_gain, first_shift, second_gain, second_shift, up_bias,
    )
    first_own = pack(pack_first_kernel, info, qkv + small, (BLOCK, 7 * PAIR))
    first_came = [along(first_own, step) for step in STEPS]
    wide_own = pack(
        pack_wide_kernel, info, (up_weight, out_weight), (BLOCK, UP_PART), after=(first_own,)
    )
    first_line, rest_copies = join(first_own, first_came, after=(wide_own,))
    first = (first_own, twin(first_own), first_line, twin(first_line))
    rest_mine = trade_plane(rest_copies)
    down_cut = cut(down_weight, after=(wide_own, *first))
    wide_line = [wide_own] + [along(wide_own, step) for step in STEPS]
    down = lax.all_gather(down_cut, "fsdp", axis=0, tiled=True)
    *saved, vectors, mark = attend(info, tokens, first, 0, 1, after=(down_cut,))
    rest = (rest_mine, twin(rest_mine))
    wide_mine = trade_plane(repeat(wide_line, after=(mark,)))
    *saved, mark = attend(info, tokens, rest, 1, 3, vectors, saved, after=wide_line)
    wide_mine, mark = lax.optimization_barrier((wide_mine, mark))
    wide = (wide_mine, twin(wide_mine))
    *saved, mark = attend(info, tokens, rest, 4, 1, vectors, saved, after=(wide_mine, mark))
    (
        output, grad_first, grad_context, sums, up_sum, down_term, up_keep, up_send
    ) = feed(info, saved[1], tokens, cotangent, wide, down, vectors)
    down_total = lax.psum_scatter(down_term, "fsdp", scatter_dimension=0, tiled=True)
    token_t = turn(tokens, after=(up_keep,))
    up_near = meet(info, up_keep, twin(up_send), after=(token_t,))
    send = lambda near: [near[0]] + [across(near[apart], apart) for apart in DISTANCES]
    pass_on = lambda layers: [layers[0]] + [along(layers[step], step) for step in STEPS]
    up_plane = send(up_near)
    together, pair_sums = attend_back(grad_context, drop(saved), 0, PAIRS, after=(up_near[0],))
    head_keep, head_send = head_grad(
        info, token_t, together, sums, up_sum, pair_sums, after=up_plane[1:]
    )
    down_plane = trade_plane(down_total.reshape(QUARTERS, BLOCK, WIDTH))
    head_near = meet(info, head_keep, twin(head_send))
    head_plane = send(head_near)
    up_layers = plane_stack(info, up_plane, after=(head_near[0], down_plane))
    up_line = trade_line(up_layers)
    token_grad = token_back(info, grad_first, together, first, rest, (up_layers,))
    wide_copies = line([[up_line], [down_plane]], after=(token_grad,))
    wide_total = trade_plane(wide_copies)
    layers = plane([head_plane], after=(wide_copies,))
    head_total = line([pass_on(layers)], 1).reshape(BLOCK, 4 * PAIR)
    head_parts = send([head_total] * QUARTERS)
    wo, up, down = finish_wide(info, wide_total, super_width, super_hidden, after=(head_total,))
    *results, up_line = finish_heads(info, head_parts, super_width, after=(wo,))
    heads, lines = results[:3], results[3:]
    order = lines[:3] + [up_line] + lines[3:]
    return (output, token_grad, *heads, wo, up, down, *order)


def widen(matrix, row_count, column_count):
    return jnp.pad(matrix, ((0, row_count - matrix.shape[0]), (0, column_count - matrix.shape[1])))


def on_device_elsewhere(
    tokens, lengths, query_weight, key_weight, value_weight, out_weight, up_weight, down_weight,
    query_bias, value_bias, out_bias, up_bias, down_bias, first_gain, first_shift, second_gain,
    second_shift, cotangent,
):
    owned, super_width = query_weight.shape
    super_hidden = up_weight.shape[1]
    info = jnp.stack([lengths[0]] + [jnp.zeros((), jnp.int32)] * 3)
    gather = lambda array: lax.all_gather(array, "fsdp", axis=0, tiled=True)
    qkv = [gather(array) for array in (query_weight, key_weight, value_weight)]
    lines = [
        gather(array)
        for array in (
            query_bias, value_bias, out_bias, down_bias,
            first_gain, first_shift, second_gain, second_shift,
        )
    ]
    up_lines = gather(up_bias).reshape(BLOCKS, QUARTERS, BLOCK).transpose(1, 0, 2)
    lines = jnp.concatenate([jnp.stack(lines), up_lines.reshape(QUARTERS, -1)], axis=0)
    columns = jnp.pad(lines, ((0, PAIR - lines.shape[0]), (0, 0))).T
    first_full = jnp.concatenate([array[:, :PAIR] for array in qkv] + [columns], axis=1)
    places = [slice(pair * PAIR, (pair + 1) * PAIR) for pair in range(1, PAIRS)]
    rest_full = jnp.concatenate([array[:, place] for place in places for array in qkv], axis=1)
    wide_full = jnp.concatenate([gather(up_weight)[:, :HIDDEN_PAD], gather(out_weight)], axis=1)
    down = gather(down_weight)[:, :WIDTH]

    back = [(LAYERS - slot) % LAYERS for slot in range(LAYERS)]

    def pieces(full):
        blocks = full.reshape(LAYERS, 2, BLOCK, QUARTERS, -1).transpose(0, 1, 3, 2, 4)
        blocks = jnp.stack([blocks[layer] for layer in back], axis=2)
        return blocks[0], blocks[1]

    blocks = first_full.reshape(LAYERS, 2, BLOCK, -1)
    blocks = jnp.stack([blocks[layer] for layer in back])
    first = (blocks[0, 0], blocks[0, 1], blocks[1:, 0], blocks[1:, 1])
    rest, wide = pieces(rest_full), pieces(wide_full)
    token_t = turn(tokens)
    *saved, vectors, mark = attend(info, tokens, first, 0, 1)
    *saved, mark = attend(info, tokens, rest, 1, 4, vectors, saved)
    (
        output, grad_first, grad_context, sums, up_sum, down_term, *up_parts
    ) = feed(info, saved[1], tokens, cotangent, wide, down, vectors)
    deep = lax.broadcasted_iota(jnp.int32, (super_hidden, 1), 0)
    down_term = jnp.where(deep < HIDDEN_PAD, down_term, 0.0)
    together, pair_sums = attend_back(grad_context, drop(saved), 0, PAIRS)

    def both(parts):
        return jnp.stack(parts, axis=2).transpose(1, 2, 3, 0, 4).reshape(super_width, -1)

    def total(array):
        array = lax.psum_scatter(array, "fsdp", scatter_dimension=0, tiled=True)
        return lax.psum(array, "dp").astype(F32)

    wide_total = total(both(up_parts))
    heads_total = total(both(head_grad(info, token_t, together, sums, up_sum, pair_sums)))
    heads_total = heads_total.reshape(owned, QUARTERS, 4 * PAIR)
    first_total = heads_total[:, :, 3 * PAIR :].reshape(owned, 4 * PAIR)
    heads_total = heads_total[:, :, : 3 * PAIR].reshape(owned, PAIRS - 1, 3, PAIR)
    down_total = total(down_term)
    token_grad = token_back(
        info, grad_first, together, first, rest, ()
    )
    full = lambda matrix: widen(matrix, owned, super_width)
    heads = [
        full(
            jnp.concatenate(
                [first_total[:, i * PAIR : (i + 1) * PAIR], heads_total[:, :, i].reshape(owned, -1)],
                axis=1,
            )
        )
        for i in range(3)
    ]
    lines = gather(first_total[:, 3 * PAIR :]).T
    up_lines = lines[8:12].reshape(QUARTERS, BLOCKS, BLOCK).transpose(1, 0, 2).reshape(-1)
    place = lax.axis_index("fsdp")
    mine = lambda array: lax.dynamic_slice_in_dim(array, place * owned, owned)
    deep = up_bias.shape[0]
    return (
        output, token_grad, *heads,
        full(wide_total[:, HIDDEN_PAD : HIDDEN_PAD + WIDTH]),
        widen(wide_total[:, :HIDDEN_PAD], owned, super_hidden),
        widen(down_total, deep, super_width),
        mine(lines[0]), mine(lines[1]), mine(lines[2]),
        lax.dynamic_slice_in_dim(up_lines, place * deep, deep),
        mine(lines[3]), mine(lines[4]), mine(lines[5]), mine(lines[6]), mine(lines[7]),
    )


def solution(mesh):
    rows = P(("dp", "fsdp"), None)
    held = P("fsdp", None)
    line = P("fsdp")
    near = mesh.shape["dp"] == QUARTERS and mesh.shape["fsdp"] == BLOCKS
    return jax.shard_map(
        on_device if near else on_device_elsewhere,
        mesh=mesh,
        in_specs=(rows, P(("dp", "fsdp"))) + (held,) * 6 + (line,) * 9 + (rows,),
        out_specs=(rows, rows) + (held,) * 6 + (line,) * 9,
        check_vma=False,
    )
```

```python
import functools

import jax
import jax.numpy as jnp
from jax import lax
from jax.experimental import pallas as pl
from jax.experimental.pallas import tpu as pltpu
from jax.sharding import PartitionSpec as P

HEAD_DIM = 64
HIDDEN_SIZE = 2240
WIDTH = 640
EPSILON = 1e-05
MASKED = -1e30
PAIR = 2 * HEAD_DIM
PAIRS = WIDTH // PAIR
BF = jnp.bfloat16
F32 = jnp.float32
VMEM_BYTES = 127 * 2**19
BLOCKS = 8
BLOCK = 96
QUARTERS = 4
LAYERS = BLOCKS // 2
HIDDEN_PAD = 2304
UP_PART = 768
PEAK = 10**9


def dot(left, right, left_dim, right_dim):
    return lax.dot_general(
        left, right, (((left_dim,), (right_dim,)), ((), ())), preferred_element_type=F32
    )


def side(shape, axis, half, own, flag):
    place = lax.broadcasted_iota(jnp.int32, shape, axis)
    mine = (place < HEAD_DIM) if half == 0 else (place >= HEAD_DIM)
    first = place == (HEAD_DIM if half == 0 else 0)
    return jnp.where(mine, own, jnp.where(first, flag, 0.0))


def rows_of(step):
    return pl.ds(pl.multiple_of(step * BLOCK, BLOCK), BLOCK)


def cost(microseconds):
    return pl.CostEstimate(flops=microseconds * PEAK, bytes_accessed=0, transcendentals=0)


def params():
    return pltpu.CompilerParams(vmem_limit_bytes=VMEM_BYTES)


SMEM = pl.BlockSpec(memory_space=pltpu.SMEM)
WHOLE = pl.BlockSpec(memory_space=pltpu.VMEM)
IDLE = pl.BlockSpec(memory_space=pl.ANY)
LENGTH, CORE, PART, LAYER = range(4)


def call_with(kernel, inputs, after, **options):
    specs = options.pop("in_specs") + [IDLE] * len(after)

    def run(*refs):
        kernel(*refs[: len(inputs)], *refs[len(inputs) + len(after) :])

    return pl.pallas_call(run, in_specs=specs, compiler_params=params(), **options)(*inputs, *after)


def pack_first_kernel(info_ref, wq_ref, wk_ref, wv_ref, *refs):
    small_refs, out_ref = refs[:9], refs[9]
    lines = [ref[...].astype(F32).reshape(1, BLOCK) for ref in small_refs[:8]]
    up_line = small_refs[8][...].astype(F32).reshape(1, -1)
    lines += [up_line[:, i * BLOCK : (i + 1) * BLOCK] for i in range(QUARTERS)]
    small = jnp.concatenate(lines + [jnp.zeros((PAIR - 12, BLOCK), F32)], axis=0).T
    place = pl.ds(pl.multiple_of((info_ref[PART] + 1) * PAIR, PAIR), PAIR)
    for i, ref in enumerate((wq_ref, wk_ref, wv_ref)):
        out_ref[:, i * PAIR : (i + 1) * PAIR] = ref[:, :PAIR]
        out_ref[:, (i + 4) * PAIR : (i + 5) * PAIR] = ref[:, place]
    out_ref[:, 3 * PAIR : 4 * PAIR] = small.astype(BF)


def pack_wide_kernel(info_ref, up_ref, wo_ref, out_ref):
    part = info_ref[PART]

    @pl.when(part < QUARTERS - 1)
    def _():
        out_ref[...] = up_ref[:, pl.ds(pl.multiple_of(part * UP_PART, UP_PART), UP_PART)]

    @pl.when(part == QUARTERS - 1)
    def _():
        out_ref[...] = wo_ref[...]


def pack(kernel, info, arrays, shape, after=()):
    return call_with(
        kernel, (info, *arrays), after,
        in_specs=[SMEM] + [WHOLE] * len(arrays),
        out_specs=WHOLE,
        out_shape=jax.ShapeDtypeStruct(shape, BF),
        cost_estimate=cost(2),
    )


def join_kernel(own_ref, *refs):
    came_refs, (line_ref, out_ref) = refs[:-2], refs[-2:]
    width = line_ref.shape[-1]
    for i, ref in enumerate(came_refs):
        line_ref[i] = ref[:, :width]
    for i, ref in enumerate((own_ref, *came_refs)):
        for copy in range(QUARTERS):
            out_ref[copy, i] = ref[:, width:]


def join(own, came, after=()):
    arrays = (own, *came)
    shape = lambda *lead: jax.ShapeDtypeStruct(lead, BF)
    return call_with(
        join_kernel, arrays, after,
        in_specs=[WHOLE] * len(arrays),
        out_specs=[WHOLE] * 2,
        out_shape=[
            shape(len(came), BLOCK, 4 * PAIR), shape(QUARTERS, len(arrays), BLOCK, 3 * PAIR),
        ],
        cost_estimate=cost(2),
    )


def repeat_kernel(*refs):
    for i, ref in enumerate(refs[:-1]):
        for copy in range(QUARTERS):
            refs[-1][copy, i] = ref[...]


def repeat(parts, after=()):
    return call_with(
        repeat_kernel, tuple(parts), after,
        in_specs=[WHOLE] * len(parts),
        out_specs=WHOLE,
        out_shape=jax.ShapeDtypeStruct((QUARTERS, len(parts)) + parts[0].shape, BF),
        cost_estimate=cost(30),
    )


def turn_kernel(source_ref, out_ref):
    out_ref[:WIDTH, :] = source_ref[...].T
    out_ref[WIDTH:, :] = jnp.zeros((BLOCKS * BLOCK - WIDTH, source_ref.shape[0]), BF)


def turn(tokens, after=()):
    return call_with(
        turn_kernel, (tokens,), after,
        in_specs=[WHOLE],
        out_specs=WHOLE,
        out_shape=jax.ShapeDtypeStruct((BLOCKS * BLOCK, tokens.shape[0]), BF),
        cost_estimate=cost(50),
    )


def cut(down, after=()):
    return call_with(
        cut_kernel, (down,), after,
        in_specs=[WHOLE],
        out_specs=WHOLE,
        out_shape=jax.ShapeDtypeStruct((down.shape[0], WIDTH), BF),
        cost_estimate=cost(1),
    )


def cut_kernel(down_ref, out_ref):
    out_ref[...] = down_ref[:, :WIDTH]


def lay_line(info_ref, target, own_ref, twin_ref, came_ref, twins_ref):
    core, layer = info_ref[CORE], info_ref[LAYER]
    width = target.shape[1]
    target[rows_of(2 * layer + core), :] = own_ref[:, :width]
    target[rows_of(2 * layer + 1 - core), :] = twin_ref[:, :width]
    for step in range(1, LAYERS):
        source = (layer + LAYERS - step) % LAYERS
        target[rows_of(2 * source + core), :] = came_ref[step - 1, :, :width]
        target[rows_of(2 * source + 1 - core), :] = twins_ref[step - 1, :, :width]


def lay(info_ref, target, width, mine_ref, other_ref):
    core, layer = info_ref[CORE], info_ref[LAYER]
    for quarter in range(QUARTERS):
        columns = slice(quarter * width, (quarter + 1) * width)
        for slot in range(LAYERS):
            source = (layer + LAYERS - slot) % LAYERS
            target[rows_of(2 * source + core), columns] = mine_ref[quarter, slot]
            target[rows_of(2 * source + 1 - core), columns] = other_ref[quarter, slot]


def attend_kernel(shift, info_ref, token_ref, *refs):
    first = shift is None
    count = 4 if first else 2
    sources, refs = refs[:count], refs[count:]
    if first:
        vectors_ref = refs[7]
        refs = refs[:7] + refs[8:]
    else:
        vectors_ref = refs[0]
        refs = refs[1:]
    (
        exp_ref, context_ref, wide_ref, inverse_ref, query_t_ref, key_ref,
        value_t_ref, mark_ref, weight_ref, held_ref, left_ref,
    ) = refs
    rows = token_ref.shape[0]
    if first:
        lay_line(info_ref, weight_ref, *sources)
        vectors_ref[...] = weight_ref[:, 3 * PAIR :].astype(F32).T[:16]
        bq = vectors_ref[0:1, :PAIR]
        bv = vectors_ref[1:2, :PAIR]
        weights = weight_ref[:WIDTH, : 3 * PAIR]
    else:
        @pl.when(pl.program_id(0) == 0)
        def _():
            lay(info_ref, weight_ref, 3 * PAIR, *sources)

        pair = pl.program_id(0) + shift
        place = pl.ds(pl.multiple_of(pair * PAIR, PAIR), PAIR)
        bq = vectors_ref[0:1, place]
        bv = vectors_ref[1:2, place]
        place = pl.ds(pl.multiple_of((pair - 1) * 3 * PAIR, 3 * PAIR), 3 * PAIR)
        weights = weight_ref[:WIDTH, place]
    product = dot(token_ref[...], weights, 1, 0)
    query = (product[:, :PAIR] + bq).astype(BF)
    key = product[:, PAIR : 2 * PAIR].astype(BF)
    value = (product[:, 2 * PAIR :] + bv).astype(BF)
    key_t = key.T
    query_t_ref[...] = query.T
    key_ref[...] = key
    value_t_ref[...] = value.T
    key_place = lax.broadcasted_iota(jnp.int32, (1, rows), 1)
    bias = jnp.where(key_place < info_ref[LENGTH], 0.0, MASKED)
    scaled = query.astype(F32) * HEAD_DIM**-0.5
    key_wide = key_t.astype(F32)
    value_wide = value.astype(F32)
    block = 128
    step = pl.program_id(0)

    def leave(half, start):
        lines = pl.ds(start, 2 * block)
        return pltpu.make_async_copy(
            held_ref.at[half, lines],
            exp_ref.at[2 * (step + (shift or 0)) + half, lines],
            left_ref.at[half, start // (2 * block)],
        )

    results = []
    for half in range(2):
        left = side((rows, PAIR), 1, half, scaled, 1.0).astype(BF)
        place = lax.broadcasted_iota(jnp.int32, (PAIR, rows), 0)
        right = jnp.where(place == (HEAD_DIM if half == 0 else 0), bias, key_wide).astype(BF)
        for start in range(0, rows, block):
            scores = dot(left[start : start + block], right, 1, 0)
            highest = jnp.max(scores, 1, keepdims=True)
            held_ref[half, start : start + block, :] = jnp.exp(scores - highest).astype(BF)
            if start % (2 * block):
                leave(half, start - block).start()
        values = side((rows, PAIR), 1, half, value_wide, 1.0).astype(BF)
        total = dot(held_ref[half], values, 1, 0)
        flag = HEAD_DIM if half == 0 else 0
        inverse = 1.0 / total[:, flag : flag + 1]
        results.append((total * inverse, inverse))
    low = lax.broadcasted_iota(jnp.int32, (rows, PAIR), 1) < HEAD_DIM
    context = jnp.where(low, results[0][0], results[1][0])
    mark_ref[...] = jnp.zeros_like(mark_ref)
    wide_ref[...] = context
    context_ref[...] = context.astype(BF)
    inverse_ref[...] = jnp.where(low, results[0][1], results[1][1])
    for half in range(2):
        for start in range(0, rows, 2 * block):
            leave(half, start).wait()


def attend(info, tokens, sources, start, pairs, vectors=None, held=(), after=()):
    rows = tokens.shape[0]
    first = vectors is None
    width = (4 if first else 12) * PAIR
    tall = lambda: pl.BlockSpec((rows, PAIR), lambda p: (0, start + p))
    flat = lambda: pl.BlockSpec((PAIR, rows), lambda p: (start + p, 0))
    array = lambda kind: jax.ShapeDtypeStruct((rows, WIDTH), kind)
    turned = jax.ShapeDtypeStruct((WIDTH, rows), BF)
    fixed = lambda *shape: pl.BlockSpec(shape, lambda p: (0, 0))
    table, mark = (16, BLOCKS * BLOCK), (8, 128)
    inputs = (info, tokens, *sources, *(() if first else (vectors,)))
    return call_with(
        functools.partial(attend_kernel, None if first else start),
        inputs,
        (*held, *after),
        grid=(pairs,),
        in_specs=[SMEM, WHOLE] + [WHOLE] * len(sources) + ([] if first else [fixed(*table)]),
        out_specs=[IDLE, tall(), tall(), tall(), flat(), tall(), flat()]
        + ([fixed(*table)] if first else [])
        + [fixed(*mark)],
        out_shape=[
            jax.ShapeDtypeStruct((2 * PAIRS, rows, rows), BF),
            array(BF), array(F32), array(F32), turned, array(BF), turned,
        ]
        + ([jax.ShapeDtypeStruct(table, F32)] if first else [])
        + [jax.ShapeDtypeStruct(mark, F32)],
        input_output_aliases={len(inputs) + i: i for i in range(len(held))},
        scratch_shapes=[
            pltpu.VMEM((BLOCKS * BLOCK, width), BF),
            pltpu.VMEM((2, rows, rows), BF),
            pltpu.SemaphoreType.DMA((2, rows // 256)),
        ],
        cost_estimate=cost(8 * pairs),
    )


def gelu_pair(values):
    t = 1.0 / (1.0 + (0.3275911 * 0.5**0.5) * jnp.abs(values))
    bell = jnp.exp(-0.5 * values * values)
    tail = t * (0.5 * 0.254829592 + t * (0.5 * -0.284496736 + t * (0.5 * 1.421413741 + t * (
        0.5 * -1.453152027 + t * (0.5 * 1.061405429)))))
    tail = tail * bell
    share = jnp.where(values >= 0.0, 1.0 - tail, tail)
    return values * share, share + values * bell * 0.3989422804014327


def row_mean(values):
    return jnp.sum(values, 1, keepdims=True) * (1.0 / WIDTH)


def column_sum(values):
    return jnp.sum(values, 0, keepdims=True)


def row_mean(values):
    return jnp.sum(values, 1, keepdims=True) * (1.0 / WIDTH)


def column_sum(values):
    return jnp.sum(values, 0, keepdims=True)


def up_places():
    for block in range(HIDDEN_PAD // (QUARTERS * BLOCK)):
        for quarter in range(QUARTERS):
            start = (block * QUARTERS + quarter) * BLOCK
            row = slice(8 + quarter, 9 + quarter)
            yield slice(start, start + BLOCK), row, slice(block * BLOCK, (block + 1) * BLOCK)


def feed_kernel(
    info_ref, context_in_ref, token_ref, cotangent_ref, *refs
):
    sources, refs = refs[:2], refs[2:]
    (
        down_ref, vector_ref,
        output_ref, first_ref, grad_context_ref, sums_ref, b1_sum_ref, down_term_ref, keep_ref,
        send_ref, w1_ref, w2_ref, b1_ref, product_ref,
        context_ref, normed_ref, active_ref, hidden_ref, feed_ref, branch_ref, came_ref,
    ) = refs
    step = pl.program_id(0)
    rows = token_ref.shape[0]

    @pl.when(step == 0)
    def _():
        core, layer = info_ref[CORE], info_ref[LAYER]
        copies = []
        for quarter in range(QUARTERS):
            columns = slice(quarter * UP_PART, (quarter + 1) * UP_PART)
            for slot in range(LAYERS):
                source = (layer + LAYERS - slot) % LAYERS
                for twin, ref in enumerate(sources):
                    block = 2 * source + (1 - core if twin else core)
                    target = w1_ref.at[rows_of(block), columns]
                    number = (quarter * LAYERS + slot) * 2 + twin
                    copies.append(
                        pltpu.make_async_copy(ref.at[quarter, slot], target, came_ref.at[number])
                    )
        lower = pltpu.make_async_copy(
            down_ref.at[:HIDDEN_PAD], w2_ref, came_ref.at[2 * QUARTERS * LAYERS]
        )
        copies.append(lower)
        for copy in copies:
            copy.start()
        for copy in copies:
            copy.wait()
        last = slice(HIDDEN_PAD - PAIR, HIDDEN_PAD)
        lane = lax.broadcasted_iota(jnp.int32, (BLOCKS * BLOCK, PAIR), 1)
        kept = lane < HIDDEN_SIZE - (HIDDEN_PAD - PAIR)
        w1_ref[:, last] = jnp.where(kept, w1_ref[:, last].astype(F32), 0.0).astype(BF)
        w2_ref[HIDDEN_SIZE:, :] = jnp.zeros((HIDDEN_PAD - HIDDEN_SIZE, WIDTH), BF)
        for place, row, columns in up_places():
            b1_ref[:, place] = vector_ref[row, columns]
        lane = lax.broadcasted_iota(jnp.int32, (1, HIDDEN_PAD), 1)
        b1_ref[...] = jnp.where(lane < HIDDEN_SIZE, b1_ref[...], 0.0)
        w2_ref[HIDDEN_SIZE:, :] = jnp.zeros((HIDDEN_PAD - HIDDEN_SIZE, WIDTH), BF)

    steps = normed_ref.shape[0] // rows
    down_steps = HIDDEN_PAD // UP_PART

    @pl.when(step < steps)
    def _():
        here = pl.ds(pl.multiple_of(step * rows, rows), rows)
        wo = w1_ref[:WIDTH, HIDDEN_PAD : HIDDEN_PAD + WIDTH]
        w1, w2 = w1_ref[:WIDTH, :HIDDEN_PAD], w2_ref[...]
        place = lax.broadcasted_iota(jnp.int32, (rows, 1), 0) + step * rows
        live = jnp.where(place < info_ref[LENGTH], 1.0, 0.0)
        vector = lambda i: vector_ref[i : i + 1, :WIDTH]
        out_add, down_add = vector(2), vector(3)
        gain_one, shift_one, gain_two, shift_two = vector(4), vector(5), vector(6), vector(7)
        context = context_in_ref[...]
        context_ref[here, :] = context
        first_sum = token_ref[...].astype(F32) + dot(context, wo, 1, 0) + out_add
        center = first_sum - row_mean(first_sum)
        rate_one = lax.rsqrt(row_mean(center * center) + EPSILON)
        unit_one = center * rate_one
        normed = (unit_one * gain_one + shift_one).astype(BF)
        normed_ref[here, :] = normed
        pre = dot(normed, w1, 1, 0) + b1_ref[...]
        active_full, slope = gelu_pair(pre)
        active = active_full.astype(BF)
        active_ref[here, :] = active
        second_sum = normed.astype(F32) + dot(active, w2, 1, 0) + down_add
        center = second_sum - row_mean(second_sum)
        rate_two = lax.rsqrt(row_mean(center * center) + EPSILON)
        unit_two = center * rate_two
        output_ref[...] = ((unit_two * gain_two + shift_two) * live).astype(BF)
        cotangent = cotangent_ref[...].astype(F32) * live
        inner = cotangent * gain_two
        grad_second = rate_two * (inner - row_mean(inner) - unit_two * row_mean(inner * unit_two))
        grad_feed = grad_second.astype(BF)
        feed_ref[here, :] = grad_feed
        grad_hidden = (dot(grad_feed, w2, 1, 1) * slope).astype(BF)
        hidden_ref[here, :] = grad_hidden
        grad_normed = grad_second + dot(grad_hidden, w1, 1, 1)
        inner = grad_normed * gain_one
        grad_first = rate_one * (inner - row_mean(inner) - unit_one * row_mean(inner * unit_one))
        first_ref[...] = grad_first
        grad_branch = grad_first.astype(BF)
        branch_ref[here, :] = grad_branch
        grad_context_ref[...] = dot(grad_branch, wo, 1, 1).astype(BF)
        sums = jnp.concatenate(
            [
                column_sum(grad_branch.astype(F32)),
                column_sum(grad_feed.astype(F32)),
                column_sum(grad_normed * unit_one),
                column_sum(grad_normed),
                column_sum(cotangent * unit_two),
                column_sum(cotangent),
                jnp.zeros((2, WIDTH), F32),
            ],
            axis=0,
        )
        b1_sum = column_sum(grad_hidden.astype(F32))

        @pl.when(step == 0)
        def _():
            sums_ref[...] = sums
            b1_sum_ref[...] = b1_sum

        @pl.when(step > 0)
        def _():
            sums_ref[...] += sums
            b1_sum_ref[...] += b1_sum

    @pl.when((step >= steps) & (step < steps + down_steps))
    def _():
        place = pl.ds(pl.multiple_of((step - steps) * UP_PART, UP_PART), UP_PART)
        down_term_ref[...] = dot(active_ref[:, place], feed_ref[...], 0, 0).astype(BF)

    @pl.when(step >= steps + down_steps)
    def _():
        part = step - steps - down_steps

        @pl.when(part == 0)
        def _():
            product_ref[WIDTH:, :] = jnp.zeros((BLOCKS * BLOCK - WIDTH, UP_PART), F32)

        @pl.when(part < QUARTERS - 1)
        def _():
            place = pl.ds(pl.multiple_of(part * UP_PART, UP_PART), UP_PART)
            product_ref[:WIDTH, :] = dot(normed_ref[...], hidden_ref[:, place], 0, 0)

        @pl.when(part == QUARTERS - 1)
        def _():
            product_ref[:WIDTH, :WIDTH] = dot(context_ref[...], branch_ref[...], 0, 0)

        deal(info_ref, product_ref, keep_ref, send_ref)


def feed(info, context, tokens, cotangent, wide, down, vectors, after=()):
    rows = tokens.shape[0]
    tile = rows // 4
    steps = rows // tile
    down_steps = HIDDEN_PAD // UP_PART
    part = lambda width: pl.BlockSpec((tile, width), lambda i: (jnp.minimum(i, steps - 1), 0))
    whole = lambda *shape: pl.BlockSpec(shape, lambda i: (0, 0))
    array = lambda width, kind: jax.ShapeDtypeStruct((rows, width), kind)
    held = lambda width: pltpu.VMEM((rows, width), BF)
    place = lambda: pl.BlockSpec(
        (1, LAYERS, BLOCK, UP_PART),
        lambda i: (jnp.clip(i - steps - down_steps, 0, QUARTERS - 1), 0, 0, 0),
    )
    shared = jax.ShapeDtypeStruct((QUARTERS, LAYERS, BLOCK, UP_PART), BF)
    return call_with(
        feed_kernel, (info, context, tokens, cotangent, *wide, down, vectors), after,
        grid=(steps + down_steps + QUARTERS,),
        in_specs=[SMEM]
        + [part(WIDTH), part(WIDTH), part(WIDTH)]
        + [IDLE] * (len(wide) + 1)
        + [whole(*vectors.shape)],
        out_specs=[
            part(WIDTH), part(WIDTH), part(WIDTH), whole(8, WIDTH), whole(1, HIDDEN_PAD),
            pl.BlockSpec((UP_PART, WIDTH), lambda i: (jnp.clip(i - steps, 0, down_steps - 1), 0)),
            place(), place(),
        ],
        out_shape=[
            array(WIDTH, BF), array(WIDTH, F32), array(WIDTH, BF),
            jax.ShapeDtypeStruct((8, WIDTH), F32),
            jax.ShapeDtypeStruct((1, HIDDEN_PAD), F32),
            jax.ShapeDtypeStruct((down.shape[0], WIDTH), BF),
            shared, shared,
        ],
        scratch_shapes=[
            pltpu.VMEM((BLOCKS * BLOCK, QUARTERS * UP_PART), BF),
            pltpu.VMEM((HIDDEN_PAD, WIDTH), BF),
            pltpu.VMEM((1, HIDDEN_PAD), F32),
            pltpu.VMEM((BLOCKS * BLOCK, UP_PART), F32),
            held(WIDTH), held(WIDTH), held(HIDDEN_PAD), held(HIDDEN_PAD), held(WIDTH), held(WIDTH),
            pltpu.SemaphoreType.DMA((2 * QUARTERS * LAYERS + 1,)),
        ],
        cost_estimate=cost(50),
    )


def deal(info_ref, product_ref, keep_ref, send_ref):
    core = info_ref[CORE]
    for layer in range(LAYERS):
        keep_ref[0, layer] = product_ref[rows_of(2 * layer + core), :].astype(BF)
        send_ref[0, layer] = product_ref[rows_of(2 * layer + 1 - core), :].astype(BF)


def head_grad_kernel(
    info_ref, token_t_ref, together_ref, first_ref, sums_ref, up_sum_ref, pair_ref,
    keep_ref, send_ref, product_ref, table_ref,
):
    step = pl.program_id(0)

    @pl.when(step < QUARTERS - 1)
    def _():
        part = first_ref[0, :, pl.ds(pl.multiple_of(step * PAIR, PAIR), PAIR)]
        both = jnp.concatenate([together_ref[0], part], axis=1)
        product_ref[...] = dot(token_t_ref[...], both, 1, 0)

    @pl.when(step == QUARTERS - 1)
    def _():
        product_ref[:, : 3 * PAIR] = dot(token_t_ref[...], together_ref[0], 1, 0)
        table_ref[...] = jnp.zeros_like(table_ref)
        table_ref[0:2, :WIDTH] = pair_ref[0:2, :]
        table_ref[2:8, :WIDTH] = sums_ref[0:6, :]
        for place, row, columns in up_places():
            table_ref[row, columns] = up_sum_ref[:, place]
        product_ref[:, 3 * PAIR :] = table_ref[...].T

    deal(info_ref, product_ref, keep_ref, send_ref)


def head_grad(info, token_t, together, sums, up_sum, pair_sums, after=()):
    rows = token_t.shape[1]
    place = lambda: pl.BlockSpec((1, LAYERS, BLOCK, 4 * PAIR), lambda d: (d, 0, 0, 0))
    array = jax.ShapeDtypeStruct((QUARTERS, LAYERS, BLOCK, 4 * PAIR), BF)
    return call_with(
        head_grad_kernel, (info, token_t, together, together, sums, up_sum, pair_sums), after,
        grid=(QUARTERS,),
        in_specs=[
            SMEM, WHOLE,
            pl.BlockSpec((1, rows, 3 * PAIR), lambda d: (d + 1, 0, 0)),
            pl.BlockSpec((1, rows, 3 * PAIR), lambda d: (0, 0, 0)),
            WHOLE, WHOLE, WHOLE,
        ],
        out_specs=[place(), place()],
        out_shape=[array, array],
        scratch_shapes=[
            pltpu.VMEM((BLOCKS * BLOCK, 4 * PAIR), F32),
            pltpu.VMEM((PAIR, BLOCKS * BLOCK), F32),
        ],
        cost_estimate=cost(8),
    )


def meet_kernel(info_ref, keep_ref, came_ref, *out_refs):
    for apart in range(QUARTERS):
        quarter = info_ref[PART] ^ apart
        out_refs[apart][0] = keep_ref[quarter, 0] + came_ref[quarter, 0]


def meet(info, keep, came, after=()):
    width = keep.shape[-1]
    block = lambda: pl.BlockSpec(
        (QUARTERS, 1, BLOCK, width), lambda s, info: (0, (info[LAYER] + s) % LAYERS, 0, 0)
    )

    def run(info_ref, keep_ref, came_ref, *refs):
        meet_kernel(info_ref, keep_ref, came_ref, *refs[len(after) :])

    return pl.pallas_call(
        run,
        grid_spec=pltpu.PrefetchScalarGridSpec(
            num_scalar_prefetch=1,
            grid=(LAYERS,),
            in_specs=[block(), block()] + [IDLE] * len(after),
            out_specs=[pl.BlockSpec((1, BLOCK, width), lambda s, info: (s, 0, 0))] * QUARTERS,
        ),
        out_shape=[jax.ShapeDtypeStruct((LAYERS, BLOCK, width), BF)] * QUARTERS,
        compiler_params=params(),
        cost_estimate=cost(3),
    )(info, keep, came, *after)


def attend_back_kernel(
    grad_ref, wide_ref, inverse_ref, exp_ref, query_t_ref, key_ref, value_t_ref,
    together_ref, sums_ref, score_ref,
):
    rows = grad_ref.shape[0]
    inverse = inverse_ref[...]
    grad = grad_ref[...].astype(F32)
    scaled = grad * inverse
    dots = scaled * wide_ref[...]
    scaled_t = scaled.T.astype(BF)
    value_wide = value_t_ref[...].astype(F32)
    lane = lax.broadcasted_iota(jnp.int32, (rows, PAIR), 1)
    place = lax.broadcasted_iota(jnp.int32, (PAIR, rows), 0)
    block = 128
    dq, dk_t, dv_t = [], [], []
    for half in range(2):
        mine = (lane < HEAD_DIM) if half == 0 else (lane >= HEAD_DIM)
        flag = HEAD_DIM if half == 0 else 0
        offset = jnp.sum(jnp.where(mine, -dots, 0.0), 1, keepdims=True)
        high = offset.astype(BF).astype(F32)
        rest = offset - high
        left = jnp.where(
            mine, scaled, jnp.where(lane == flag, high, jnp.where(lane == flag + 1, rest, 0.0))
        ).astype(BF)
        right = jnp.where((place == flag) | (place == flag + 1), 1.0, value_wide).astype(BF)
        for start in range(0, rows, block):
            grad_probs = dot(left[start : start + block], right, 1, 0)
            weight = exp_ref[half, start : start + block, :].astype(F32)
            score_ref[half, start : start + block, :] = (grad_probs * weight).astype(BF)
        own = slice(half * HEAD_DIM, (half + 1) * HEAD_DIM)
        dv_t.append(dot(scaled_t[own], exp_ref[half], 1, 0))
        dk_t.append(dot(query_t_ref[own, :], score_ref[half], 1, 0))
        dq.append(dot(score_ref[half], key_ref[...], 1, 0))
    factor = HEAD_DIM**-0.5
    dq_low = (jnp.where(lane < HEAD_DIM, dq[0], dq[1]) * factor).astype(BF)
    dk_low = (jnp.concatenate(dk_t, axis=0) * factor).T.astype(BF)
    dv_low = jnp.concatenate(dv_t, axis=0).T.astype(BF)
    together_ref[0] = jnp.concatenate([dq_low, dk_low, dv_low], axis=1)
    query_sum = column_sum(dq_low.astype(F32))
    value_sum = column_sum(dv_low.astype(F32))
    sums_ref[...] = jnp.concatenate([query_sum, value_sum, jnp.zeros((6, PAIR), F32)], axis=0)


def attend_back(grad_context, saved, start, pairs, after=()):
    exps, wide, inverse, query_t, key, value_t = saved
    rows = grad_context.shape[0]
    tall = lambda: pl.BlockSpec((rows, PAIR), lambda p: (0, start + p))
    flat = lambda: pl.BlockSpec((PAIR, rows), lambda p: (start + p, 0))
    return call_with(
        attend_back_kernel,
        (grad_context, wide, inverse, exps, query_t, key, value_t),
        after,
        grid=(pairs,),
        in_specs=[
            tall(), tall(), tall(),
            pl.BlockSpec((2, rows, rows), lambda p: (start + p, 0, 0)),
            flat(), tall(), flat(),
        ],
        out_specs=[
            pl.BlockSpec((1, rows, 3 * PAIR), lambda p: (p, 0, 0)),
            pl.BlockSpec((8, PAIR), lambda p: (0, p)),
        ],
        out_shape=[
            jax.ShapeDtypeStruct((pairs, rows, 3 * PAIR), BF),
            jax.ShapeDtypeStruct((8, pairs * PAIR), F32),
        ],
        scratch_shapes=[pltpu.VMEM((2, rows, rows), BF)],
        cost_estimate=cost(8 * pairs),
    )


def token_kernel(info_ref, grad_ref, together_ref, *refs):
    count = 4
    first_sources, rest_sources = refs[:count], refs[count : count + 2]
    out_ref, first_ref, rest_ref = refs[-3:]

    @pl.when(pl.program_id(0) == 0)
    def _():
        lay_line(info_ref, first_ref, *first_sources)
        lay(info_ref, rest_ref, 3 * PAIR, *rest_sources)

    pieces = [together_ref[i] for i in range(1, PAIRS)]
    total = grad_ref[...] + dot(together_ref[0], first_ref[:WIDTH, : 3 * PAIR], 1, 1)
    total += dot(jnp.concatenate(pieces, axis=1), rest_ref[:WIDTH, :], 1, 1)
    out_ref[...] = total.astype(BF)


def token_back(info, grad_first, together, first, rest, after):
    rows = grad_first.shape[0]
    tile = 256
    part = pl.BlockSpec((tile, WIDTH), lambda i: (i, 0))
    piece = pl.BlockSpec((PAIRS, tile, 3 * PAIR), lambda i: (0, i, 0))
    return call_with(
        token_kernel, (info, grad_first, together, *first, *rest), after,
        grid=(rows // tile,),
        in_specs=[SMEM, part, piece]
        + [WHOLE] * (len(first) + len(rest)),
        out_specs=part,
        out_shape=jax.ShapeDtypeStruct((rows, WIDTH), BF),
        scratch_shapes=[
            pltpu.VMEM((BLOCKS * BLOCK, 4 * PAIR), BF),
            pltpu.VMEM((BLOCKS * BLOCK, 12 * PAIR), BF),
        ],
        cost_estimate=cost(7),
    )


def plane_kernel(groups, *refs):
    inputs, outputs = refs[: groups * QUARTERS], refs[groups * QUARTERS :]
    start = 0
    for group in range(groups):
        mine = inputs[group * QUARTERS : (group + 1) * QUARTERS]
        width = mine[0].shape[-1]
        for step in range(LAYERS):
            total = sum(ref[step].astype(F32) for ref in mine)
            outputs[step][:, start : start + width] = total.astype(BF)
        start += width


def plane(groups, after=()):
    width = sum(group[0].shape[-1] for group in groups)
    return call_with(
        functools.partial(plane_kernel, len(groups)),
        tuple(array for group in groups for array in group),
        after,
        in_specs=[WHOLE] * (len(groups) * QUARTERS),
        out_specs=[WHOLE] * LAYERS,
        out_shape=[jax.ShapeDtypeStruct((BLOCK, width), BF)] * LAYERS,
        cost_estimate=cost(2),
    )


def plane_stack_kernel(info_ref, *refs):
    for step in range(LAYERS):
        total = sum(ref[step].astype(F32) for ref in refs[:-1])
        refs[-1][(info_ref[LAYER] + step) % LAYERS] = total.astype(BF)


def plane_stack(info, parts, after=()):
    return call_with(
        plane_stack_kernel, (info, *parts), after,
        in_specs=[SMEM] + [WHOLE] * len(parts),
        out_specs=WHOLE,
        out_shape=jax.ShapeDtypeStruct(parts[0].shape, BF),
        cost_estimate=cost(2),
    )


def line_kernel(counts, *refs):
    inputs, out_ref = refs[:-1], refs[-1]
    start = 0
    for count in counts:
        mine, inputs = inputs[:count], inputs[count:]
        width = mine[0].shape[-1]
        parts = [ref[...] for ref in mine] if count > 1 else [mine[0][i] for i in range(QUARTERS)]
        total = sum(part.astype(F32) for part in parts).astype(BF)
        for copy in range(out_ref.shape[0]):
            out_ref[copy, :, start : start + width] = total
        start += width


def line(groups, copies=QUARTERS, after=()):
    width = sum(group[0].shape[-1] for group in groups)
    arrays = tuple(array for group in groups for array in group)
    return call_with(
        functools.partial(line_kernel, [len(group) for group in groups]), arrays, after,
        in_specs=[WHOLE] * len(arrays),
        out_specs=WHOLE,
        out_shape=jax.ShapeDtypeStruct((copies, BLOCK, width), BF),
        cost_estimate=cost(1),
    )


def finish_wide_kernel(info_ref, wide_ref, wo_ref, up_ref, down_ref):
    extra = wo_ref.shape[1] - WIDTH
    blank = jnp.zeros((BLOCK, extra), F32)
    used = HIDDEN_PAD // (QUARTERS * BLOCK)
    owner = 2 * info_ref[LAYER] + info_ref[CORE]
    for quarter in range(QUARTERS):
        lines = slice(quarter * BLOCK, (quarter + 1) * BLOCK)
        down = wide_ref[quarter, :, UP_PART:].astype(F32)
        down_ref[lines, :WIDTH] = jnp.where(owner < used, down, 0.0)
        down_ref[lines, WIDTH:] = blank
    for quarter in range(QUARTERS - 1):
        columns = slice(quarter * UP_PART, (quarter + 1) * UP_PART)
        up_ref[:, columns] = wide_ref[quarter, :, :UP_PART].astype(F32)
    up_ref[:, HIDDEN_PAD:] = jnp.zeros((BLOCK, up_ref.shape[1] - HIDDEN_PAD), F32)
    wo_ref[:, :WIDTH] = wide_ref[QUARTERS - 1, :, :WIDTH].astype(F32)
    wo_ref[:, WIDTH:] = blank


def finish_wide(info, wide, super_width, super_hidden, after=()):
    array = lambda *shape: jax.ShapeDtypeStruct(shape, F32)
    return call_with(
        finish_wide_kernel, (info, wide), after,
        in_specs=[SMEM, WHOLE],
        out_specs=[WHOLE] * 3,
        out_shape=[
            array(BLOCK, super_width), array(BLOCK, super_hidden),
            array(QUARTERS * BLOCK, super_width),
        ],
        cost_estimate=cost(3),
    )


def finish_heads_kernel(info_ref, *refs):
    parts, three, line_refs = refs[:QUARTERS], refs[4:7], refs[7:15]
    up_line_ref, heads_ref = refs[15:]
    for apart, ref in enumerate(parts):
        heads_ref[info_ref[PART] ^ apart] = ref[...].astype(F32)
    for i, ref in enumerate(three):
        ref[:, :PAIR] = heads_ref[i, :, 3 * PAIR :]
        for pair in range(1, PAIRS):
            part = heads_ref[pair - 1, :, i * PAIR : (i + 1) * PAIR]
            ref[:, pair * PAIR : (pair + 1) * PAIR] = part
        ref[:, WIDTH:] = jnp.zeros((BLOCK, ref.shape[1] - WIDTH), F32)
    lines = heads_ref[QUARTERS - 1, :, 3 * PAIR :].T
    for i, ref in enumerate(line_refs):
        ref[...] = lines[i]
    for i in range(QUARTERS):
        up_line_ref[i * BLOCK : (i + 1) * BLOCK] = lines[8 + i]


def finish_heads(info, parts, super_width, after=()):
    array = lambda *shape: jax.ShapeDtypeStruct(shape, F32)
    return call_with(
        finish_heads_kernel, (info, *parts), after,
        in_specs=[SMEM] + [WHOLE] * QUARTERS,
        out_specs=[WHOLE] * 12,
        out_shape=[array(BLOCK, super_width)] * 3
        + [array(BLOCK)] * 8
        + [array(QUARTERS * BLOCK)],
        scratch_shapes=[pltpu.VMEM((QUARTERS, BLOCK, 4 * PAIR), F32)],
        cost_estimate=cost(2),
    )


SWAP = [(i, i ^ 1) for i in range(BLOCKS)]
STEPS = range(1, LAYERS)
DISTANCES = range(1, QUARTERS)


def twin(part):
    return lax.ppermute(part, "fsdp", SWAP)


def along(part, step):
    pairs = [(i, (i + 2 * step) % BLOCKS) for i in range(BLOCKS)]
    return lax.ppermute(part, "fsdp", pairs)


LINES = [[2 * layer + core for layer in range(LAYERS)] for core in range(2)]


def trade_plane(parts):
    return lax.all_to_all(parts, "dp", 0, 0)


def trade_line(parts):
    return lax.all_to_all(parts, "fsdp", 0, 0, axis_index_groups=LINES)


def copies(part):
    return jnp.broadcast_to(part[None], (QUARTERS,) + part.shape)


def across(part, apart):
    return lax.ppermute(part, "dp", [(i, i ^ apart) for i in range(QUARTERS)])


def drop(saved):
    return (saved[0],) + tuple(saved[2:])


def on_device(
    tokens, lengths, query_weight, key_weight, value_weight, out_weight, up_weight, down_weight,
    query_bias, value_bias, out_bias, up_bias, down_bias, first_gain, first_shift, second_gain,
    second_shift, cotangent,
):
    super_width, super_hidden = query_weight.shape[1], up_weight.shape[1]
    index = lax.axis_index("fsdp").astype(jnp.int32)
    part = lax.axis_index("dp").astype(jnp.int32)
    info = jnp.stack([lengths[0], index % 2, part, index // 2])
    qkv = (query_weight, key_weight, value_weight)
    small = (
        query_bias, value_bias, out_bias, down_bias,
        first_gain, first_shift, second_gain, second_shift, up_bias,
    )
    first_own = pack(pack_first_kernel, info, qkv + small, (BLOCK, 7 * PAIR))
    first_came = [along(first_own, step) for step in STEPS]
    wide_own = pack(
        pack_wide_kernel, info, (up_weight, out_weight), (BLOCK, UP_PART), after=(first_own,)
    )
    first_line, rest_copies = join(first_own, first_came, after=(wide_own,))
    first = (first_own, twin(first_own), first_line, twin(first_line))
    rest_mine = trade_plane(rest_copies)
    down_cut = cut(down_weight, after=(wide_own, *first))
    wide_line = [wide_own] + [along(wide_own, step) for step in STEPS]
    down = lax.all_gather(down_cut, "fsdp", axis=0, tiled=True)
    *saved, vectors, mark = attend(info, tokens, first, 0, 1, after=(down_cut,))
    rest = (rest_mine, twin(rest_mine))
    wide_mine = trade_plane(repeat(wide_line, after=(mark,)))
    *saved, mark = attend(info, tokens, rest, 1, 3, vectors, saved, after=wide_line)
    wide_mine, mark = lax.optimization_barrier((wide_mine, mark))
    wide = (wide_mine, twin(wide_mine))
    *saved, mark = attend(info, tokens, rest, 4, 1, vectors, saved, after=(wide_mine, mark))
    (
        output, grad_first, grad_context, sums, up_sum, down_term, up_keep, up_send
    ) = feed(info, saved[1], tokens, cotangent, wide, down, vectors)
    down_total = lax.psum_scatter(down_term, "fsdp", scatter_dimension=0, tiled=True)
    token_t = turn(tokens, after=(up_keep,))
    up_near = meet(info, up_keep, twin(up_send), after=(token_t,))
    send = lambda near: [near[0]] + [across(near[apart], apart) for apart in DISTANCES]
    pass_on = lambda layers: [layers[0]] + [along(layers[step], step) for step in STEPS]
    up_plane = send(up_near)
    together, pair_sums = attend_back(grad_context, drop(saved), 0, PAIRS, after=(up_near[0],))
    head_keep, head_send = head_grad(
        info, token_t, together, sums, up_sum, pair_sums, after=up_plane[1:]
    )
    down_plane = trade_plane(down_total.reshape(QUARTERS, BLOCK, WIDTH))
    head_near = meet(info, head_keep, twin(head_send))
    head_plane = send(head_near)
    up_layers = plane_stack(info, up_plane, after=(head_near[0], down_plane))
    up_line = trade_line(up_layers)
    layers = plane([head_plane], after=(up_layers,))
    head_line = pass_on(layers)
    token_grad = token_back(info, grad_first, together, first, rest, (layers[0],))
    wide_copies = line([[up_line], [down_plane]], after=(token_grad, *head_line[1:]))
    wide_total = trade_plane(wide_copies)
    head_total = line([head_line], 1, after=(token_grad,)).reshape(BLOCK, 4 * PAIR)
    head_parts = send([head_total] * QUARTERS)
    wo, up, down = finish_wide(info, wide_total, super_width, super_hidden, after=(head_total,))
    *results, up_line = finish_heads(info, head_parts, super_width, after=(wo,))
    heads, lines = results[:3], results[3:]
    order = lines[:3] + [up_line] + lines[3:]
    return (output, token_grad, *heads, wo, up, down, *order)


def widen(matrix, row_count, column_count):
    return jnp.pad(matrix, ((0, row_count - matrix.shape[0]), (0, column_count - matrix.shape[1])))


def on_device_elsewhere(
    tokens, lengths, query_weight, key_weight, value_weight, out_weight, up_weight, down_weight,
    query_bias, value_bias, out_bias, up_bias, down_bias, first_gain, first_shift, second_gain,
    second_shift, cotangent,
):
    owned, super_width = query_weight.shape
    super_hidden = up_weight.shape[1]
    info = jnp.stack([lengths[0]] + [jnp.zeros((), jnp.int32)] * 3)
    gather = lambda array: lax.all_gather(array, "fsdp", axis=0, tiled=True)
    qkv = [gather(array) for array in (query_weight, key_weight, value_weight)]
    lines = [
        gather(array)
        for array in (
            query_bias, value_bias, out_bias, down_bias,
            first_gain, first_shift, second_gain, second_shift,
        )
    ]
    up_lines = gather(up_bias).reshape(BLOCKS, QUARTERS, BLOCK).transpose(1, 0, 2)
    lines = jnp.concatenate([jnp.stack(lines), up_lines.reshape(QUARTERS, -1)], axis=0)
    columns = jnp.pad(lines, ((0, PAIR - lines.shape[0]), (0, 0))).T
    first_full = jnp.concatenate([array[:, :PAIR] for array in qkv] + [columns], axis=1)
    places = [slice(pair * PAIR, (pair + 1) * PAIR) for pair in range(1, PAIRS)]
    rest_full = jnp.concatenate([array[:, place] for place in places for array in qkv], axis=1)
    wide_full = jnp.concatenate([gather(up_weight)[:, :HIDDEN_PAD], gather(out_weight)], axis=1)
    down = gather(down_weight)[:, :WIDTH]

    back = [(LAYERS - slot) % LAYERS for slot in range(LAYERS)]

    def pieces(full):
        blocks = full.reshape(LAYERS, 2, BLOCK, QUARTERS, -1).transpose(0, 1, 3, 2, 4)
        blocks = jnp.stack([blocks[layer] for layer in back], axis=2)
        return blocks[0], blocks[1]

    blocks = first_full.reshape(LAYERS, 2, BLOCK, -1)
    blocks = jnp.stack([blocks[layer] for layer in back])
    first = (blocks[0, 0], blocks[0, 1], blocks[1:, 0], blocks[1:, 1])
    rest, wide = pieces(rest_full), pieces(wide_full)
    token_t = turn(tokens)
    *saved, vectors, mark = attend(info, tokens, first, 0, 1)
    *saved, mark = attend(info, tokens, rest, 1, 4, vectors, saved)
    (
        output, grad_first, grad_context, sums, up_sum, down_term, *up_parts
    ) = feed(info, saved[1], tokens, cotangent, wide, down, vectors)
    deep = lax.broadcasted_iota(jnp.int32, (super_hidden, 1), 0)
    down_term = jnp.where(deep < HIDDEN_PAD, down_term, 0.0)
    together, pair_sums = attend_back(grad_context, drop(saved), 0, PAIRS)

    def both(parts):
        return jnp.stack(parts, axis=2).transpose(1, 2, 3, 0, 4).reshape(super_width, -1)

    def total(array):
        array = lax.psum_scatter(array, "fsdp", scatter_dimension=0, tiled=True)
        return lax.psum(array, "dp").astype(F32)

    wide_total = total(both(up_parts))
    heads_total = total(both(head_grad(info, token_t, together, sums, up_sum, pair_sums)))
    heads_total = heads_total.reshape(owned, QUARTERS, 4 * PAIR)
    first_total = heads_total[:, :, 3 * PAIR :].reshape(owned, 4 * PAIR)
    heads_total = heads_total[:, :, : 3 * PAIR].reshape(owned, PAIRS - 1, 3, PAIR)
    down_total = total(down_term)
    token_grad = token_back(
        info, grad_first, together, first, rest, ()
    )
    full = lambda matrix: widen(matrix, owned, super_width)
    heads = [
        full(
            jnp.concatenate(
                [first_total[:, i * PAIR : (i + 1) * PAIR], heads_total[:, :, i].reshape(owned, -1)],
                axis=1,
            )
        )
        for i in range(3)
    ]
    lines = gather(first_total[:, 3 * PAIR :]).T
    up_lines = lines[8:12].reshape(QUARTERS, BLOCKS, BLOCK).transpose(1, 0, 2).reshape(-1)
    place = lax.axis_index("fsdp")
    mine = lambda array: lax.dynamic_slice_in_dim(array, place * owned, owned)
    deep = up_bias.shape[0]
    return (
        output, token_grad, *heads,
        full(wide_total[:, HIDDEN_PAD : HIDDEN_PAD + WIDTH]),
        widen(wide_total[:, :HIDDEN_PAD], owned, super_hidden),
        widen(down_total, deep, super_width),
        mine(lines[0]), mine(lines[1]), mine(lines[2]),
        lax.dynamic_slice_in_dim(up_lines, place * deep, deep),
        mine(lines[3]), mine(lines[4]), mine(lines[5]), mine(lines[6]), mine(lines[7]),
    )


def solution(mesh):
    rows = P(("dp", "fsdp"), None)
    held = P("fsdp", None)
    line = P("fsdp")
    near = mesh.shape["dp"] == QUARTERS and mesh.shape["fsdp"] == BLOCKS
    return jax.shard_map(
        on_device if near else on_device_elsewhere,
        mesh=mesh,
        in_specs=(rows, P(("dp", "fsdp"))) + (held,) * 6 + (line,) * 9 + (rows,),
        out_specs=(rows, rows) + (held,) * 6 + (line,) * 9,
        check_vma=False,
    )
```

```python
import functools

import jax
import jax.numpy as jnp
from jax import lax
from jax.experimental import pallas as pl
from jax.experimental.pallas import tpu as pltpu
from jax.sharding import PartitionSpec as P

HEAD_DIM = 64
HIDDEN_SIZE = 2240
WIDTH = 640
EPSILON = 1e-05
MASKED = -1e30
PAIR = 2 * HEAD_DIM
PAIRS = WIDTH // PAIR
BF = jnp.bfloat16
F32 = jnp.float32
VMEM_BYTES = 127 * 2**19
BLOCKS = 8
BLOCK = 96
QUARTERS = 4
LAYERS = BLOCKS // 2
HIDDEN_PAD = 2304
UP_PART = 768
PEAK = 10**9


def dot(left, right, left_dim, right_dim):
    return lax.dot_general(
        left, right, (((left_dim,), (right_dim,)), ((), ())), preferred_element_type=F32
    )


def side(shape, axis, half, own, flag):
    place = lax.broadcasted_iota(jnp.int32, shape, axis)
    mine = (place < HEAD_DIM) if half == 0 else (place >= HEAD_DIM)
    first = place == (HEAD_DIM if half == 0 else 0)
    return jnp.where(mine, own, jnp.where(first, flag, 0.0))


def rows_of(step):
    return pl.ds(pl.multiple_of(step * BLOCK, BLOCK), BLOCK)


def cost(microseconds):
    return pl.CostEstimate(flops=microseconds * PEAK, bytes_accessed=0, transcendentals=0)


def params():
    return pltpu.CompilerParams(vmem_limit_bytes=VMEM_BYTES)


SMEM = pl.BlockSpec(memory_space=pltpu.SMEM)
WHOLE = pl.BlockSpec(memory_space=pltpu.VMEM)
IDLE = pl.BlockSpec(memory_space=pl.ANY)
LENGTH, CORE, PART, LAYER = range(4)


def call_with(kernel, inputs, after, **options):
    specs = options.pop("in_specs") + [IDLE] * len(after)

    def run(*refs):
        kernel(*refs[: len(inputs)], *refs[len(inputs) + len(after) :])

    return pl.pallas_call(run, in_specs=specs, compiler_params=params(), **options)(*inputs, *after)


def pack_first_kernel(info_ref, wq_ref, wk_ref, wv_ref, *refs):
    small_refs, out_ref = refs[:9], refs[9]
    lines = [ref[...].astype(F32).reshape(1, BLOCK) for ref in small_refs[:8]]
    up_line = small_refs[8][...].astype(F32).reshape(1, -1)
    lines += [up_line[:, i * BLOCK : (i + 1) * BLOCK] for i in range(QUARTERS)]
    small = jnp.concatenate(lines + [jnp.zeros((PAIR - 12, BLOCK), F32)], axis=0).T
    place = pl.ds(pl.multiple_of((info_ref[PART] + 1) * PAIR, PAIR), PAIR)
    for i, ref in enumerate((wq_ref, wk_ref, wv_ref)):
        out_ref[:, i * PAIR : (i + 1) * PAIR] = ref[:, :PAIR]
        out_ref[:, (i + 4) * PAIR : (i + 5) * PAIR] = ref[:, place]
    out_ref[:, 3 * PAIR : 4 * PAIR] = small.astype(BF)


def pack_wide_kernel(info_ref, up_ref, wo_ref, out_ref):
    part = info_ref[PART]

    @pl.when(part < QUARTERS - 1)
    def _():
        out_ref[...] = up_ref[:, pl.ds(pl.multiple_of(part * UP_PART, UP_PART), UP_PART)]

    @pl.when(part == QUARTERS - 1)
    def _():
        out_ref[...] = wo_ref[...]


def pack(kernel, info, arrays, shape, after=()):
    return call_with(
        kernel, (info, *arrays), after,
        in_specs=[SMEM] + [WHOLE] * len(arrays),
        out_specs=WHOLE,
        out_shape=jax.ShapeDtypeStruct(shape, BF),
        cost_estimate=cost(2),
    )


def join_kernel(own_ref, *refs):
    came_refs, (line_ref, out_ref) = refs[:-2], refs[-2:]
    width = line_ref.shape[-1]
    for i, ref in enumerate(came_refs):
        line_ref[i] = ref[:, :width]
    for i, ref in enumerate((own_ref, *came_refs)):
        for copy in range(QUARTERS):
            out_ref[copy, i] = ref[:, width:]


def join(own, came, after=()):
    arrays = (own, *came)
    shape = lambda *lead: jax.ShapeDtypeStruct(lead, BF)
    return call_with(
        join_kernel, arrays, after,
        in_specs=[WHOLE] * len(arrays),
        out_specs=[WHOLE] * 2,
        out_shape=[
            shape(len(came), BLOCK, 4 * PAIR), shape(QUARTERS, len(arrays), BLOCK, 3 * PAIR),
        ],
        cost_estimate=cost(2),
    )


def repeat_kernel(*refs):
    for i, ref in enumerate(refs[:-1]):
        for copy in range(QUARTERS):
            refs[-1][copy, i] = ref[...]


def repeat(parts, after=()):
    return call_with(
        repeat_kernel, tuple(parts), after,
        in_specs=[WHOLE] * len(parts),
        out_specs=WHOLE,
        out_shape=jax.ShapeDtypeStruct((QUARTERS, len(parts)) + parts[0].shape, BF),
        cost_estimate=cost(30),
    )


def turn_kernel(source_ref, out_ref):
    out_ref[:WIDTH, :] = source_ref[...].T
    out_ref[WIDTH:, :] = jnp.zeros((BLOCKS * BLOCK - WIDTH, source_ref.shape[0]), BF)


def turn(tokens, after=()):
    return call_with(
        turn_kernel, (tokens,), after,
        in_specs=[WHOLE],
        out_specs=WHOLE,
        out_shape=jax.ShapeDtypeStruct((BLOCKS * BLOCK, tokens.shape[0]), BF),
        cost_estimate=cost(50),
    )


def cut(down, after=()):
    return call_with(
        cut_kernel, (down,), after,
        in_specs=[WHOLE],
        out_specs=WHOLE,
        out_shape=jax.ShapeDtypeStruct((down.shape[0], WIDTH), BF),
        cost_estimate=cost(1),
    )


def cut_kernel(down_ref, out_ref):
    out_ref[...] = down_ref[:, :WIDTH]


def lay_line(info_ref, target, own_ref, twin_ref, came_ref, twins_ref):
    core, layer = info_ref[CORE], info_ref[LAYER]
    width = target.shape[1]
    target[rows_of(2 * layer + core), :] = own_ref[:, :width]
    target[rows_of(2 * layer + 1 - core), :] = twin_ref[:, :width]
    for step in range(1, LAYERS):
        source = (layer + LAYERS - step) % LAYERS
        target[rows_of(2 * source + core), :] = came_ref[step - 1, :, :width]
        target[rows_of(2 * source + 1 - core), :] = twins_ref[step - 1, :, :width]


def lay(info_ref, target, width, mine_ref, other_ref):
    core, layer = info_ref[CORE], info_ref[LAYER]
    for quarter in range(QUARTERS):
        columns = slice(quarter * width, (quarter + 1) * width)
        for slot in range(LAYERS):
            source = (layer + LAYERS - slot) % LAYERS
            target[rows_of(2 * source + core), columns] = mine_ref[quarter, slot]
            target[rows_of(2 * source + 1 - core), columns] = other_ref[quarter, slot]


def attend_kernel(shift, info_ref, token_ref, *refs):
    first = shift is None
    count = 4 if first else 2
    sources, refs = refs[:count], refs[count:]
    if first:
        vectors_ref = refs[7]
        refs = refs[:7] + refs[8:]
    else:
        vectors_ref = refs[0]
        refs = refs[1:]
    (
        exp_ref, context_ref, wide_ref, inverse_ref, query_t_ref, key_ref,
        value_t_ref, mark_ref, weight_ref, held_ref, left_ref,
    ) = refs
    rows = token_ref.shape[0]
    if first:
        lay_line(info_ref, weight_ref, *sources)
        vectors_ref[...] = weight_ref[:, 3 * PAIR :].astype(F32).T[:16]
        bq = vectors_ref[0:1, :PAIR]
        bv = vectors_ref[1:2, :PAIR]
        weights = weight_ref[:WIDTH, : 3 * PAIR]
    else:
        @pl.when(pl.program_id(0) == 0)
        def _():
            lay(info_ref, weight_ref, 3 * PAIR, *sources)

        pair = pl.program_id(0) + shift
        place = pl.ds(pl.multiple_of(pair * PAIR, PAIR), PAIR)
        bq = vectors_ref[0:1, place]
        bv = vectors_ref[1:2, place]
        place = pl.ds(pl.multiple_of((pair - 1) * 3 * PAIR, 3 * PAIR), 3 * PAIR)
        weights = weight_ref[:WIDTH, place]
    product = dot(token_ref[...], weights, 1, 0)
    query = (product[:, :PAIR] + bq).astype(BF)
    key = product[:, PAIR : 2 * PAIR].astype(BF)
    value = (product[:, 2 * PAIR :] + bv).astype(BF)
    key_t = key.T
    query_t_ref[...] = query.T
    key_ref[...] = key
    value_t_ref[...] = value.T
    key_place = lax.broadcasted_iota(jnp.int32, (1, rows), 1)
    bias = jnp.where(key_place < info_ref[LENGTH], 0.0, MASKED)
    scaled = query.astype(F32) * HEAD_DIM**-0.5
    key_wide = key_t.astype(F32)
    value_wide = value.astype(F32)
    block = 128
    step = pl.program_id(0)

    def leave(half, start):
        lines = pl.ds(start, 2 * block)
        return pltpu.make_async_copy(
            held_ref.at[half, lines],
            exp_ref.at[2 * (step + (shift or 0)) + half, lines],
            left_ref.at[half, start // (2 * block)],
        )

    results = []
    for half in range(2):
        left = side((rows, PAIR), 1, half, scaled, 1.0).astype(BF)
        place = lax.broadcasted_iota(jnp.int32, (PAIR, rows), 0)
        right = jnp.where(place == (HEAD_DIM if half == 0 else 0), bias, key_wide).astype(BF)
        for start in range(0, rows, block):
            scores = dot(left[start : start + block], right, 1, 0)
            highest = jnp.max(scores, 1, keepdims=True)
            held_ref[half, start : start + block, :] = jnp.exp(scores - highest).astype(BF)
            if start % (2 * block):
                leave(half, start - block).start()
        values = side((rows, PAIR), 1, half, value_wide, 1.0).astype(BF)
        total = dot(held_ref[half], values, 1, 0)
        flag = HEAD_DIM if half == 0 else 0
        inverse = 1.0 / total[:, flag : flag + 1]
        results.append((total * inverse, inverse))
    low = lax.broadcasted_iota(jnp.int32, (rows, PAIR), 1) < HEAD_DIM
    context = jnp.where(low, results[0][0], results[1][0])
    mark_ref[...] = jnp.zeros_like(mark_ref)
    wide_ref[...] = context
    context_ref[...] = context.astype(BF)
    inverse_ref[...] = jnp.where(low, results[0][1], results[1][1])
    for half in range(2):
        for start in range(0, rows, 2 * block):
            leave(half, start).wait()


def attend(info, tokens, sources, start, pairs, vectors=None, held=(), after=()):
    rows = tokens.shape[0]
    first = vectors is None
    width = (4 if first else 12) * PAIR
    tall = lambda: pl.BlockSpec((rows, PAIR), lambda p: (0, start + p))
    flat = lambda: pl.BlockSpec((PAIR, rows), lambda p: (start + p, 0))
    array = lambda kind: jax.ShapeDtypeStruct((rows, WIDTH), kind)
    turned = jax.ShapeDtypeStruct((WIDTH, rows), BF)
    fixed = lambda *shape: pl.BlockSpec(shape, lambda p: (0, 0))
    table, mark = (16, BLOCKS * BLOCK), (8, 128)
    inputs = (info, tokens, *sources, *(() if first else (vectors,)))
    return call_with(
        functools.partial(attend_kernel, None if first else start),
        inputs,
        (*held, *after),
        grid=(pairs,),
        in_specs=[SMEM, WHOLE] + [WHOLE] * len(sources) + ([] if first else [fixed(*table)]),
        out_specs=[IDLE, tall(), tall(), tall(), flat(), tall(), flat()]
        + ([fixed(*table)] if first else [])
        + [fixed(*mark)],
        out_shape=[
            jax.ShapeDtypeStruct((2 * PAIRS, rows, rows), BF),
            array(BF), array(F32), array(F32), turned, array(BF), turned,
        ]
        + ([jax.ShapeDtypeStruct(table, F32)] if first else [])
        + [jax.ShapeDtypeStruct(mark, F32)],
        input_output_aliases={len(inputs) + i: i for i in range(len(held))},
        scratch_shapes=[
            pltpu.VMEM((BLOCKS * BLOCK, width), BF),
            pltpu.VMEM((2, rows, rows), BF),
            pltpu.SemaphoreType.DMA((2, rows // 256)),
        ],
        cost_estimate=cost(8 * pairs),
    )


def gelu_pair(values):
    t = 1.0 / (1.0 + (0.3275911 * 0.5**0.5) * jnp.abs(values))
    bell = jnp.exp(-0.5 * values * values)
    tail = t * (0.5 * 0.254829592 + t * (0.5 * -0.284496736 + t * (0.5 * 1.421413741 + t * (
        0.5 * -1.453152027 + t * (0.5 * 1.061405429)))))
    tail = tail * bell
    share = jnp.where(values >= 0.0, 1.0 - tail, tail)
    return values * share, share + values * bell * 0.3989422804014327


def row_mean(values):
    return jnp.sum(values, 1, keepdims=True) * (1.0 / WIDTH)


def column_sum(values):
    return jnp.sum(values, 0, keepdims=True)


def row_mean(values):
    return jnp.sum(values, 1, keepdims=True) * (1.0 / WIDTH)


def column_sum(values):
    return jnp.sum(values, 0, keepdims=True)


def up_places():
    for block in range(HIDDEN_PAD // (QUARTERS * BLOCK)):
        for quarter in range(QUARTERS):
            start = (block * QUARTERS + quarter) * BLOCK
            row = slice(8 + quarter, 9 + quarter)
            yield slice(start, start + BLOCK), row, slice(block * BLOCK, (block + 1) * BLOCK)


def feed_kernel(
    info_ref, context_in_ref, token_ref, cotangent_ref, *refs
):
    sources, refs = refs[:2], refs[2:]
    (
        down_ref, vector_ref,
        output_ref, first_ref, grad_context_ref, sums_ref, b1_sum_ref, down_term_ref, keep_ref,
        send_ref, w1_ref, w2_ref, b1_ref, product_ref,
        context_ref, normed_ref, active_ref, hidden_ref, feed_ref, branch_ref, came_ref,
    ) = refs
    step = pl.program_id(0)
    rows = token_ref.shape[0]

    @pl.when(step == 0)
    def _():
        core, layer = info_ref[CORE], info_ref[LAYER]
        copies = []
        for quarter in range(QUARTERS):
            columns = slice(quarter * UP_PART, (quarter + 1) * UP_PART)
            for slot in range(LAYERS):
                source = (layer + LAYERS - slot) % LAYERS
                for twin, ref in enumerate(sources):
                    block = 2 * source + (1 - core if twin else core)
                    target = w1_ref.at[rows_of(block), columns]
                    number = (quarter * LAYERS + slot) * 2 + twin
                    copies.append(
                        pltpu.make_async_copy(ref.at[quarter, slot], target, came_ref.at[number])
                    )
        lower = pltpu.make_async_copy(
            down_ref.at[:HIDDEN_PAD], w2_ref, came_ref.at[2 * QUARTERS * LAYERS]
        )
        copies.append(lower)
        for copy in copies:
            copy.start()
        for copy in copies:
            copy.wait()
        last = slice(HIDDEN_PAD - PAIR, HIDDEN_PAD)
        lane = lax.broadcasted_iota(jnp.int32, (BLOCKS * BLOCK, PAIR), 1)
        kept = lane < HIDDEN_SIZE - (HIDDEN_PAD - PAIR)
        w1_ref[:, last] = jnp.where(kept, w1_ref[:, last].astype(F32), 0.0).astype(BF)
        w2_ref[HIDDEN_SIZE:, :] = jnp.zeros((HIDDEN_PAD - HIDDEN_SIZE, WIDTH), BF)
        for place, row, columns in up_places():
            b1_ref[:, place] = vector_ref[row, columns]
        lane = lax.broadcasted_iota(jnp.int32, (1, HIDDEN_PAD), 1)
        b1_ref[...] = jnp.where(lane < HIDDEN_SIZE, b1_ref[...], 0.0)
        w2_ref[HIDDEN_SIZE:, :] = jnp.zeros((HIDDEN_PAD - HIDDEN_SIZE, WIDTH), BF)

    steps = normed_ref.shape[0] // rows
    down_steps = HIDDEN_PAD // UP_PART

    @pl.when(step < steps)
    def _():
        here = pl.ds(pl.multiple_of(step * rows, rows), rows)
        wo = w1_ref[:WIDTH, HIDDEN_PAD : HIDDEN_PAD + WIDTH]
        w1, w2 = w1_ref[:WIDTH, :HIDDEN_PAD], w2_ref[...]
        place = lax.broadcasted_iota(jnp.int32, (rows, 1), 0) + step * rows
        live = jnp.where(place < info_ref[LENGTH], 1.0, 0.0)
        vector = lambda i: vector_ref[i : i + 1, :WIDTH]
        out_add, down_add = vector(2), vector(3)
        gain_one, shift_one, gain_two, shift_two = vector(4), vector(5), vector(6), vector(7)
        context = context_in_ref[...]
        context_ref[here, :] = context
        first_sum = token_ref[...].astype(F32) + dot(context, wo, 1, 0) + out_add
        center = first_sum - row_mean(first_sum)
        rate_one = lax.rsqrt(row_mean(center * center) + EPSILON)
        unit_one = center * rate_one
        normed = (unit_one * gain_one + shift_one).astype(BF)
        normed_ref[here, :] = normed
        pre = dot(normed, w1, 1, 0) + b1_ref[...]
        active_full, slope = gelu_pair(pre)
        active = active_full.astype(BF)
        active_ref[here, :] = active
        second_sum = normed.astype(F32) + dot(active, w2, 1, 0) + down_add
        center = second_sum - row_mean(second_sum)
        rate_two = lax.rsqrt(row_mean(center * center) + EPSILON)
        unit_two = center * rate_two
        output_ref[...] = ((unit_two * gain_two + shift_two) * live).astype(BF)
        cotangent = cotangent_ref[...].astype(F32) * live
        inner = cotangent * gain_two
        grad_second = rate_two * (inner - row_mean(inner) - unit_two * row_mean(inner * unit_two))
        grad_feed = grad_second.astype(BF)
        feed_ref[here, :] = grad_feed
        grad_hidden = (dot(grad_feed, w2, 1, 1) * slope).astype(BF)
        hidden_ref[here, :] = grad_hidden
        grad_normed = grad_second + dot(grad_hidden, w1, 1, 1)
        inner = grad_normed * gain_one
        grad_first = rate_one * (inner - row_mean(inner) - unit_one * row_mean(inner * unit_one))
        first_ref[...] = grad_first
        grad_branch = grad_first.astype(BF)
        branch_ref[here, :] = grad_branch
        grad_context_ref[...] = dot(grad_branch, wo, 1, 1).astype(BF)
        sums = jnp.concatenate(
            [
                column_sum(grad_branch.astype(F32)),
                column_sum(grad_feed.astype(F32)),
                column_sum(grad_normed * unit_one),
                column_sum(grad_normed),
                column_sum(cotangent * unit_two),
                column_sum(cotangent),
                jnp.zeros((2, WIDTH), F32),
            ],
            axis=0,
        )
        b1_sum = column_sum(grad_hidden.astype(F32))

        @pl.when(step == 0)
        def _():
            sums_ref[...] = sums
            b1_sum_ref[...] = b1_sum

        @pl.when(step > 0)
        def _():
            sums_ref[...] += sums
            b1_sum_ref[...] += b1_sum

    @pl.when((step >= steps) & (step < steps + down_steps))
    def _():
        place = pl.ds(pl.multiple_of((step - steps) * UP_PART, UP_PART), UP_PART)
        down_term_ref[...] = dot(active_ref[:, place], feed_ref[...], 0, 0).astype(BF)

    @pl.when(step >= steps + down_steps)
    def _():
        part = step - steps - down_steps

        @pl.when(part == 0)
        def _():
            product_ref[WIDTH:, :] = jnp.zeros((BLOCKS * BLOCK - WIDTH, UP_PART), F32)

        @pl.when(part < QUARTERS - 1)
        def _():
            place = pl.ds(pl.multiple_of(part * UP_PART, UP_PART), UP_PART)
            product_ref[:WIDTH, :] = dot(normed_ref[...], hidden_ref[:, place], 0, 0)

        @pl.when(part == QUARTERS - 1)
        def _():
            product_ref[:WIDTH, :WIDTH] = dot(context_ref[...], branch_ref[...], 0, 0)

        deal(info_ref, product_ref, keep_ref, send_ref)


def feed(info, context, tokens, cotangent, wide, down, vectors, after=()):
    rows = tokens.shape[0]
    tile = rows // 4
    steps = rows // tile
    down_steps = HIDDEN_PAD // UP_PART
    part = lambda width: pl.BlockSpec((tile, width), lambda i: (jnp.minimum(i, steps - 1), 0))
    whole = lambda *shape: pl.BlockSpec(shape, lambda i: (0, 0))
    array = lambda width, kind: jax.ShapeDtypeStruct((rows, width), kind)
    held = lambda width: pltpu.VMEM((rows, width), BF)
    place = lambda: pl.BlockSpec(
        (1, LAYERS, BLOCK, UP_PART),
        lambda i: (jnp.clip(i - steps - down_steps, 0, QUARTERS - 1), 0, 0, 0),
    )
    shared = jax.ShapeDtypeStruct((QUARTERS, LAYERS, BLOCK, UP_PART), BF)
    return call_with(
        feed_kernel, (info, context, tokens, cotangent, *wide, down, vectors), after,
        grid=(steps + down_steps + QUARTERS,),
        in_specs=[SMEM]
        + [part(WIDTH), part(WIDTH), part(WIDTH)]
        + [IDLE] * (len(wide) + 1)
        + [whole(*vectors.shape)],
        out_specs=[
            part(WIDTH), part(WIDTH), part(WIDTH), whole(8, WIDTH), whole(1, HIDDEN_PAD),
            pl.BlockSpec((UP_PART, WIDTH), lambda i: (jnp.clip(i - steps, 0, down_steps - 1), 0)),
            place(), place(),
        ],
        out_shape=[
            array(WIDTH, BF), array(WIDTH, F32), array(WIDTH, BF),
            jax.ShapeDtypeStruct((8, WIDTH), F32),
            jax.ShapeDtypeStruct((1, HIDDEN_PAD), F32),
            jax.ShapeDtypeStruct((down.shape[0], WIDTH), BF),
            shared, shared,
        ],
        scratch_shapes=[
            pltpu.VMEM((BLOCKS * BLOCK, QUARTERS * UP_PART), BF),
            pltpu.VMEM((HIDDEN_PAD, WIDTH), BF),
            pltpu.VMEM((1, HIDDEN_PAD), F32),
            pltpu.VMEM((BLOCKS * BLOCK, UP_PART), F32),
            held(WIDTH), held(WIDTH), held(HIDDEN_PAD), held(HIDDEN_PAD), held(WIDTH), held(WIDTH),
            pltpu.SemaphoreType.DMA((2 * QUARTERS * LAYERS + 1,)),
        ],
        cost_estimate=cost(50),
    )


def deal(info_ref, product_ref, keep_ref, send_ref):
    core = info_ref[CORE]
    for layer in range(LAYERS):
        keep_ref[0, layer] = product_ref[rows_of(2 * layer + core), :].astype(BF)
        send_ref[0, layer] = product_ref[rows_of(2 * layer + 1 - core), :].astype(BF)


def head_grad_kernel(
    info_ref, token_t_ref, together_ref, first_ref, sums_ref, up_sum_ref, pair_ref,
    keep_ref, send_ref, product_ref, table_ref,
):
    step = pl.program_id(0)

    @pl.when(step < QUARTERS - 1)
    def _():
        part = first_ref[0, :, pl.ds(pl.multiple_of(step * PAIR, PAIR), PAIR)]
        both = jnp.concatenate([together_ref[0], part], axis=1)
        product_ref[...] = dot(token_t_ref[...], both, 1, 0)

    @pl.when(step == QUARTERS - 1)
    def _():
        product_ref[:, : 3 * PAIR] = dot(token_t_ref[...], together_ref[0], 1, 0)
        table_ref[...] = jnp.zeros_like(table_ref)
        table_ref[0:2, :WIDTH] = pair_ref[0:2, :]
        table_ref[2:8, :WIDTH] = sums_ref[0:6, :]
        for place, row, columns in up_places():
            table_ref[row, columns] = up_sum_ref[:, place]
        product_ref[:, 3 * PAIR :] = table_ref[...].T

    deal(info_ref, product_ref, keep_ref, send_ref)


def head_grad(info, token_t, together, sums, up_sum, pair_sums, after=()):
    rows = token_t.shape[1]
    place = lambda: pl.BlockSpec((1, LAYERS, BLOCK, 4 * PAIR), lambda d: (d, 0, 0, 0))
    array = jax.ShapeDtypeStruct((QUARTERS, LAYERS, BLOCK, 4 * PAIR), BF)
    return call_with(
        head_grad_kernel, (info, token_t, together, together, sums, up_sum, pair_sums), after,
        grid=(QUARTERS,),
        in_specs=[
            SMEM, WHOLE,
            pl.BlockSpec((1, rows, 3 * PAIR), lambda d: (d + 1, 0, 0)),
            pl.BlockSpec((1, rows, 3 * PAIR), lambda d: (0, 0, 0)),
            WHOLE, WHOLE, WHOLE,
        ],
        out_specs=[place(), place()],
        out_shape=[array, array],
        scratch_shapes=[
            pltpu.VMEM((BLOCKS * BLOCK, 4 * PAIR), F32),
            pltpu.VMEM((PAIR, BLOCKS * BLOCK), F32),
        ],
        cost_estimate=cost(8),
    )


def meet_kernel(info_ref, keep_ref, came_ref, *out_refs):
    for apart in range(QUARTERS):
        quarter = info_ref[PART] ^ apart
        out_refs[apart][0] = keep_ref[quarter, 0] + came_ref[quarter, 0]


def meet(info, keep, came, after=()):
    width = keep.shape[-1]
    block = lambda: pl.BlockSpec(
        (QUARTERS, 1, BLOCK, width), lambda s, info: (0, (info[LAYER] + s) % LAYERS, 0, 0)
    )

    def run(info_ref, keep_ref, came_ref, *refs):
        meet_kernel(info_ref, keep_ref, came_ref, *refs[len(after) :])

    return pl.pallas_call(
        run,
        grid_spec=pltpu.PrefetchScalarGridSpec(
            num_scalar_prefetch=1,
            grid=(LAYERS,),
            in_specs=[block(), block()] + [IDLE] * len(after),
            out_specs=[pl.BlockSpec((1, BLOCK, width), lambda s, info: (s, 0, 0))] * QUARTERS,
        ),
        out_shape=[jax.ShapeDtypeStruct((LAYERS, BLOCK, width), BF)] * QUARTERS,
        compiler_params=params(),
        cost_estimate=cost(3),
    )(info, keep, came, *after)


def attend_back_kernel(
    grad_ref, wide_ref, inverse_ref, exp_ref, query_t_ref, key_ref, value_t_ref,
    together_ref, sums_ref, score_ref,
):
    rows = grad_ref.shape[0]
    inverse = inverse_ref[...]
    grad = grad_ref[...].astype(F32)
    scaled = grad * inverse
    dots = scaled * wide_ref[...]
    scaled_t = scaled.T.astype(BF)
    value_wide = value_t_ref[...].astype(F32)
    lane = lax.broadcasted_iota(jnp.int32, (rows, PAIR), 1)
    place = lax.broadcasted_iota(jnp.int32, (PAIR, rows), 0)
    block = 128
    dq, dk_t, dv_t = [], [], []
    for half in range(2):
        mine = (lane < HEAD_DIM) if half == 0 else (lane >= HEAD_DIM)
        flag = HEAD_DIM if half == 0 else 0
        offset = jnp.sum(jnp.where(mine, -dots, 0.0), 1, keepdims=True)
        high = offset.astype(BF).astype(F32)
        rest = offset - high
        left = jnp.where(
            mine, scaled, jnp.where(lane == flag, high, jnp.where(lane == flag + 1, rest, 0.0))
        ).astype(BF)
        right = jnp.where((place == flag) | (place == flag + 1), 1.0, value_wide).astype(BF)
        for start in range(0, rows, block):
            grad_probs = dot(left[start : start + block], right, 1, 0)
            weight = exp_ref[half, start : start + block, :].astype(F32)
            score_ref[half, start : start + block, :] = (grad_probs * weight).astype(BF)
        own = slice(half * HEAD_DIM, (half + 1) * HEAD_DIM)
        dv_t.append(dot(scaled_t[own], exp_ref[half], 1, 0))
        dk_t.append(dot(query_t_ref[own, :], score_ref[half], 1, 0))
        dq.append(dot(score_ref[half], key_ref[...], 1, 0))
    factor = HEAD_DIM**-0.5
    dq_low = (jnp.where(lane < HEAD_DIM, dq[0], dq[1]) * factor).astype(BF)
    dk_low = (jnp.concatenate(dk_t, axis=0) * factor).T.astype(BF)
    dv_low = jnp.concatenate(dv_t, axis=0).T.astype(BF)
    together_ref[0] = jnp.concatenate([dq_low, dk_low, dv_low], axis=1)
    query_sum = column_sum(dq_low.astype(F32))
    value_sum = column_sum(dv_low.astype(F32))
    sums_ref[...] = jnp.concatenate([query_sum, value_sum, jnp.zeros((6, PAIR), F32)], axis=0)


def attend_back(grad_context, saved, start, pairs, after=()):
    exps, wide, inverse, query_t, key, value_t = saved
    rows = grad_context.shape[0]
    tall = lambda: pl.BlockSpec((rows, PAIR), lambda p: (0, start + p))
    flat = lambda: pl.BlockSpec((PAIR, rows), lambda p: (start + p, 0))
    return call_with(
        attend_back_kernel,
        (grad_context, wide, inverse, exps, query_t, key, value_t),
        after,
        grid=(pairs,),
        in_specs=[
            tall(), tall(), tall(),
            pl.BlockSpec((2, rows, rows), lambda p: (start + p, 0, 0)),
            flat(), tall(), flat(),
        ],
        out_specs=[
            pl.BlockSpec((1, rows, 3 * PAIR), lambda p: (p, 0, 0)),
            pl.BlockSpec((8, PAIR), lambda p: (0, p)),
        ],
        out_shape=[
            jax.ShapeDtypeStruct((pairs, rows, 3 * PAIR), BF),
            jax.ShapeDtypeStruct((8, pairs * PAIR), F32),
        ],
        scratch_shapes=[pltpu.VMEM((2, rows, rows), BF)],
        cost_estimate=cost(8 * pairs),
    )


def token_kernel(info_ref, grad_ref, together_ref, *refs):
    count = 4
    first_sources, rest_sources = refs[:count], refs[count : count + 2]
    out_ref, first_ref, rest_ref = refs[-3:]

    @pl.when(pl.program_id(0) == 0)
    def _():
        lay_line(info_ref, first_ref, *first_sources)
        lay(info_ref, rest_ref, 3 * PAIR, *rest_sources)

    pieces = [together_ref[i] for i in range(1, PAIRS)]
    total = grad_ref[...] + dot(together_ref[0], first_ref[:WIDTH, : 3 * PAIR], 1, 1)
    total += dot(jnp.concatenate(pieces, axis=1), rest_ref[:WIDTH, :], 1, 1)
    out_ref[...] = total.astype(BF)


def token_back(info, grad_first, together, first, rest, after):
    rows = grad_first.shape[0]
    tile = 256
    part = pl.BlockSpec((tile, WIDTH), lambda i: (i, 0))
    piece = pl.BlockSpec((PAIRS, tile, 3 * PAIR), lambda i: (0, i, 0))
    return call_with(
        token_kernel, (info, grad_first, together, *first, *rest), after,
        grid=(rows // tile,),
        in_specs=[SMEM, part, piece]
        + [WHOLE] * (len(first) + len(rest)),
        out_specs=part,
        out_shape=jax.ShapeDtypeStruct((rows, WIDTH), BF),
        scratch_shapes=[
            pltpu.VMEM((BLOCKS * BLOCK, 4 * PAIR), BF),
            pltpu.VMEM((BLOCKS * BLOCK, 12 * PAIR), BF),
        ],
        cost_estimate=cost(7),
    )


def plane_kernel(groups, *refs):
    inputs, outputs = refs[: groups * QUARTERS], refs[groups * QUARTERS :]
    start = 0
    for group in range(groups):
        mine = inputs[group * QUARTERS : (group + 1) * QUARTERS]
        width = mine[0].shape[-1]
        for step in range(LAYERS):
            total = sum(ref[step].astype(F32) for ref in mine)
            outputs[step][:, start : start + width] = total.astype(BF)
        start += width


def plane(groups, after=()):
    width = sum(group[0].shape[-1] for group in groups)
    return call_with(
        functools.partial(plane_kernel, len(groups)),
        tuple(array for group in groups for array in group),
        after,
        in_specs=[WHOLE] * (len(groups) * QUARTERS),
        out_specs=[WHOLE] * LAYERS,
        out_shape=[jax.ShapeDtypeStruct((BLOCK, width), BF)] * LAYERS,
        cost_estimate=cost(2),
    )


def plane_stack_kernel(info_ref, *refs):
    for step in range(LAYERS):
        total = sum(ref[step].astype(F32) for ref in refs[:-1])
        refs[-1][(info_ref[LAYER] + step) % LAYERS] = total.astype(BF)


def plane_stack(info, parts, after=()):
    return call_with(
        plane_stack_kernel, (info, *parts), after,
        in_specs=[SMEM] + [WHOLE] * len(parts),
        out_specs=WHOLE,
        out_shape=jax.ShapeDtypeStruct(parts[0].shape, BF),
        cost_estimate=cost(2),
    )


def line_kernel(counts, *refs):
    inputs, out_ref = refs[:-1], refs[-1]
    start = 0
    for count in counts:
        mine, inputs = inputs[:count], inputs[count:]
        width = mine[0].shape[-1]
        parts = [ref[...] for ref in mine] if count > 1 else [mine[0][i] for i in range(QUARTERS)]
        total = sum(part.astype(F32) for part in parts).astype(BF)
        for copy in range(out_ref.shape[0]):
            out_ref[copy, :, start : start + width] = total
        start += width


def line(groups, copies=QUARTERS, after=()):
    width = sum(group[0].shape[-1] for group in groups)
    arrays = tuple(array for group in groups for array in group)
    return call_with(
        functools.partial(line_kernel, [len(group) for group in groups]), arrays, after,
        in_specs=[WHOLE] * len(arrays),
        out_specs=WHOLE,
        out_shape=jax.ShapeDtypeStruct((copies, BLOCK, width), BF),
        cost_estimate=cost(1),
    )


def finish_wide_kernel(info_ref, wide_ref, wo_ref, up_ref, down_ref):
    extra = wo_ref.shape[1] - WIDTH
    blank = jnp.zeros((BLOCK, extra), F32)
    used = HIDDEN_PAD // (QUARTERS * BLOCK)
    owner = 2 * info_ref[LAYER] + info_ref[CORE]
    for quarter in range(QUARTERS):
        lines = slice(quarter * BLOCK, (quarter + 1) * BLOCK)
        down = wide_ref[quarter, :, UP_PART:].astype(F32)
        down_ref[lines, :WIDTH] = jnp.where(owner < used, down, 0.0)
        down_ref[lines, WIDTH:] = blank
    for quarter in range(QUARTERS - 1):
        columns = slice(quarter * UP_PART, (quarter + 1) * UP_PART)
        up_ref[:, columns] = wide_ref[quarter, :, :UP_PART].astype(F32)
    up_ref[:, HIDDEN_PAD:] = jnp.zeros((BLOCK, up_ref.shape[1] - HIDDEN_PAD), F32)
    wo_ref[:, :WIDTH] = wide_ref[QUARTERS - 1, :, :WIDTH].astype(F32)
    wo_ref[:, WIDTH:] = blank


def finish_wide(info, wide, super_width, super_hidden, after=()):
    array = lambda *shape: jax.ShapeDtypeStruct(shape, F32)
    return call_with(
        finish_wide_kernel, (info, wide), after,
        in_specs=[SMEM, WHOLE],
        out_specs=[WHOLE] * 3,
        out_shape=[
            array(BLOCK, super_width), array(BLOCK, super_hidden),
            array(QUARTERS * BLOCK, super_width),
        ],
        cost_estimate=cost(3),
    )


def finish_heads_kernel(info_ref, *refs):
    parts, three, line_refs = refs[:QUARTERS], refs[4:7], refs[7:15]
    up_line_ref, heads_ref = refs[15:]
    for apart, ref in enumerate(parts):
        heads_ref[info_ref[PART] ^ apart] = ref[...].astype(F32)
    for i, ref in enumerate(three):
        ref[:, :PAIR] = heads_ref[i, :, 3 * PAIR :]
        for pair in range(1, PAIRS):
            part = heads_ref[pair - 1, :, i * PAIR : (i + 1) * PAIR]
            ref[:, pair * PAIR : (pair + 1) * PAIR] = part
        ref[:, WIDTH:] = jnp.zeros((BLOCK, ref.shape[1] - WIDTH), F32)
    lines = heads_ref[QUARTERS - 1, :, 3 * PAIR :].T
    for i, ref in enumerate(line_refs):
        ref[...] = lines[i]
    for i in range(QUARTERS):
        up_line_ref[i * BLOCK : (i + 1) * BLOCK] = lines[8 + i]


def finish_heads(info, parts, super_width, after=()):
    array = lambda *shape: jax.ShapeDtypeStruct(shape, F32)
    return call_with(
        finish_heads_kernel, (info, *parts), after,
        in_specs=[SMEM] + [WHOLE] * QUARTERS,
        out_specs=[WHOLE] * 12,
        out_shape=[array(BLOCK, super_width)] * 3
        + [array(BLOCK)] * 8
        + [array(QUARTERS * BLOCK)],
        scratch_shapes=[pltpu.VMEM((QUARTERS, BLOCK, 4 * PAIR), F32)],
        cost_estimate=cost(2),
    )


SWAP = [(i, i ^ 1) for i in range(BLOCKS)]
STEPS = range(1, LAYERS)
DISTANCES = range(1, QUARTERS)


def twin(part):
    return lax.ppermute(part, "fsdp", SWAP)


def along(part, step):
    pairs = [(i, (i + 2 * step) % BLOCKS) for i in range(BLOCKS)]
    return lax.ppermute(part, "fsdp", pairs)


LINES = [[2 * layer + core for layer in range(LAYERS)] for core in range(2)]


def trade_plane(parts):
    return lax.all_to_all(parts, "dp", 0, 0)


def trade_line(parts):
    return lax.all_to_all(parts, "fsdp", 0, 0, axis_index_groups=LINES)


def copies(part):
    return jnp.broadcast_to(part[None], (QUARTERS,) + part.shape)


def across(part, apart):
    return lax.ppermute(part, "dp", [(i, i ^ apart) for i in range(QUARTERS)])


def drop(saved):
    return (saved[0],) + tuple(saved[2:])


def on_device(
    tokens, lengths, query_weight, key_weight, value_weight, out_weight, up_weight, down_weight,
    query_bias, value_bias, out_bias, up_bias, down_bias, first_gain, first_shift, second_gain,
    second_shift, cotangent,
):
    super_width, super_hidden = query_weight.shape[1], up_weight.shape[1]
    index = lax.axis_index("fsdp").astype(jnp.int32)
    part = lax.axis_index("dp").astype(jnp.int32)
    info = jnp.stack([lengths[0], index % 2, part, index // 2])
    qkv = (query_weight, key_weight, value_weight)
    small = (
        query_bias, value_bias, out_bias, down_bias,
        first_gain, first_shift, second_gain, second_shift, up_bias,
    )
    first_own = pack(pack_first_kernel, info, qkv + small, (BLOCK, 7 * PAIR))
    first_came = [along(first_own, step) for step in STEPS]
    wide_own = pack(
        pack_wide_kernel, info, (up_weight, out_weight), (BLOCK, UP_PART), after=(first_own,)
    )
    first_line, rest_copies = join(first_own, first_came, after=(wide_own,))
    first = (first_own, twin(first_own), first_line, twin(first_line))
    rest_mine = trade_plane(rest_copies)
    down_cut = cut(down_weight, after=(wide_own, *first))
    wide_line = [wide_own] + [along(wide_own, step) for step in STEPS]
    down = lax.all_gather(down_cut, "fsdp", axis=0, tiled=True)
    *saved, vectors, mark = attend(info, tokens, first, 0, 1, after=(down_cut,))
    rest = (rest_mine, twin(rest_mine))
    wide_mine = trade_plane(repeat(wide_line, after=(mark,)))
    *saved, mark = attend(info, tokens, rest, 1, 3, vectors, saved, after=wide_line)
    wide_mine, mark = lax.optimization_barrier((wide_mine, mark))
    wide = (wide_mine, twin(wide_mine))
    *saved, mark = attend(info, tokens, rest, 4, 1, vectors, saved, after=(wide_mine, mark))
    (
        output, grad_first, grad_context, sums, up_sum, down_term, up_keep, up_send
    ) = feed(info, saved[1], tokens, cotangent, wide, down, vectors)
    down_total = lax.psum_scatter(down_term, "fsdp", scatter_dimension=0, tiled=True)
    token_t = turn(tokens, after=(up_keep,))
    up_near = meet(info, up_keep, twin(up_send), after=(token_t,))
    send = lambda near: [near[0]] + [across(near[apart], apart) for apart in DISTANCES]
    pass_on = lambda layers: [layers[0]] + [along(layers[step], step) for step in STEPS]
    up_plane = send(up_near)
    together, pair_sums = attend_back(grad_context, drop(saved), 0, PAIRS, after=(up_near[0],))
    head_keep, head_send = head_grad(
        info, token_t, together, sums, up_sum, pair_sums, after=up_plane[1:]
    )
    down_plane = trade_plane(down_total.reshape(QUARTERS, BLOCK, WIDTH))
    head_near = meet(info, head_keep, twin(head_send))
    head_plane = send(head_near)
    up_layers = plane_stack(info, up_plane, after=(head_near[0], down_plane))
    up_line = trade_line(up_layers)
    layers = plane([head_plane], after=(up_layers,))
    head_line = pass_on(layers)
    token_grad = token_back(info, grad_first, together, first, rest, (layers[0],))
    wide_copies = line([[up_line], [down_plane]], after=(token_grad, *head_line[1:]))
    wide_total = trade_plane(wide_copies)
    head_total = line([head_line], 1, after=(token_grad,)).reshape(BLOCK, 4 * PAIR)
    head_parts = send([head_total] * QUARTERS)
    *results, up_line = finish_heads(info, head_parts, super_width)
    heads, lines = results[:3], results[3:]
    wo, up, down = finish_wide(info, wide_total, super_width, super_hidden, after=(heads[0],))
    order = lines[:3] + [up_line] + lines[3:]
    return (output, token_grad, *heads, wo, up, down, *order)


def widen(matrix, row_count, column_count):
    return jnp.pad(matrix, ((0, row_count - matrix.shape[0]), (0, column_count - matrix.shape[1])))


def on_device_elsewhere(
    tokens, lengths, query_weight, key_weight, value_weight, out_weight, up_weight, down_weight,
    query_bias, value_bias, out_bias, up_bias, down_bias, first_gain, first_shift, second_gain,
    second_shift, cotangent,
):
    owned, super_width = query_weight.shape
    super_hidden = up_weight.shape[1]
    info = jnp.stack([lengths[0]] + [jnp.zeros((), jnp.int32)] * 3)
    gather = lambda array: lax.all_gather(array, "fsdp", axis=0, tiled=True)
    qkv = [gather(array) for array in (query_weight, key_weight, value_weight)]
    lines = [
        gather(array)
        for array in (
            query_bias, value_bias, out_bias, down_bias,
            first_gain, first_shift, second_gain, second_shift,
        )
    ]
    up_lines = gather(up_bias).reshape(BLOCKS, QUARTERS, BLOCK).transpose(1, 0, 2)
    lines = jnp.concatenate([jnp.stack(lines), up_lines.reshape(QUARTERS, -1)], axis=0)
    columns = jnp.pad(lines, ((0, PAIR - lines.shape[0]), (0, 0))).T
    first_full = jnp.concatenate([array[:, :PAIR] for array in qkv] + [columns], axis=1)
    places = [slice(pair * PAIR, (pair + 1) * PAIR) for pair in range(1, PAIRS)]
    rest_full = jnp.concatenate([array[:, place] for place in places for array in qkv], axis=1)
    wide_full = jnp.concatenate([gather(up_weight)[:, :HIDDEN_PAD], gather(out_weight)], axis=1)
    down = gather(down_weight)[:, :WIDTH]

    back = [(LAYERS - slot) % LAYERS for slot in range(LAYERS)]

    def pieces(full):
        blocks = full.reshape(LAYERS, 2, BLOCK, QUARTERS, -1).transpose(0, 1, 3, 2, 4)
        blocks = jnp.stack([blocks[layer] for layer in back], axis=2)
        return blocks[0], blocks[1]

    blocks = first_full.reshape(LAYERS, 2, BLOCK, -1)
    blocks = jnp.stack([blocks[layer] for layer in back])
    first = (blocks[0, 0], blocks[0, 1], blocks[1:, 0], blocks[1:, 1])
    rest, wide = pieces(rest_full), pieces(wide_full)
    token_t = turn(tokens)
    *saved, vectors, mark = attend(info, tokens, first, 0, 1)
    *saved, mark = attend(info, tokens, rest, 1, 4, vectors, saved)
    (
        output, grad_first, grad_context, sums, up_sum, down_term, *up_parts
    ) = feed(info, saved[1], tokens, cotangent, wide, down, vectors)
    deep = lax.broadcasted_iota(jnp.int32, (super_hidden, 1), 0)
    down_term = jnp.where(deep < HIDDEN_PAD, down_term, 0.0)
    together, pair_sums = attend_back(grad_context, drop(saved), 0, PAIRS)

    def both(parts):
        return jnp.stack(parts, axis=2).transpose(1, 2, 3, 0, 4).reshape(super_width, -1)

    def total(array):
        array = lax.psum_scatter(array, "fsdp", scatter_dimension=0, tiled=True)
        return lax.psum(array, "dp").astype(F32)

    wide_total = total(both(up_parts))
    heads_total = total(both(head_grad(info, token_t, together, sums, up_sum, pair_sums)))
    heads_total = heads_total.reshape(owned, QUARTERS, 4 * PAIR)
    first_total = heads_total[:, :, 3 * PAIR :].reshape(owned, 4 * PAIR)
    heads_total = heads_total[:, :, : 3 * PAIR].reshape(owned, PAIRS - 1, 3, PAIR)
    down_total = total(down_term)
    token_grad = token_back(
        info, grad_first, together, first, rest, ()
    )
    full = lambda matrix: widen(matrix, owned, super_width)
    heads = [
        full(
            jnp.concatenate(
                [first_total[:, i * PAIR : (i + 1) * PAIR], heads_total[:, :, i].reshape(owned, -1)],
                axis=1,
            )
        )
        for i in range(3)
    ]
    lines = gather(first_total[:, 3 * PAIR :]).T
    up_lines = lines[8:12].reshape(QUARTERS, BLOCKS, BLOCK).transpose(1, 0, 2).reshape(-1)
    place = lax.axis_index("fsdp")
    mine = lambda array: lax.dynamic_slice_in_dim(array, place * owned, owned)
    deep = up_bias.shape[0]
    return (
        output, token_grad, *heads,
        full(wide_total[:, HIDDEN_PAD : HIDDEN_PAD + WIDTH]),
        widen(wide_total[:, :HIDDEN_PAD], owned, super_hidden),
        widen(down_total, deep, super_width),
        mine(lines[0]), mine(lines[1]), mine(lines[2]),
        lax.dynamic_slice_in_dim(up_lines, place * deep, deep),
        mine(lines[3]), mine(lines[4]), mine(lines[5]), mine(lines[6]), mine(lines[7]),
    )


def solution(mesh):
    rows = P(("dp", "fsdp"), None)
    held = P("fsdp", None)
    line = P("fsdp")
    near = mesh.shape["dp"] == QUARTERS and mesh.shape["fsdp"] == BLOCKS
    return jax.shard_map(
        on_device if near else on_device_elsewhere,
        mesh=mesh,
        in_specs=(rows, P(("dp", "fsdp"))) + (held,) * 6 + (line,) * 9 + (rows,),
        out_specs=(rows, rows) + (held,) * 6 + (line,) * 9,
        check_vma=False,
    )
```
